256 devices in a mesh: gx: 16 (over z_hi, y), gy: 16 (over z_lo, x, core).
Axes of the slice: x: 4, y: 4, z: 8 (z_hi: 4, z_lo: 2; z = z_hi * 2 + z_lo), core: 2. Of those that a mesh axis runs over, the one named last changes fastest.
Arguments:
- field_e: bfloat16 [3, 192, 384, 128], P(None, 'gx', 'gy'), may hold values from -6 to 6
- field_h: bfloat16 [3, 192, 384, 128], P(None, 'gx', 'gy'), may hold values from -6 to 6
- current: bfloat16 [3, 192, 384, 128], P(None, 'gx', 'gy'), may hold values from -6 to 6
- adjoint_e: bfloat16 [3, 192, 384, 128], P(None, 'gx', 'gy'), may hold values from -6 to 6
- adjoint_h: bfloat16 [3, 192, 384, 128], P(None, 'gx', 'gy'), may hold values from -6 to 6
- adjoint_j: bfloat16 [3, 192, 384, 128], P(None, 'gx', 'gy'), may hold values from -6 to 6
- permittivity: bfloat16 [192, 384, 128], P('gx', 'gy'), may hold values from 1.1953125 to 3
- material: int32 [48, 96, 32], P('gx', 'gy'), may hold values 0 or 1
- design_block: int32 [48, 96, 32], P('gx', 'gy'), may hold values from 0 to 511
Outputs:
- adjoint_e_start: bfloat16 [3, 192, 384, 128], P(None, 'gx', 'gy')
- adjoint_h_start: bfloat16 [3, 192, 384, 128], P(None, 'gx', 'gy')
- adjoint_j_start: bfloat16 [3, 192, 384, 128], P(None, 'gx', 'gy')
- gradient: float32 [512], P(('gx', 'gy'))
The draws below stay inside these ranges and needn't reach their ends.
All inputs are finite; a program needn't handle non-finite values. No bound on the sum of `material` on one device may be relied on, other than what follows from the above.
Results may differ from the reference program's by a relative error of at most 0.001.
Values sent between devices are 32-bit elements; how exact they have to be, the bound alone decides.
A program may use at most 64 MiB of HBM per device.

```python
import math
import jax
import jax.numpy as jnp
import numpy as np
from jax import lax

EXD = 3
EYD = 6
EZ = 32
CB = 3
STEPS = 2
NXE = 48
NYE = 96
NX = 192
NY = 384
NZ = 128
NB = 512


def shaped_field(key, rough_part, level_lo, level_hi, spread):
    elem_shape = (3, NXE, NYE, EZ)
    levels = jax.random.uniform(jax.random.fold_in(key, 5), elem_shape, jnp.float32, level_lo, level_hi)
    elem_x = lax.broadcasted_iota(jnp.int32, elem_shape, 1)
    elem_y = lax.broadcasted_iota(jnp.int32, elem_shape, 2)
    parity = ((elem_x + elem_y) % 2).astype(jnp.float32)
    signed = levels * (1.0 - 2.0 * parity)
    node_values = jnp.broadcast_to(signed[:, :, None, :, None, :, None], (3, NXE, 4, NYE, 4, EZ, 4)).reshape(3, NX, NY, NZ)
    blocks_x = NXE // EXD
    blocks_y = NYE // EYD
    loud_factor = jnp.exp(jax.random.uniform(jax.random.fold_in(key, 6), (blocks_x, blocks_y), jnp.float32, -spread, spread))
    loud_nodes = jnp.broadcast_to(loud_factor[:, None, :, None], (blocks_x, 4 * EXD, blocks_y, 4 * EYD)).reshape(NX, NY)
    return jnp.clip(loud_nodes[None, :, :, None] * (node_values + rough_part), -6.0, 6.0).astype(jnp.bfloat16)


def draw_field_e(key, part):
    key = jax.random.fold_in(key, 11)
    full_shape = (3, NX, NY, NZ)
    rough_part = 0.7 * jax.random.normal(jax.random.fold_in(key, 7), full_shape, jnp.float32)
    return shaped_field(key, rough_part, 1.5, 2.5, 1.0)


def draw_field_h(key, part):
    key = jax.random.fold_in(key, 12)
    full_shape = (3, NX, NY, NZ)
    rough_part = 0.7 * jax.random.normal(jax.random.fold_in(key, 7), full_shape, jnp.float32)
    return shaped_field(key, rough_part, 1.5, 2.5, 1.0)


def draw_current(key, part):
    key = jax.random.fold_in(key, 13)
    full_shape = (3, NX, NY, NZ)
    rough_part = 0.7 * jax.random.normal(jax.random.fold_in(key, 7), full_shape, jnp.float32)
    return shaped_field(key, rough_part, 1.5, 2.5, 1.0)


def draw_adjoint_e(key, part):
    key = jax.random.fold_in(key, 14)
    full_shape = (3, NX, NY, NZ)
    rough_part = 0.7 * jax.random.normal(jax.random.fold_in(key, 7), full_shape, jnp.float32)
    return shaped_field(key, rough_part, 1.5, 2.5, 1.0)


def draw_adjoint_h(key, part):
    key = jax.random.fold_in(key, 15)
    full_shape = (3, NX, NY, NZ)
    rough_part = 0.7 * jax.random.normal(jax.random.fold_in(key, 7), full_shape, jnp.float32)
    return shaped_field(key, rough_part, 1.5, 2.5, 1.0)


def draw_adjoint_j(key, part):
    key = jax.random.fold_in(key, 16)
    full_shape = (3, NX, NY, NZ)
    rough_part = 0.7 * jax.random.normal(jax.random.fold_in(key, 7), full_shape, jnp.float32)
    return shaped_field(key, rough_part, 1.5, 2.5, 1.0)


def draw_design_block(key, part):
    full_shape = (NXE, NYE, EZ)
    elem_x = lax.broadcasted_iota(jnp.int32, full_shape, 0)
    elem_y = lax.broadcasted_iota(jnp.int32, full_shape, 1)
    elem_z = lax.broadcasted_iota(jnp.int32, full_shape, 2)
    home_block = elem_x // CB * (NYE // CB) + elem_y // CB
    relabel = jax.random.permutation(jax.random.fold_in(key, 31), NB).astype(jnp.int32)
    bottom = relabel[home_block]
    spread = jax.random.randint(jax.random.fold_in(key, 29), full_shape, 0, NB)
    return jnp.where(elem_z == 0, bottom, spread).astype(jnp.int32)


def place_ends(values, key, least, high):
    longest = values.shape.index(max(values.shape))
    spots = []
    for shift in (0, 1):
        where = [jax.random.randint(jax.random.fold_in(key, axis), (), 0, length) for axis, length in enumerate(values.shape)]
        where[longest] = (where[longest] + shift) % values.shape[longest]
        spots.append(tuple(where))
    return values.at[spots[0]].set(least).at[spots[1]].set(high)


def block_levels(own_key, dims, pieces, low, largest):
    def one(dim, shards_of):
        steps = jax.random.uniform(jax.random.fold_in(jax.random.fold_in(own_key, 6), dim), (shards_of,), jnp.float32, low / len(pieces), largest / len(pieces))
        return jnp.repeat(jnp.exp(steps), dims[dim] // shards_of).reshape((-1,) + (1,) * (len(dims) - dim - 1))

    gain = one(*pieces[0])
    for cut in pieces[1:]:
        gain = gain * one(*cut)
    return gain


def setup_inputs(seed: int = 0) -> dict:
    seeds = jax.random.split(jax.random.key(seed), 10)
    field_e = draw_field_e(jax.random.fold_in(seeds[9], 71), 0)
    field_h = draw_field_h(jax.random.fold_in(seeds[9], 71), 0)
    current = draw_current(jax.random.fold_in(seeds[9], 71), 0)
    adjoint_e = draw_adjoint_e(jax.random.fold_in(seeds[9], 71), 0)
    adjoint_h = draw_adjoint_h(jax.random.fold_in(seeds[9], 71), 0)
    adjoint_j = draw_adjoint_j(jax.random.fold_in(seeds[9], 71), 0)
    permittivity = jnp.clip(1.1953125 + 1.8046875 * jax.random.uniform(seeds[6], (NX, NY, NZ), jnp.float32) ** block_levels(seeds[6], (NX, NY, NZ), ((0, 16), (1, 16)), -0.2, 0.2), 1.1953125, 3.0).astype(jnp.bfloat16)
    material = place_ends((jax.random.randint(seeds[7], (NXE, NYE, EZ), 0, 2) < 1).astype(jnp.int32), jax.random.fold_in(seeds[7], 1), 0, 1)
    design_block = draw_design_block(jax.random.fold_in(seeds[9], 71), 0)
    return {"field_e": field_e, "field_h": field_h, "current": current, "adjoint_e": adjoint_e, "adjoint_h": adjoint_h, "adjoint_j": adjoint_j, "permittivity": permittivity, "material": material, "design_block": design_block}


time_step = 0.06
decay_factor = 0.96
plasma_square = 16.0
lift_factor = 6.0

def gll_tables():
    points = np.array([-1.0, -math.sqrt(0.2), math.sqrt(0.2), 1.0])
    weights = np.array([1.0 / 6.0, 5.0 / 6.0, 5.0 / 6.0, 1.0 / 6.0])
    products = np.array([np.prod([points[row_index] - points[other] for other in range(4) if other != row_index]) for row_index in range(4)])
    matrix = np.zeros((4, 4))
    for row_index in range(4):
        for col_index in range(4):
            if row_index != col_index:
                matrix[row_index, col_index] = products[row_index] / products[col_index] / (points[row_index] - points[col_index])
    for row_index in range(4):
        matrix[row_index, row_index] = -np.sum(matrix[row_index])
    return (matrix, weights)

def weight_cube():
    matrix, weights = gll_tables()
    cube = weights.reshape(1, 4, 1, 1, 1, 1) * weights.reshape(1, 1, 1, 4, 1, 1) * weights.reshape(1, 1, 1, 1, 1, 4) / 8.0
    return cube

def derive(source, padded, dim_index):
    matrix, weights = gll_tables()
    deriv_matrix = jnp.asarray(2.0 * matrix, jnp.float32)
    full_shape = source.shape
    node_count = full_shape[dim_index]
    split_shape = full_shape[:dim_index] + (node_count // 4, 4) + full_shape[dim_index + 1:]
    base_letters = 'gcpqs'
    src_letters = base_letters[:dim_index] + 'eb' + base_letters[dim_index + 1:]
    dst_letters = base_letters[:dim_index] + 'ea' + base_letters[dim_index + 1:]
    formula = 'ab,' + src_letters + '->' + dst_letters
    volume = jnp.einsum(formula, deriv_matrix, source.reshape(split_shape), precision=lax.Precision.HIGHEST).reshape(full_shape)
    following = lax.slice_in_dim(padded, 2, node_count + 2, axis=dim_index)
    preceding = lax.slice_in_dim(padded, 0, node_count, axis=dim_index)
    position = jnp.arange(node_count) % 4
    bshape = [1] * source.ndim
    bshape[dim_index] = node_count
    right_face = (position == 3).astype(jnp.float32).reshape(bshape)
    left_face = (position == 0).astype(jnp.float32).reshape(bshape)
    return volume + lift_factor * (right_face * (following - source) - left_face * (preceding - source))

def combine(source, padded_x, padded_y):
    padded_z = jnp.pad(source[:, 0:2], ((0, 0), (0, 0), (0, 0), (0, 0), (1, 1)))
    along_x = derive(source[:, 1:3], padded_x, 2)
    along_y = derive(source[:, 0::2], padded_y, 3)
    along_z = derive(source[:, 0:2], padded_z, 4)
    return jnp.stack([along_y[:, 1] - along_z[:, 1], along_z[:, 0] - along_x[:, 1], along_x[:, 0] - along_y[:, 0]], axis=1)

def curl_of(source):
    padded_x = jnp.pad(source[:, 1:3], ((0, 0), (0, 0), (1, 1), (0, 0), (0, 0)), mode='wrap')
    padded_y = jnp.pad(source[:, 0::2], ((0, 0), (0, 0), (0, 0), (1, 1), (0, 0)), mode='wrap')
    return combine(source, padded_x, padded_y)

def reference(field_e, field_h, current, adjoint_e, adjoint_h, adjoint_j, permittivity, material, design_block):
    elec = field_e.astype(jnp.float32)[None]
    magn = field_h.astype(jnp.float32)[None]
    cur_j = current.astype(jnp.float32)[None]
    adj_e = adjoint_e.astype(jnp.float32)[None]
    adj_h = adjoint_h.astype(jnp.float32)[None]
    adj_j = adjoint_j.astype(jnp.float32)[None]
    permf = permittivity.astype(jnp.float32)
    step_perm = time_step / permf
    drude = jnp.broadcast_to(material[:, None, :, None, :, None], (NXE, 4, NYE, 4, EZ, 4)).reshape(NX, NY, NZ).astype(jnp.float32)
    deltas = []
    for step_index in range(STEPS):
        magn = magn - time_step * curl_of(elec)
        next_e = elec + step_perm * (curl_of(magn) - drude * cur_j)
        cur_j = drude * (decay_factor * cur_j + plasma_square * time_step * next_e)
        deltas.append(next_e - elec)
        elec = next_e
    totals = []
    for step_index in range(STEPS):
        total_adj = adj_e + plasma_square * time_step * drude * adj_j
        scaled = step_perm * total_adj
        middle = adj_h + curl_of(scaled)
        adj_j = drude * (decay_factor * adj_j - scaled)
        adj_e = total_adj - time_step * curl_of(middle)
        adj_h = middle
        totals.append(total_adj)
    node_grad = jnp.zeros((NX, NY, NZ), jnp.float32)
    for step_index in range(STEPS):
        node_grad = node_grad - lax.optimization_barrier(jnp.sum(totals[STEPS - 1 - step_index][0] * deltas[step_index][0], axis=0)) / permf
    cube = jnp.asarray(weight_cube(), jnp.float32)
    element = lax.optimization_barrier(jnp.sum(node_grad.reshape(NXE, 4, NYE, 4, EZ, 4) * cube, axis=(1, 3, 5)))
    gradient = jax.ops.segment_sum(element.reshape(-1), design_block.reshape(-1), num_segments=NB)
    return (adj_e[0].astype(jnp.bfloat16), adj_h[0].astype(jnp.bfloat16), adj_j[0].astype(jnp.bfloat16), gradient)
```

```python
import functools
import math

import jax
import jax.numpy as jnp
import numpy as np
from jax import lax
from jax.experimental import pallas as pl
from jax.experimental.pallas import tpu as pltpu
from jax.sharding import PartitionSpec as P

CB = 3
DT = 0.06
DECAY = 0.96
PLASMA = 16.0
PDT = PLASMA * DT
LIFT = 6.0
MESH = pl.DeviceIdType.MESH
F32 = jnp.float32
BF16 = jnp.bfloat16

EX, EY, EZ = 3, 6, 32
NX, NY, NZ = 4 * EX, 4 * EY, 4 * EZ
ROWS = NX * NY
CHUNK = 4 * NY


def gll_tables():
    points = np.array([-1.0, -math.sqrt(0.2), math.sqrt(0.2), 1.0])
    products = np.array(
        [np.prod([points[i] - points[j] for j in range(4) if j != i]) for i in range(4)]
    )
    matrix = np.zeros((4, 4))
    for i in range(4):
        for j in range(4):
            if i != j:
                matrix[i, j] = products[i] / products[j] / (points[i] - points[j])
    for i in range(4):
        matrix[i, i] = -np.sum(matrix[i])
    return matrix


def line_matrix(elements):
    n = 4 * elements
    full = np.kron(np.eye(elements), 2.0 * gll_tables())
    for e in range(elements):
        lo, hi = 4 * e, 4 * e + 3
        full[hi, hi] -= LIFT
        if hi + 1 < n:
            full[hi, hi + 1] += LIFT
        full[lo, lo] += LIFT
        if lo > 0:
            full[lo, lo - 1] -= LIFT
    return full


def two_parts(matrix):
    high = matrix.astype(np.float32).astype(jnp.bfloat16)
    low = (matrix - high.astype(np.float64)).astype(np.float32).astype(jnp.bfloat16)
    return high, low


def constant_arrays():
    zh, zl = two_parts(line_matrix(EZ).T)
    wz = np.block([[zh, zl], [zh, zl]])
    yh, yl = two_parts(np.kron(np.eye(4), line_matrix(EY)))
    wy = np.block([[yh, yh], [yl, yl]])
    w4 = np.array([1.0, 5.0, 5.0, 1.0])
    wsum = np.kron(np.eye(EZ), w4.reshape(4, 1))
    wt = np.tile(wsum, (1, EY)).astype(jnp.bfloat16)
    wm = np.kron(np.kron(np.eye(EY), w4.reshape(4, 1)), np.ones((1, EZ))).astype(np.float32)
    return wz, wy, wt, wm


def split(value):
    high = value.astype(BF16)
    low = (value - high.astype(F32)).astype(BF16)
    return high, low


def curl_chunk(src, ex, wz_ref, wy_ref, exact=False):
    r0 = CHUNK * ex
    comps = [src[c, r0 : r0 + CHUNK, :] for c in range(3)]
    if exact:
        high = [v.astype(BF16) for v in comps]
        zin = jnp.concatenate([high[0], high[1]], axis=0)
        zout = jnp.dot(zin, wz_ref[0:NZ, :], preferred_element_type=F32)
        yin = jnp.concatenate([high[0], high[2]], axis=1)
        yout = jnp.dot(wy_ref[:, 0:CHUNK], yin, preferred_element_type=F32)
    else:
        high, low = zip(*[split(v) for v in comps])
        zin = jnp.concatenate(
            [
                jnp.concatenate([high[0], low[0]], axis=1),
                jnp.concatenate([high[1], low[1]], axis=1),
            ],
            axis=0,
        )
        zout = jnp.dot(zin, wz_ref[...], preferred_element_type=F32)
        yin = jnp.concatenate(
            [
                jnp.concatenate([high[0], high[2]], axis=1),
                jnp.concatenate([low[0], low[2]], axis=1),
            ],
            axis=0,
        )
        yout = jnp.dot(wy_ref[...], yin, preferred_element_type=F32)
    zsum = zout[:, 0:NZ] + zout[:, NZ : 2 * NZ]
    dz_x, dz_y = zsum[0:CHUNK], zsum[CHUNK : 2 * CHUNK]
    ysum = yout[0:CHUNK] + yout[CHUNK : 2 * CHUNK]
    dy_x, dy_z = ysum[:, 0:NZ], ysum[:, NZ : 2 * NZ]

    m = 2.0 * gll_tables()

    def along_x(c):
        p = [comps[c][NY * a : NY * (a + 1)] for a in range(4)]
        out0 = m[0, 1] * p[1] + m[0, 2] * p[2] + m[0, 3] * p[3]
        if ex > 0:
            out0 = out0 - LIFT * src[c, r0 - NY : r0, :]
        out1 = m[1, 0] * p[0] + m[1, 2] * p[2] + m[1, 3] * p[3]
        out2 = m[2, 0] * p[0] + m[2, 1] * p[1] + m[2, 3] * p[3]
        out3 = m[3, 0] * p[0] + m[3, 1] * p[1] + m[3, 2] * p[2]
        if ex < EX - 1:
            out3 = out3 + LIFT * src[c, r0 + CHUNK : r0 + CHUNK + NY, :]
        return jnp.concatenate([out0, out1, out2, out3], axis=0)

    dx_y, dx_z = along_x(1), along_x(2)
    return dy_z - dz_y, dz_x - dx_z, dx_y - dy_x


def kernel(
    n_gx,
    n_gy,
    e_in, h_in, j_in, le_in, lh_in, lj_in, eps_in, mat_in, blk_in, wz_in, wy_in, wt_in, wm_in,
    oe_out, oh_out, oj_out, grad_ref,
    eb, hb, jb, leb, lhb, ljb, epsb, mat, blk, wz, wy, wt, wm,
    e0, h1, e1, h2, d1, tot1, sc1, mid1, tot0, sc0, mid0, le0, lj1,
    step, drude, part, onehot, oeb, ohb, ojb,
    ys, xr, yr, gsend, grecv, msend, mrecv,
    in_sem, out_sem, send_sem, recv_sem, g_send_sem, g_recv_sem, m_send_sem, m_recv_sem,
):
    gx, gy = lax.axis_index("gx"), lax.axis_index("gy")

    def load(index, src, dst):
        copy = pltpu.make_async_copy(src, dst, in_sem.at[index])
        copy.start()
        return copy

    in_e = load(0, e_in, eb)
    in_le = load(1, le_in, leb)
    in_lj = load(2, lj_in, ljb)
    in_eps = load(3, eps_in, epsb)
    in_mat = load(4, mat_in, mat)
    in_wz = load(5, wz_in, wz)
    in_wy = load(6, wy_in, wy)
    in_h = load(7, h_in, hb)
    in_lh = load(8, lh_in, lhb)
    in_j = load(9, j_in, jb)
    in_blk = load(10, blk_in, blk)
    in_wt = load(11, wt_in, wt)
    in_wm = load(12, wm_in, wm)

    barrier = pltpu.get_barrier_semaphore()
    for k in range(1, n_gx):
        pl.semaphore_signal(
            barrier, inc=1, device_id=(lax.rem(gx + k, n_gx), gy), device_id_type=MESH
        )
    for k in range(1, n_gy):
        pl.semaphore_signal(
            barrier, inc=1, device_id=(gx, lax.rem(gy + k, n_gy)), device_id_type=MESH
        )

    right = (lax.rem(gx + 1, n_gx), gy)
    left = (lax.rem(gx + n_gx - 1, n_gx), gy)
    up = (gx, lax.rem(gy + 1, n_gy))
    down = (gx, lax.rem(gy + n_gy - 1, n_gy))
    first_y = pl.ds(0, NX, stride=NY)
    last_y = pl.ds(NY - 1, NX, stride=NY)
    first_x = slice(0, NY)
    last_x = slice(ROWS - NY, ROWS)

    def stage_y(k, field):
        ys[k, 0, 0] = field[0, first_y, :]
        ys[k, 0, 1] = field[2, first_y, :]
        ys[k, 1, 0] = field[0, last_y, :]
        ys[k, 1, 1] = field[2, last_y, :]

    def send(k, field):
        plan = (
            (field.at[pl.ds(1, 2), pl.ds(ROWS - NY, NY)], xr.at[k, 0], right),
            (field.at[pl.ds(1, 2), pl.ds(0, NY)], xr.at[k, 1], left),
            (ys.at[k, 1], yr.at[k, 0], up),
            (ys.at[k, 0], yr.at[k, 1], down),
        )
        copies = []
        for i, (src, dst, target) in enumerate(plan):
            copy = pltpu.make_async_remote_copy(
                src_ref=src, dst_ref=dst, send_sem=send_sem.at[k, i], recv_sem=recv_sem.at[k, i],
                device_id=target, device_id_type=MESH,
            )
            copy.start()
            copies.append(copy)
        return copies

    def arrived(copies):
        for copy in copies:
            copy.wait_recv()

    def fix(k, field, factor):
        f = factor(first_x) * LIFT
        field[1, first_x, :] += f * xr[k, 0, 1]
        field[2, first_x, :] -= f * xr[k, 0, 0]
        f = factor(last_x) * LIFT
        field[1, last_x, :] -= f * xr[k, 1, 1]
        field[2, last_x, :] += f * xr[k, 1, 0]
        f = factor(first_y) * LIFT
        field[0, first_y, :] -= f * yr[k, 0, 1]
        field[2, first_y, :] += f * yr[k, 0, 0]
        f = factor(last_y) * LIFT
        field[0, last_y, :] += f * yr[k, 1, 1]
        field[2, last_y, :] -= f * yr[k, 1, 0]

    by_dt = lambda rows: -DT
    by_one = lambda rows: 1.0
    by_step = lambda rows: step[rows, :]
    by_step_dt = lambda rows: -DT * step[rows, :]

    def chunks():
        return [(ex, slice(CHUNK * ex, CHUNK * (ex + 1))) for ex in range(EX)]

    in_e.wait()
    for c in range(3):
        e0[c] = eb[c].astype(F32)
    stage_y(0, e0)
    pl.semaphore_wait(barrier, n_gx + n_gy - 2)
    f1 = send(0, e0)

    in_mat.wait()
    in_eps.wait()
    zpick = (
        lax.broadcasted_iota(jnp.int32, (EZ, NZ), 0) == lax.broadcasted_iota(jnp.int32, (EZ, NZ), 1) >> 2
    ).astype(F32).astype(BF16)
    ypick = (
        lax.broadcasted_iota(jnp.int32, (NY, EY), 0) >> 2 == lax.broadcasted_iota(jnp.int32, (NY, EY), 1)
    ).astype(F32).astype(BF16)
    for ex, rows in chunks():
        picked = jnp.dot(mat[ex].astype(F32).astype(BF16), zpick, preferred_element_type=F32)
        plane = jnp.dot(ypick, picked.astype(BF16), preferred_element_type=F32)
        for a in range(4):
            drude[CHUNK * ex + NY * a : CHUNK * ex + NY * (a + 1), :] = plane
    step[...] = DT / epsb[...].astype(F32)
    in_le.wait()
    in_lj.wait()
    for c in range(3):
        total = leb[c].astype(F32) + PDT * drude[...] * ljb[c].astype(F32)
        tot1[c] = total
        sc1[c] = step[...] * total
    stage_y(1, sc1)
    a1 = send(1, sc1)

    in_wz.wait()
    in_wy.wait()
    in_h.wait()
    for ex, rows in chunks():
        curl = curl_chunk(e0, ex, wz, wy, exact=True)
        for c in range(3):
            h1[c, rows, :] = hb[c, rows, :].astype(F32) - DT * curl[c]
    in_lh.wait()
    for ex, rows in chunks():
        curl = curl_chunk(sc1, ex, wz, wy)
        for c in range(3):
            mid1[c, rows, :] = lhb[c, rows, :].astype(F32) + curl[c]

    arrived(f1)
    fix(0, h1, by_dt)
    stage_y(2, h1)
    f2 = send(2, h1)
    arrived(a1)
    fix(1, mid1, by_one)
    stage_y(3, mid1)
    a2 = send(3, mid1)

    in_j.wait()
    for ex, rows in chunks():
        curl = curl_chunk(h1, ex, wz, wy)
        for c in range(3):
            e1[c, rows, :] = e0[c, rows, :] + step[rows, :] * (
                curl[c] - drude[rows, :] * jb[c, rows, :].astype(F32)
            )
    for ex, rows in chunks():
        curl = curl_chunk(mid1, ex, wz, wy)
        for c in range(3):
            lj = drude[rows, :] * (DECAY * ljb[c, rows, :].astype(F32) - sc1[c, rows, :])
            lj1[c, rows, :] = lj
            total = tot1[c, rows, :] - DT * curl[c] + PDT * lj
            tot0[c, rows, :] = total
            sc0[c, rows, :] = step[rows, :] * total

    arrived(f2)
    fix(2, e1, by_step)
    stage_y(4, e1)
    f3 = send(4, e1)
    arrived(a2)
    fix(3, tot0, by_dt)
    fix(3, sc0, by_step_dt)
    stage_y(5, sc0)
    a3 = send(5, sc0)

    for ex, rows in chunks():
        curl = curl_chunk(e1, ex, wz, wy)
        for c in range(3):
            h2[c, rows, :] = h1[c, rows, :] - DT * curl[c]
    for ex, rows in chunks():
        curl = curl_chunk(sc0, ex, wz, wy)
        for c in range(3):
            mid0[c, rows, :] = mid1[c, rows, :] + curl[c]

    in_blk.wait()
    eye = lax.broadcasted_iota(jnp.int32, (EZ, EZ), 0) == lax.broadcasted_iota(jnp.int32, (EZ, EZ), 1)
    ones = jnp.ones((EZ, 128), BF16)
    n_rows = gsend.shape[0]
    lane = lax.broadcasted_iota(jnp.int32, (EY * EZ, 128), 1)
    for ex in range(EX):
        ids = blk[ex]
        coarse, fine = (ids & -16).astype(F32), (ids & 15).astype(F32)
        wide = jnp.concatenate(
            [jnp.where(eye, coarse[ey : ey + 1, :], 0.0) for ey in range(EY)], axis=0
        ).astype(BF16)
        narrow = jnp.concatenate(
            [jnp.where(eye, fine[ey : ey + 1, :], 0.0) for ey in range(EY)], axis=0
        ).astype(BF16)
        column = jnp.dot(wide, ones, preferred_element_type=F32) + jnp.dot(
            narrow, ones, preferred_element_type=F32
        )
        column = column.astype(jnp.int32)
        for q in range(n_rows):
            onehot[ex, :, 128 * q : 128 * (q + 1)] = (
                (column == lane + 128 * q).astype(F32).astype(BF16)
            )

    arrived(f3)
    fix(4, h2, by_dt)
    stage_y(6, h2)
    f4 = send(6, h2)
    arrived(a3)
    fix(5, mid0, by_one)
    stage_y(7, mid0)
    a4 = send(7, mid0)

    for c in range(3):
        ohb[c] = mid0[c].astype(BF16)
    out_h = pltpu.make_async_copy(ohb, oh_out, out_sem.at[0])
    out_h.start()
    for c in range(3):
        ojb[c] = (drude[...] * (DECAY * lj1[c] - sc0[c])).astype(BF16)
    out_j = pltpu.make_async_copy(ojb, oj_out, out_sem.at[1])
    out_j.start()

    for ex, rows in chunks():
        curl = curl_chunk(h2, ex, wz, wy)
        for c in range(3):
            current = drude[rows, :] * (DECAY * jb[c, rows, :].astype(F32) + PDT * e1[c, rows, :])
            d1[c, rows, :] = step[rows, :] * (curl[c] - current)
    part[...] = (
        tot0[0] * (e1[0] - e0[0]) + tot0[1] * (e1[1] - e0[1]) + tot0[2] * (e1[2] - e0[2])
    )
    for ex, rows in chunks():
        curl = curl_chunk(mid0, ex, wz, wy)
        for c in range(3):
            le0[c, rows, :] = tot0[c, rows, :] - DT * curl[c]

    in_wt.wait()
    in_wm.wait()
    arrived(f4)
    fix(6, d1, by_step)
    sums = jnp.zeros((16, 128 * n_rows), F32)
    row16 = lax.broadcasted_iota(jnp.int32, (16, EY * EZ), 0)
    scale = -1.0 / (216.0 * 8.0 * DT)
    for ex, rows in chunks():
        node = part[rows, :]
        for c in range(3):
            node = node + tot1[c, rows, :] * d1[c, rows, :]
        node = node * step[rows, :]
        layer = (
            node[0:NY] + 5.0 * node[NY : 2 * NY] + 5.0 * node[2 * NY : 3 * NY] + node[3 * NY : 4 * NY]
        )
        high = layer.astype(BF16)
        rest = layer - high.astype(F32)
        mid = rest.astype(BF16)
        low = (rest - mid.astype(F32)).astype(BF16)
        wide = (
            jnp.dot(high, wt[...], preferred_element_type=F32)
            + jnp.dot(mid, wt[...], preferred_element_type=F32)
            + jnp.dot(low, wt[...], preferred_element_type=F32)
        )
        flat = jnp.sum(wide * wm[...], axis=0, keepdims=True)
        flat = jnp.broadcast_to(flat * scale, (16, EY * EZ))
        top = flat.astype(BF16).astype(F32)
        rest = flat - top
        mid = rest.astype(BF16).astype(F32)
        pieces = jnp.where(
            row16 == 0, top, jnp.where(row16 == 1, mid, jnp.where(row16 == 2, rest - mid, 0.0))
        ).astype(BF16)
        sums = sums + jnp.dot(pieces, onehot[ex], preferred_element_type=F32)
    total = jnp.sum(sums, axis=0, keepdims=True)
    for q in range(n_rows):
        gsend[q] = total[:, 128 * q : 128 * (q + 1)]
    width = 2 * n_gy
    per_row = 128 // width
    phase1 = []
    for k in range(1, n_gx):
        p = lax.rem(gx + k, n_gx)
        copy = pltpu.make_async_remote_copy(
            src_ref=gsend.at[lax.div(p, per_row)], dst_ref=grecv.at[k],
            send_sem=g_send_sem.at[k], recv_sem=g_recv_sem.at[k],
            device_id=(p, gy), device_id_type=MESH,
        )
        copy.start()
        phase1.append(copy)

    arrived(a4)
    fix(7, le0, by_dt)
    for c in range(3):
        oeb[c] = le0[c].astype(BF16)
    out_e = pltpu.make_async_copy(oeb, oe_out, out_sem.at[2])
    out_e.start()

    mine = gsend[lax.div(gx, per_row)]
    arrived(phase1)
    for k in range(1, n_gx):
        mine = mine + grecv[k]
    msend[...] = mine
    phase2 = []
    for k in range(1, n_gy):
        copy = pltpu.make_async_remote_copy(
            src_ref=msend, dst_ref=mrecv.at[k],
            send_sem=m_send_sem.at[k], recv_sem=m_recv_sem.at[k],
            device_id=(gx, lax.rem(gy + k, n_gy)), device_id_type=MESH,
        )
        copy.start()
        phase2.append(copy)
    for copies in (f1, a1, f2, a2, f3, a3, f4, a4, phase1):
        for copy in copies:
            copy.wait_send()
    out_h.wait()
    out_j.wait()
    out_e.wait()
    arrived(phase2)
    for k in range(1, n_gy):
        mine = mine + mrecv[k]
    at = lax.rem(gx, per_row) * width + 2 * gy
    lanes = lax.broadcasted_iota(jnp.int32, (1, 128), 1)
    first = jnp.sum(jnp.where(lanes == at, mine, 0.0), axis=1, keepdims=True)
    second = jnp.sum(jnp.where(lanes == at + 1, mine, 0.0), axis=1, keepdims=True)
    grad_ref[...] = jnp.where(lanes == 0, first, second)
    for copy in phase2:
        copy.wait_send()


def per_device(n_gx, n_gy, *args):
    fields = [a.reshape(3, ROWS, NZ) for a in args[0:6]]
    eps = args[6].reshape(ROWS, NZ)
    blocks = EX * n_gx // CB * (EY * n_gy // CB)
    n_rows = -(-blocks // 128)
    consts = [jnp.asarray(a) for a in constant_arrays()]
    hbm = pl.BlockSpec(memory_space=pl.ANY)
    field32 = pltpu.VMEM((3, ROWS, NZ), F32)
    field16 = pltpu.VMEM((3, ROWS, NZ), BF16)
    plane32 = pltpu.VMEM((ROWS, NZ), F32)
    out16 = jax.ShapeDtypeStruct((3, ROWS, NZ), BF16)
    oe, oh, oj, grad = pl.pallas_call(
        functools.partial(kernel, n_gx, n_gy),
        out_shape=(out16, out16, out16, jax.ShapeDtypeStruct((1, 128), F32)),
        in_specs=[hbm] * 13,
        out_specs=(hbm, hbm, hbm, pl.BlockSpec(memory_space=pltpu.VMEM)),
        scratch_shapes=[
            *[field16] * 6,
            pltpu.VMEM((ROWS, NZ), BF16),
            pltpu.VMEM((EX, EY, EZ), jnp.int32),
            pltpu.VMEM((EX, EY, EZ), jnp.int32),
            *[pltpu.VMEM(a.shape, a.dtype) for a in consts],
            *[field32] * 13,
            plane32,
            plane32,
            plane32,
            pltpu.VMEM((EX, EY * EZ, 128 * n_rows), BF16),
            *[field16] * 3,
            pltpu.VMEM((8, 2, 2, NX, NZ), F32),
            pltpu.VMEM((8, 2, 2, NY, NZ), F32),
            pltpu.VMEM((8, 2, 2, NX, NZ), F32),
            pltpu.VMEM((n_rows, 1, 128), F32),
            pltpu.VMEM((n_gx, 1, 128), F32),
            pltpu.VMEM((1, 128), F32),
            pltpu.VMEM((n_gy, 1, 128), F32),
            pltpu.SemaphoreType.DMA((13,)),
            pltpu.SemaphoreType.DMA((3,)),
            pltpu.SemaphoreType.DMA((8, 4)),
            pltpu.SemaphoreType.DMA((8, 4)),
            pltpu.SemaphoreType.DMA((n_gx,)),
            pltpu.SemaphoreType.DMA((n_gx,)),
            pltpu.SemaphoreType.DMA((n_gy,)),
            pltpu.SemaphoreType.DMA((n_gy,)),
        ],
        compiler_params=pltpu.CompilerParams(
            collective_id=0, has_side_effects=True, vmem_limit_bytes=48 * 1024 * 1024
        ),
    )(*fields, eps, args[7], args[8], *consts)
    shape = args[0].shape
    return oe.reshape(shape), oh.reshape(shape), oj.reshape(shape), grad[0, 0:2]


def solution(mesh):
    n_gx, n_gy = mesh.shape["gx"], mesh.shape["gy"]
    field = P(None, "gx", "gy", None)
    node = P("gx", "gy", None)
    return jax.shard_map(
        functools.partial(per_device, n_gx, n_gy),
        mesh=mesh,
        in_specs=(field,) * 6 + (node,) * 3,
        out_specs=(field, field, field, P(("gx", "gy"))),
        check_vma=False,
    )
```

```python
import functools
import math

import jax
import jax.numpy as jnp
import numpy as np
from jax import lax
from jax.experimental import pallas as pl
from jax.experimental.pallas import tpu as pltpu
from jax.sharding import PartitionSpec as P

CB = 3
DT = 0.06
DECAY = 0.96
PLASMA = 16.0
PDT = PLASMA * DT
LIFT = 6.0
MESH = pl.DeviceIdType.MESH
F32 = jnp.float32
BF16 = jnp.bfloat16

EX, EY, EZ = 3, 6, 32
NX, NY, NZ = 4 * EX, 4 * EY, 4 * EZ
ROWS = NX * NY
CHUNK = 4 * NY


def gll_tables():
    points = np.array([-1.0, -math.sqrt(0.2), math.sqrt(0.2), 1.0])
    products = np.array(
        [np.prod([points[i] - points[j] for j in range(4) if j != i]) for i in range(4)]
    )
    matrix = np.zeros((4, 4))
    for i in range(4):
        for j in range(4):
            if i != j:
                matrix[i, j] = products[i] / products[j] / (points[i] - points[j])
    for i in range(4):
        matrix[i, i] = -np.sum(matrix[i])
    return matrix


def line_matrix(elements):
    n = 4 * elements
    full = np.kron(np.eye(elements), 2.0 * gll_tables())
    for e in range(elements):
        lo, hi = 4 * e, 4 * e + 3
        full[hi, hi] -= LIFT
        if hi + 1 < n:
            full[hi, hi + 1] += LIFT
        full[lo, lo] += LIFT
        if lo > 0:
            full[lo, lo - 1] -= LIFT
    return full


def two_parts(matrix):
    high = matrix.astype(np.float32).astype(jnp.bfloat16)
    low = (matrix - high.astype(np.float64)).astype(np.float32).astype(jnp.bfloat16)
    return high, low


def constant_arrays():
    zh, zl = two_parts(line_matrix(EZ).T)
    wz = np.block([[zh, zl], [zh, zl]])
    yh, yl = two_parts(np.kron(np.eye(4), line_matrix(EY)))
    wy = np.block([[yh, yh], [yl, yl]])
    w4 = np.array([1.0, 5.0, 5.0, 1.0])
    wsum = np.kron(np.eye(EZ), w4.reshape(4, 1))
    wt = np.tile(wsum, (1, EY)).astype(jnp.bfloat16)
    wm = np.kron(np.kron(np.eye(EY), w4.reshape(4, 1)), np.ones((1, EZ))).astype(np.float32)
    return wz, wy, wt, wm


def split(value):
    high = value.astype(BF16)
    low = (value - high.astype(F32)).astype(BF16)
    return high, low


def curl_chunk(src, ex, wz_ref, wy_ref, exact=False):
    r0 = CHUNK * ex
    comps = [src[c, r0 : r0 + CHUNK, :] for c in range(3)]
    if exact:
        high = [v.astype(BF16) for v in comps]
        zin = jnp.concatenate([high[0], high[1]], axis=0)
        zout = jnp.dot(zin, wz_ref[0:NZ, :], preferred_element_type=F32)
        yin = jnp.concatenate([high[0], high[2]], axis=1)
        yout = jnp.dot(wy_ref[:, 0:CHUNK], yin, preferred_element_type=F32)
    else:
        high, low = zip(*[split(v) for v in comps])
        zin = jnp.concatenate(
            [
                jnp.concatenate([high[0], low[0]], axis=1),
                jnp.concatenate([high[1], low[1]], axis=1),
            ],
            axis=0,
        )
        zout = jnp.dot(zin, wz_ref[...], preferred_element_type=F32)
        yin = jnp.concatenate(
            [
                jnp.concatenate([high[0], high[2]], axis=1),
                jnp.concatenate([low[0], low[2]], axis=1),
            ],
            axis=0,
        )
        yout = jnp.dot(wy_ref[...], yin, preferred_element_type=F32)
    zsum = zout[:, 0:NZ] + zout[:, NZ : 2 * NZ]
    dz_x, dz_y = zsum[0:CHUNK], zsum[CHUNK : 2 * CHUNK]
    ysum = yout[0:CHUNK] + yout[CHUNK : 2 * CHUNK]
    dy_x, dy_z = ysum[:, 0:NZ], ysum[:, NZ : 2 * NZ]

    m = 2.0 * gll_tables()

    def along_x(c):
        p = [comps[c][NY * a : NY * (a + 1)] for a in range(4)]
        out0 = m[0, 1] * p[1] + m[0, 2] * p[2] + m[0, 3] * p[3]
        if ex > 0:
            out0 = out0 - LIFT * src[c, r0 - NY : r0, :]
        out1 = m[1, 0] * p[0] + m[1, 2] * p[2] + m[1, 3] * p[3]
        out2 = m[2, 0] * p[0] + m[2, 1] * p[1] + m[2, 3] * p[3]
        out3 = m[3, 0] * p[0] + m[3, 1] * p[1] + m[3, 2] * p[2]
        if ex < EX - 1:
            out3 = out3 + LIFT * src[c, r0 + CHUNK : r0 + CHUNK + NY, :]
        return jnp.concatenate([out0, out1, out2, out3], axis=0)

    dx_y, dx_z = along_x(1), along_x(2)
    return dy_z - dz_y, dz_x - dx_z, dx_y - dy_x


LOW, HIGH = 0, 1
SIDES = (LOW, HIGH)
FIRST_X = slice(0, NY)
LAST_X = slice(ROWS - NY, ROWS)
X_FACE = (FIRST_X, LAST_X)
Y_FACE = (pl.ds(0, NX, stride=NY), pl.ds(NY - 1, NX, stride=NY))
CORNER = ((0, NY - 1), (ROWS - NY, ROWS - 1))
FACE = (-LIFT, LIFT)
F, A, B = 0, 1, 2


def chunks():
    return [(ex, slice(CHUNK * ex, CHUNK * (ex + 1))) for ex in range(EX)]


def add_faces(xr, yr, field, factor):
    for s in SIDES:
        f = factor(X_FACE[s]) * FACE[s]
        field[1, X_FACE[s], :] -= f * xr[s, 1]
        field[2, X_FACE[s], :] += f * xr[s, 0]
    for s in SIDES:
        f = factor(Y_FACE[s]) * FACE[s]
        field[0, Y_FACE[s], :] += f * yr[s, 1]
        field[2, Y_FACE[s], :] -= f * yr[s, 0]


def complete_faces(xr, yr, corners, field, factor):
    for s in SIDES:
        f = -FACE[s] * factor
        xr[s, 0] -= f * field[2, X_FACE[s], :]
        xr[s, 1] += f * field[1, X_FACE[s], :]
        xr[s, 1, 0:1, :] -= FACE[LOW] * factor * corners[2 * s + LOW, 0:1, :]
        xr[s, 1, NY - 1 : NY, :] -= FACE[HIGH] * factor * corners[2 * s + HIGH, 0:1, :]
    for s in SIDES:
        f = -FACE[s] * factor
        yr[s, 0] += f * field[2, Y_FACE[s], :]
        yr[s, 1] -= f * field[0, Y_FACE[s], :]
        yr[s, 1, 0:1, :] += FACE[LOW] * factor * corners[2 * LOW + s, 1:2, :]
        yr[s, 1, NX - 1 : NX, :] += FACE[HIGH] * factor * corners[2 * HIGH + s, 1:2, :]


def kernel(
    n_gx,
    n_gy,
    e_in, h_in, j_in, le_in, lh_in, lj_in, eps_in, mat_in, blk_in, wz_in, wy_in, wt_in, wm_in,
    oe_out, oh_out, oj_out, grad_ref,
    eb, hb, jb, leb, lhb, ljb, epsb, mat, blk, wz, wy, wt, wm,
    e0, h1, e1, h2, tot1, sc1, mid1, tot0, sc0, mid0, le0, lj1, q,
    step, drude, part, onehot, oeb, ohb, ojb,
    uys, vxs, vys, cs, uxr, uyr, vxr, vyr, cr,
    wxs, wys, wcs, ids, wxr, wyr, wcr, idr,
    gsend, grecv, msend, mrecv,
    in_sem, out_sem, u_send, u_recv, v_send, v_recv, c_send, c_recv,
    w_send, w_recv, i_send, i_recv, g_send_sem, g_recv_sem, m_send_sem, m_recv_sem,
):
    gx, gy = lax.axis_index("gx"), lax.axis_index("gy")
    near_x = (lax.rem(gx + n_gx - 1, n_gx), lax.rem(gx + 1, n_gx))
    near_y = (lax.rem(gy + n_gy - 1, n_gy), lax.rem(gy + 1, n_gy))

    def load(index, src, dst):
        copy = pltpu.make_async_copy(src, dst, in_sem.at[index])
        copy.start()
        return copy

    in_e = load(0, e_in, eb)
    in_h = load(7, h_in, hb)
    in_wz = load(5, wz_in, wz)
    in_wy = load(6, wy_in, wy)

    barrier = pltpu.get_barrier_semaphore()
    peers = [(near_x[a], near_y[b]) for a in SIDES for b in SIDES]
    peers += [(lax.rem(gx + k, n_gx), gy) for k in range(1, n_gx)]
    peers += [(gx, lax.rem(gy + k, n_gy)) for k in range(1, n_gy)]
    for peer in peers:
        pl.semaphore_signal(barrier, inc=1, device_id=peer, device_id_type=MESH)

    in_le = load(1, le_in, leb)
    in_lj = load(2, lj_in, ljb)
    in_eps = load(3, eps_in, epsb)
    in_mat = load(4, mat_in, mat)
    in_lh = load(8, lh_in, lhb)
    in_j = load(9, j_in, jb)
    in_blk = load(10, blk_in, blk)
    in_wt = load(11, wt_in, wt)
    in_wm = load(12, wm_in, wm)

    started = []

    def remote(src, dst, send_sem, recv_sem, target):
        copy = pltpu.make_async_remote_copy(
            src_ref=src, dst_ref=dst, send_sem=send_sem, recv_sem=recv_sem,
            device_id=target, device_id_type=MESH,
        )
        copy.start()
        started.append(copy)
        return copy

    def stage_u(k, field):
        for s in SIDES:
            uys[k, s, 0] = field[0, Y_FACE[s], :]
            uys[k, s, 1] = field[2, Y_FACE[s], :]
            for t in SIDES:
                row = CORNER[s][t]
                cs[k, 2 * s + t, 0:1, :] = field[0, row : row + 1, :]
                cs[k, 2 * s + t, 1:2, :] = field[1, row : row + 1, :]

    def stage_v(k, field):
        for s in SIDES:
            vxs[k, s, 0] = field[1, X_FACE[s], :]
            vxs[k, s, 1] = field[2, X_FACE[s], :]
            vys[k, s, 0] = field[0, Y_FACE[s], :]
            vys[k, s, 1] = field[2, Y_FACE[s], :]

    def send_u(k, field):
        copies = []
        for s in SIDES:
            src = field.at[pl.ds(1, 2), pl.ds(s * (ROWS - NY), NY)]
            copies.append(
                remote(src, uxr.at[k, 1 - s], u_send.at[k, s], u_recv.at[k, s], (near_x[s], gy))
            )
        for s in SIDES:
            copies.append(
                remote(
                    uys.at[k, s], uyr.at[k, 1 - s], u_send.at[k, 2 + s], u_recv.at[k, 2 + s],
                    (gx, near_y[s]),
                )
            )
        return copies

    def send_corners(k):
        return [
            remote(
                cs.at[k, 2 * s + t], cr.at[k, 2 * (1 - s) + 1 - t],
                c_send.at[k, 2 * s + t], c_recv.at[k, 2 * s + t], (near_x[s], near_y[t]),
            )
            for s in SIDES
            for t in SIDES
        ]

    def send_v(k):
        copies = []
        for s in SIDES:
            copies.append(
                remote(
                    vxs.at[k, s], vxr.at[k, 1 - s], v_send.at[k, s], v_recv.at[k, s],
                    (near_x[s], gy),
                )
            )
        for s in SIDES:
            copies.append(
                remote(
                    vys.at[k, s], vyr.at[k, 1 - s], v_send.at[k, 2 + s], v_recv.at[k, 2 + s],
                    (gx, near_y[s]),
                )
            )
        return copies

    def arrived(copies):
        for copy in copies:
            copy.wait_recv()

    by_step = lambda rows: step[rows, :]
    by_dt = lambda rows: -DT
    by_one = lambda rows: 1.0
    by_step_dt = lambda rows: -DT * step[rows, :]

    in_e.wait()
    for c in range(3):
        e0[c] = eb[c].astype(F32)
    in_wz.wait()
    in_wy.wait()
    in_h.wait()
    for ex, rows in chunks():
        curl = curl_chunk(e0, ex, wz, wy, exact=True)
        for c in range(3):
            h1[c, rows, :] = hb[c, rows, :].astype(F32) - DT * curl[c]
    stage_u(F, e0)
    stage_v(F, h1)

    in_mat.wait()
    in_eps.wait()
    zpick = (
        lax.broadcasted_iota(jnp.int32, (EZ, NZ), 0) == lax.broadcasted_iota(jnp.int32, (EZ, NZ), 1) >> 2
    ).astype(F32).astype(BF16)
    ypick = (
        lax.broadcasted_iota(jnp.int32, (NY, EY), 0) >> 2 == lax.broadcasted_iota(jnp.int32, (NY, EY), 1)
    ).astype(F32).astype(BF16)
    for ex, rows in chunks():
        picked = jnp.dot(mat[ex].astype(F32).astype(BF16), zpick, preferred_element_type=F32)
        plane = jnp.dot(ypick, picked.astype(BF16), preferred_element_type=F32)
        for a in range(4):
            drude[CHUNK * ex + NY * a : CHUNK * ex + NY * (a + 1), :] = plane
    step[...] = DT / epsb[...].astype(F32)
    in_le.wait()
    in_lj.wait()
    for c in range(3):
        total = leb[c].astype(F32) + PDT * drude[...] * ljb[c].astype(F32)
        tot1[c] = total
        sc1[c] = step[...] * total
    in_lh.wait()
    for ex, rows in chunks():
        curl = curl_chunk(sc1, ex, wz, wy)
        for c in range(3):
            mid1[c, rows, :] = lhb[c, rows, :].astype(F32) + curl[c]
    stage_u(A, sc1)
    stage_v(A, mid1)

    pl.semaphore_wait(barrier, len(peers))
    fu = send_u(F, e0)
    fv = send_v(F)
    fc = send_corners(F)
    au = send_u(A, sc1)
    av = send_v(A)
    ac = send_corners(A)

    for c in range(3):
        q[c] = sc1[c] * step[...]
    m = 2.0 * gll_tables()
    w4 = (1.0, 5.0, 5.0, 1.0)
    for s in SIDES:
        end = 3 * s
        for c in range(3):
            wxs[s, c] = q[c, X_FACE[s], :]
            wys[s, c] = q[c, Y_FACE[s], :]
        inner = [a for a in range(4) if a != end]
        for slot, c in ((3, 1), (4, 2)):
            acc = None
            for a in inner:
                r0 = NY * ((NX - 4) * s + a)
                term = (m[a, end] * w4[a]) * q[c, r0 : r0 + NY, :]
                acc = term if acc is None else acc + term
            wxs[s, slot] = acc
        for slot, c in ((3, 0), (4, 2)):
            acc = None
            for a in inner:
                term = (m[a, end] * w4[a]) * q[c, pl.ds((NY - 4) * s + a, NX, stride=NY), :]
                acc = term if acc is None else acc + term
            wys[s, slot] = acc
        for t in SIDES:
            row = CORNER[s][t]
            wcs[2 * s + t, 0:1, :] = q[0, row : row + 1, :]
            wcs[2 * s + t, 1:2, :] = q[1, row : row + 1, :]
    in_blk.wait()
    ids[...] = jnp.zeros_like(ids)
    for s in SIDES:
        ids[s, 0:EY, 0:EZ] = blk[(EX - 1) * s]
        for ex in range(EX):
            ids[2 + s, ex : ex + 1, 0:EZ] = blk[ex, (EY - 1) * s : (EY - 1) * s + 1, :]
        for t in SIDES:
            ids[4 + 2 * s + t, 0:1, 0:EZ] = blk[(EX - 1) * s, (EY - 1) * t : (EY - 1) * t + 1, :]
    ws = []
    for s in SIDES:
        to_x, to_y = (near_x[s], gy), (gx, near_y[s])
        ws.append(remote(wxs.at[s], wxr.at[1 - s], w_send.at[s], w_recv.at[s], to_x))
        ws.append(remote(ids.at[s], idr.at[1 - s], i_send.at[s], i_recv.at[s], to_x))
        ws.append(remote(wys.at[s], wyr.at[1 - s], w_send.at[2 + s], w_recv.at[2 + s], to_y))
        ws.append(remote(ids.at[2 + s], idr.at[3 - s], i_send.at[2 + s], i_recv.at[2 + s], to_y))
        for t in SIDES:
            here, there = 2 * s + t, 2 * (1 - s) + 1 - t
            to = (near_x[s], near_y[t])
            ws.append(remote(wcs.at[here], wcr.at[there], w_send.at[4 + here], w_recv.at[4 + here], to))
            ws.append(
                remote(ids.at[4 + here], idr.at[4 + there], i_send.at[4 + here], i_recv.at[4 + here], to)
            )

    n_rows = gsend.shape[0]
    eye = lax.broadcasted_iota(jnp.int32, (EZ, EZ), 0) == lax.broadcasted_iota(jnp.int32, (EZ, EZ), 1)
    ones = jnp.ones((EZ, 128), BF16)

    def mark(at, rows):
        coarse = jnp.concatenate(
            [jnp.where(eye, (r & -16).astype(F32), 0.0) for r in rows], axis=0
        ).astype(BF16)
        fine = jnp.concatenate(
            [jnp.where(eye, (r & 15).astype(F32), 0.0) for r in rows], axis=0
        ).astype(BF16)
        column = jnp.dot(coarse, ones, preferred_element_type=F32) + jnp.dot(
            fine, ones, preferred_element_type=F32
        )
        column = column.astype(jnp.int32)
        lane = lax.broadcasted_iota(jnp.int32, column.shape, 1)
        for n in range(n_rows):
            onehot[at : at + EZ * len(rows), 128 * n : 128 * (n + 1)] = (
                (column == lane + 128 * n).astype(F32).astype(BF16)
            )

    layer_len = EY * EZ
    for ex in range(EX):
        mark(layer_len * ex, [blk[ex, ey : ey + 1, :] for ey in range(EY)])
    x_at = layer_len * EX
    y_at = x_at + 2 * layer_len
    c_at = y_at + 2 * EX * EZ

    in_j.wait()
    arrived(fu)
    add_faces(uxr.at[F], uyr.at[F], h1, by_dt)
    for ex, rows in chunks():
        curl = curl_chunk(h1, ex, wz, wy)
        for c in range(3):
            e1[c, rows, :] = e0[c, rows, :] + step[rows, :] * (
                curl[c] - drude[rows, :] * jb[c, rows, :].astype(F32)
            )
    arrived(fv)
    arrived(fc)
    complete_faces(vxr.at[F], vyr.at[F], cr.at[F], e0, -DT)
    add_faces(vxr.at[F], vyr.at[F], e1, by_step)

    arrived(au)
    add_faces(uxr.at[A], uyr.at[A], mid1, by_one)
    for ex, rows in chunks():
        curl = curl_chunk(mid1, ex, wz, wy)
        for c in range(3):
            lj = drude[rows, :] * (DECAY * ljb[c, rows, :].astype(F32) - sc1[c, rows, :])
            lj1[c, rows, :] = lj
            total = tot1[c, rows, :] - DT * curl[c] + PDT * lj
            tot0[c, rows, :] = total
            sc0[c, rows, :] = step[rows, :] * total
    arrived(av)
    arrived(ac)
    complete_faces(vxr.at[A], vyr.at[A], cr.at[A], sc1, 1.0)
    add_faces(vxr.at[A], vyr.at[A], tot0, by_dt)
    add_faces(vxr.at[A], vyr.at[A], sc0, by_step_dt)
    stage_u(B, sc0)
    bu = send_u(B, sc0)
    bc = send_corners(B)
    for ex, rows in chunks():
        curl = curl_chunk(sc0, ex, wz, wy)
        for c in range(3):
            mid0[c, rows, :] = mid1[c, rows, :] + curl[c]
    stage_v(B, mid0)
    bv = send_v(B)

    for ex, rows in chunks():
        curl = curl_chunk(e1, ex, wz, wy)
        for c in range(3):
            h2[c, rows, :] = h1[c, rows, :] - DT * curl[c]
    for ex, rows in chunks():
        curl = curl_chunk(h2, ex, wz, wy)
        node, early = None, None
        for c in range(3):
            current = drude[rows, :] * (DECAY * jb[c, rows, :].astype(F32) + PDT * e1[c, rows, :])
            term = q[c, rows, :] * (curl[c] - current)
            node = term if node is None else node + term
            term = tot0[c, rows, :] * (e1[c, rows, :] - e0[c, rows, :])
            early = term if early is None else early + term
        part[rows, :] = node + step[rows, :] * early
    back = LIFT * LIFT * DT
    for s in SIDES:
        x, y = X_FACE[s], Y_FACE[s]
        part[x, :] -= back * (q[1, x, :] * e1[1, x, :] + q[2, x, :] * e1[2, x, :])
        part[y, :] -= back * (q[0, y, :] * e1[0, y, :] + q[2, y, :] * e1[2, y, :])

    arrived(ws)
    mark(x_at, [idr[s, ey : ey + 1, 0:EZ] for s in SIDES for ey in range(EY)])
    mark(y_at, [idr[2 + s, ex : ex + 1, 0:EZ] for s in SIDES for ex in range(EX)])
    mark(c_at, [idr[4 + k, 0:1, 0:EZ] for k in range(4)])
    xa = [-FACE[s] * DT * e1[2, X_FACE[s], :] for s in SIDES]
    xb = [FACE[s] * DT * e1[1, X_FACE[s], :] for s in SIDES]
    ya = [FACE[s] * DT * e1[2, Y_FACE[s], :] for s in SIDES]
    yb = [-FACE[s] * DT * e1[0, Y_FACE[s], :] for s in SIDES]

    def along_z(value):
        high, low = split(value)
        out = jnp.dot(jnp.concatenate([high, low], axis=1), wz[...], preferred_element_type=F32)
        return out[:, 0:NZ] + out[:, NZ : 2 * NZ]

    def along_rows(values):
        n = values[0].shape[0]
        high, low = split(jnp.concatenate(values, axis=1))
        top, rest = wy[0:n, 0:n], wy[CHUNK : CHUNK + n, 0:n]
        out = (
            jnp.dot(top, high, preferred_element_type=F32)
            + jnp.dot(top, low, preferred_element_type=F32)
            + jnp.dot(rest, high, preferred_element_type=F32)
        )
        return out[:, 0:NZ], out[:, NZ : 2 * NZ]

    xaz, yaz = [along_z(v) for v in xa], [along_z(v) for v in ya]
    xby, ybx = along_rows(xb), along_rows(yb)
    planes = []
    for s in SIDES:
        w = wxr.at[s]
        hy, hz = h2[1, X_FACE[s], :], h2[2, X_FACE[s], :]
        planes.append(
            w[0] * (xby[s] - xaz[s]) - w[3] * xb[s] + w[4] * xa[s]
            + FACE[s] * (w[1] * hz - w[2] * hy)
        )
    for s in SIDES:
        w = wyr.at[s]
        hx, hz = h2[0, Y_FACE[s], :], h2[2, Y_FACE[s], :]
        planes.append(
            w[1] * (yaz[s] - ybx[s]) + w[3] * yb[s] - w[4] * ya[s]
            + FACE[s] * (w[2] * hx - w[0] * hz)
        )
    for s in SIDES:
        for t in SIDES:
            row = CORNER[s][t]
            planes.append(
                (-FACE[s] * FACE[t] * DT)
                * (
                    wcr[2 * s + t, 1:2, :] * e1[0, row : row + 1, :]
                    + wcr[2 * s + t, 0:1, :] * e1[1, row : row + 1, :]
                )
            )

    in_wt.wait()
    in_wm.wait()
    layers = []
    for ex in range(EX):
        n = [part[CHUNK * ex + NY * a : CHUNK * ex + NY * (a + 1), :] for a in range(4)]
        layers.append(n[0] + n[3] + 5.0 * (n[1] + n[2]))
    scale = -1.0 / (216.0 * 8.0 * DT)

    def by_element(layer, count, weights):
        high, low = split(layer)
        w = wt[:, 0 : count * EZ]
        wide = jnp.dot(high, w, preferred_element_type=F32) + jnp.dot(
            low, w, preferred_element_type=F32
        )
        return jnp.sum(wide * weights, axis=0, keepdims=True) * scale

    def by_block(flat, at):
        n = flat.shape[1]
        row = lax.broadcasted_iota(jnp.int32, (16, n), 0)
        flat = jnp.broadcast_to(flat, (16, n))
        top = flat.astype(BF16).astype(F32)
        mid = (flat - top).astype(BF16).astype(F32)
        pieces = jnp.where(
            row == 0, top, jnp.where(row == 1, mid, jnp.where(row == 2, flat - top - mid, 0.0))
        ).astype(BF16)
        return jnp.dot(pieces, onehot[at : at + n, :], preferred_element_type=F32)

    sums = jnp.zeros((16, 128 * n_rows), F32)
    for i, layer in enumerate(layers + planes[0:2]):
        sums = sums + by_block(by_element(layer, EY, wm[...]), layer_len * i)
    for s in SIDES:
        flat = by_element(planes[2 + s], EX, wm[0:NX, 0 : EX * EZ])
        sums = sums + by_block(flat, y_at + EX * EZ * s)
    for k in range(4):
        flat = by_element(jnp.broadcast_to(planes[4 + k], (8, NZ)), 1, 0.125)
        sums = sums + by_block(flat, c_at + EZ * k)
    total = jnp.sum(sums, axis=0, keepdims=True)
    for n in range(n_rows):
        gsend[n] = total[:, 128 * n : 128 * (n + 1)]
    width = 2 * n_gy
    per_row = 128 // width
    phase1 = []
    for k in range(1, n_gx):
        p = lax.rem(gx + k, n_gx)
        phase1.append(
            remote(
                gsend.at[lax.div(p, per_row)], grecv.at[k], g_send_sem.at[k], g_recv_sem.at[k], (p, gy)
            )
        )

    for c in range(3):
        ojb[c] = (drude[...] * (DECAY * lj1[c] - sc0[c])).astype(BF16)
    out_j = pltpu.make_async_copy(ojb, oj_out, out_sem.at[1])
    out_j.start()

    mine = gsend[lax.div(gx, per_row)]
    arrived(phase1)
    for k in range(1, n_gx):
        mine = mine + grecv[k]
    msend[...] = mine
    phase2 = []
    for k in range(1, n_gy):
        phase2.append(
            remote(
                msend, mrecv.at[k], m_send_sem.at[k], m_recv_sem.at[k], (gx, lax.rem(gy + k, n_gy))
            )
        )

    arrived(bu)
    add_faces(uxr.at[B], uyr.at[B], mid0, by_one)
    for c in range(3):
        ohb[c] = mid0[c].astype(BF16)
    out_h = pltpu.make_async_copy(ohb, oh_out, out_sem.at[0])
    out_h.start()
    for ex, rows in chunks():
        curl = curl_chunk(mid0, ex, wz, wy)
        for c in range(3):
            le0[c, rows, :] = tot0[c, rows, :] - DT * curl[c]
    arrived(bv)
    arrived(bc)
    complete_faces(vxr.at[B], vyr.at[B], cr.at[B], sc0, 1.0)
    add_faces(vxr.at[B], vyr.at[B], le0, by_dt)
    for c in range(3):
        oeb[c] = le0[c].astype(BF16)
    out_e = pltpu.make_async_copy(oeb, oe_out, out_sem.at[2])
    out_e.start()

    for copy in started:
        copy.wait_send()
    out_h.wait()
    out_j.wait()
    out_e.wait()
    arrived(phase2)
    for k in range(1, n_gy):
        mine = mine + mrecv[k]
    at = lax.rem(gx, per_row) * width + 2 * gy
    lanes = lax.broadcasted_iota(jnp.int32, (1, 128), 1)
    first = jnp.sum(jnp.where(lanes == at, mine, 0.0), axis=1, keepdims=True)
    second = jnp.sum(jnp.where(lanes == at + 1, mine, 0.0), axis=1, keepdims=True)
    grad_ref[...] = jnp.where(lanes == 0, first, second)


def per_device(n_gx, n_gy, *args):
    fields = [a.reshape(3, ROWS, NZ) for a in args[0:6]]
    eps = args[6].reshape(ROWS, NZ)
    blocks = EX * n_gx // CB * (EY * n_gy // CB)
    n_rows = -(-blocks // 128)
    consts = [jnp.asarray(a) for a in constant_arrays()]
    hbm = pl.BlockSpec(memory_space=pl.ANY)
    field32 = pltpu.VMEM((3, ROWS, NZ), F32)
    field16 = pltpu.VMEM((3, ROWS, NZ), BF16)
    plane32 = pltpu.VMEM((ROWS, NZ), F32)
    out16 = jax.ShapeDtypeStruct((3, ROWS, NZ), BF16)
    dma = pltpu.SemaphoreType.DMA
    x_faces = pltpu.VMEM((3, 2, 2, NY, NZ), F32)
    y_faces = pltpu.VMEM((3, 2, 2, NX, NZ), F32)
    corners = pltpu.VMEM((3, 4, 2, NZ), F32)
    weights = [
        pltpu.VMEM((2, 5, NY, NZ), F32),
        pltpu.VMEM((2, 5, NX, NZ), F32),
        pltpu.VMEM((4, 2, NZ), F32),
        pltpu.VMEM((8, 8, 128), jnp.int32),
    ]
    marked = EX * EY * EZ + 2 * EY * EZ + 2 * EX * EZ + 4 * EZ
    oe, oh, oj, grad = pl.pallas_call(
        functools.partial(kernel, n_gx, n_gy),
        out_shape=(out16, out16, out16, jax.ShapeDtypeStruct((1, 128), F32)),
        in_specs=[hbm] * 13,
        out_specs=(hbm, hbm, hbm, pl.BlockSpec(memory_space=pltpu.VMEM)),
        scratch_shapes=[
            *[field16] * 6,
            pltpu.VMEM((ROWS, NZ), BF16),
            pltpu.VMEM((EX, EY, EZ), jnp.int32),
            pltpu.VMEM((EX, EY, EZ), jnp.int32),
            *[pltpu.VMEM(a.shape, a.dtype) for a in consts],
            *[field32] * 13,
            plane32,
            plane32,
            plane32,
            pltpu.VMEM((marked, 128 * n_rows), BF16),
            *[field16] * 3,
            y_faces, x_faces, y_faces, corners,
            x_faces, y_faces, x_faces, y_faces, corners,
            *weights,
            *weights,
            pltpu.VMEM((n_rows, 1, 128), F32),
            pltpu.VMEM((n_gx, 1, 128), F32),
            pltpu.VMEM((1, 128), F32),
            pltpu.VMEM((n_gy, 1, 128), F32),
            dma((13,)), dma((3,)),
            dma((3, 4)), dma((3, 4)), dma((3, 4)), dma((3, 4)), dma((3, 4)), dma((3, 4)),
            dma((8,)), dma((8,)), dma((8,)), dma((8,)),
            dma((n_gx,)), dma((n_gx,)), dma((n_gy,)), dma((n_gy,)),
        ],
        compiler_params=pltpu.CompilerParams(
            collective_id=0, has_side_effects=True, vmem_limit_bytes=60 * 1024 * 1024
        ),
    )(*fields, eps, args[7], args[8], *consts)
    shape = args[0].shape
    return oe.reshape(shape), oh.reshape(shape), oj.reshape(shape), grad[0, 0:2]


def solution(mesh):
    n_gx, n_gy = mesh.shape["gx"], mesh.shape["gy"]
    field = P(None, "gx", "gy", None)
    node = P("gx", "gy", None)
    return jax.shard_map(
        functools.partial(per_device, n_gx, n_gy),
        mesh=mesh,
        in_specs=(field,) * 6 + (node,) * 3,
        out_specs=(field, field, field, P(("gx", "gy"))),
        check_vma=False,
    )
```

```python
import functools
import math

import jax
import jax.numpy as jnp
import numpy as np
from jax import lax
from jax.experimental import pallas as pl
from jax.experimental.pallas import tpu as pltpu
from jax.sharding import PartitionSpec as P

CB = 3
DT = 0.06
DECAY = 0.96
PLASMA = 16.0
PDT = PLASMA * DT
LIFT = 6.0
MESH = pl.DeviceIdType.MESH
F32 = jnp.float32
BF16 = jnp.bfloat16

EX, EY, EZ = 3, 6, 32
NX, NY, NZ = 4 * EX, 4 * EY, 4 * EZ
ROWS = NX * NY
CHUNK = 4 * NY


def gll_tables():
    points = np.array([-1.0, -math.sqrt(0.2), math.sqrt(0.2), 1.0])
    products = np.array(
        [np.prod([points[i] - points[j] for j in range(4) if j != i]) for i in range(4)]
    )
    matrix = np.zeros((4, 4))
    for i in range(4):
        for j in range(4):
            if i != j:
                matrix[i, j] = products[i] / products[j] / (points[i] - points[j])
    for i in range(4):
        matrix[i, i] = -np.sum(matrix[i])
    return matrix


def line_matrix(elements):
    n = 4 * elements
    full = np.kron(np.eye(elements), 2.0 * gll_tables())
    for e in range(elements):
        lo, hi = 4 * e, 4 * e + 3
        full[hi, hi] -= LIFT
        if hi + 1 < n:
            full[hi, hi + 1] += LIFT
        full[lo, lo] += LIFT
        if lo > 0:
            full[lo, lo - 1] -= LIFT
    return full


def two_parts(matrix):
    high = matrix.astype(np.float32).astype(jnp.bfloat16)
    low = (matrix - high.astype(np.float64)).astype(np.float32).astype(jnp.bfloat16)
    return high, low


def constant_arrays():
    zh, zl = two_parts(line_matrix(EZ).T)
    wz = np.block([[zh, zl], [zh, zl]])
    yh, yl = two_parts(np.kron(np.eye(4), line_matrix(EY)))
    wy = np.block([[yh, yh], [yl, yl]])
    w4 = np.array([1.0, 5.0, 5.0, 1.0])
    wsum = np.kron(np.eye(EZ), w4.reshape(4, 1))
    wt = np.tile(wsum, (1, EY)).astype(jnp.bfloat16)
    wm = np.kron(np.kron(np.eye(EY), w4.reshape(4, 1)), np.ones((1, EZ))).astype(np.float32)
    return wz, wy, wt, wm


def split(value):
    high = value.astype(BF16)
    low = (value - high.astype(F32)).astype(BF16)
    return high, low


def curl_chunk(src, ex, wz_ref, wy_ref, exact=False):
    r0 = CHUNK * ex
    comps = [src[c, r0 : r0 + CHUNK, :] for c in range(3)]
    if exact:
        high = [v.astype(BF16) for v in comps]
        zin = jnp.concatenate([high[0], high[1]], axis=0)
        zout = jnp.dot(zin, wz_ref[0:NZ, :], preferred_element_type=F32)
        yin = jnp.concatenate([high[0], high[2]], axis=1)
        yout = jnp.dot(wy_ref[:, 0:CHUNK], yin, preferred_element_type=F32)
    else:
        high, low = zip(*[split(v) for v in comps])
        zin = jnp.concatenate(
            [
                jnp.concatenate([high[0], low[0]], axis=1),
                jnp.concatenate([high[1], low[1]], axis=1),
            ],
            axis=0,
        )
        zout = jnp.dot(zin, wz_ref[...], preferred_element_type=F32)
        yin = jnp.concatenate(
            [
                jnp.concatenate([high[0], high[2]], axis=1),
                jnp.concatenate([low[0], low[2]], axis=1),
            ],
            axis=0,
        )
        yout = jnp.dot(wy_ref[...], yin, preferred_element_type=F32)
    zsum = zout[:, 0:NZ] + zout[:, NZ : 2 * NZ]
    dz_x, dz_y = zsum[0:CHUNK], zsum[CHUNK : 2 * CHUNK]
    ysum = yout[0:CHUNK] + yout[CHUNK : 2 * CHUNK]
    dy_x, dy_z = ysum[:, 0:NZ], ysum[:, NZ : 2 * NZ]

    m = 2.0 * gll_tables()

    def along_x(c):
        p = [comps[c][NY * a : NY * (a + 1)] for a in range(4)]
        out0 = m[0, 1] * p[1] + m[0, 2] * p[2] + m[0, 3] * p[3]
        if ex > 0:
            out0 = out0 - LIFT * src[c, r0 - NY : r0, :]
        out1 = m[1, 0] * p[0] + m[1, 2] * p[2] + m[1, 3] * p[3]
        out2 = m[2, 0] * p[0] + m[2, 1] * p[1] + m[2, 3] * p[3]
        out3 = m[3, 0] * p[0] + m[3, 1] * p[1] + m[3, 2] * p[2]
        if ex < EX - 1:
            out3 = out3 + LIFT * src[c, r0 + CHUNK : r0 + CHUNK + NY, :]
        return jnp.concatenate([out0, out1, out2, out3], axis=0)

    dx_y, dx_z = along_x(1), along_x(2)
    return dy_z - dz_y, dz_x - dx_z, dx_y - dy_x


LOW, HIGH = 0, 1
SIDES = (LOW, HIGH)
FIRST_X = slice(0, NY)
LAST_X = slice(ROWS - NY, ROWS)
X_FACE = (FIRST_X, LAST_X)
Y_FACE = (pl.ds(0, NX, stride=NY), pl.ds(NY - 1, NX, stride=NY))
CORNER = ((0, NY - 1), (ROWS - NY, ROWS - 1))
FACE = (-LIFT, LIFT)
F, A, B = 0, 1, 2


def chunks():
    return [(ex, slice(CHUNK * ex, CHUNK * (ex + 1))) for ex in range(EX)]


def add_faces(xr, yr, field, factor):
    for s in SIDES:
        f = factor(X_FACE[s]) * FACE[s]
        field[1, X_FACE[s], :] -= f * xr[s, 1]
        field[2, X_FACE[s], :] += f * xr[s, 0]
    for s in SIDES:
        f = factor(Y_FACE[s]) * FACE[s]
        field[0, Y_FACE[s], :] += f * yr[s, 1]
        field[2, Y_FACE[s], :] -= f * yr[s, 0]


def complete_faces(xr, yr, corners, field, factor):
    for s in SIDES:
        f = -FACE[s] * factor
        xr[s, 0] -= f * field[2, X_FACE[s], :]
        xr[s, 1] += f * field[1, X_FACE[s], :]
        xr[s, 1, 0:1, :] -= FACE[LOW] * factor * corners[2 * s + LOW, 0:1, :]
        xr[s, 1, NY - 1 : NY, :] -= FACE[HIGH] * factor * corners[2 * s + HIGH, 0:1, :]
    for s in SIDES:
        f = -FACE[s] * factor
        yr[s, 0] += f * field[2, Y_FACE[s], :]
        yr[s, 1] -= f * field[0, Y_FACE[s], :]
        yr[s, 1, 0:1, :] += FACE[LOW] * factor * corners[2 * LOW + s, 1:2, :]
        yr[s, 1, NX - 1 : NX, :] += FACE[HIGH] * factor * corners[2 * HIGH + s, 1:2, :]


def kernel(
    n_gx,
    n_gy,
    e_in, h_in, j_in, le_in, lh_in, lj_in, eps_in, mat_in, blk_in, wz_in, wy_in, wt_in, wm_in,
    oe_out, oh_out, oj_out, grad_ref,
    eb, hb, jb, leb, lhb, ljb, epsb, mat, blk, wz, wy, wt, wm,
    e0, h1, e1, h2, tot1, sc1, mid1, tot0, sc0, mid0, le0, lj1, q,
    step, drude, part, onehot,
    uys, vxs, vys, cs, uxr, uyr, vxr, vyr, cr,
    wxs, wys, wcs, ids, wxr, wyr, wcr, idr,
    gsend, grecv, msend, mrecv,
    in_sem, u_send, u_recv, v_send, v_recv, c_send, c_recv,
    w_send, w_recv, i_send, i_recv, g_send_sem, g_recv_sem, m_send_sem, m_recv_sem,
):
    gx, gy = lax.axis_index("gx"), lax.axis_index("gy")
    near_x = (lax.rem(gx + n_gx - 1, n_gx), lax.rem(gx + 1, n_gx))
    near_y = (lax.rem(gy + n_gy - 1, n_gy), lax.rem(gy + 1, n_gy))

    def load(index, src, dst):
        copy = pltpu.make_async_copy(src, dst, in_sem.at[index])
        copy.start()
        return copy

    in_e = load(0, e_in, eb)
    in_h = load(7, h_in, hb)
    in_wz = load(5, wz_in, wz)
    in_wy = load(6, wy_in, wy)

    barrier = pltpu.get_barrier_semaphore()
    peers = [(near_x[a], near_y[b]) for a in SIDES for b in SIDES]
    peers += [(lax.rem(gx + k, n_gx), gy) for k in range(1, n_gx)]
    peers += [(gx, lax.rem(gy + k, n_gy)) for k in range(1, n_gy)]
    for peer in peers:
        pl.semaphore_signal(barrier, inc=1, device_id=peer, device_id_type=MESH)

    in_le = load(1, le_in, leb)
    in_lj = load(2, lj_in, ljb)
    in_eps = load(3, eps_in, epsb)
    in_mat = load(4, mat_in, mat)
    in_lh = load(8, lh_in, lhb)
    in_j = load(9, j_in, jb)
    in_blk = load(10, blk_in, blk)
    in_wt = load(11, wt_in, wt)
    in_wm = load(12, wm_in, wm)

    started = []

    def remote(src, dst, send_sem, recv_sem, target):
        copy = pltpu.make_async_remote_copy(
            src_ref=src, dst_ref=dst, send_sem=send_sem, recv_sem=recv_sem,
            device_id=target, device_id_type=MESH,
        )
        copy.start()
        started.append(copy)
        return copy

    def stage_u(k, field):
        for s in SIDES:
            uys[k, s, 0] = field[0, Y_FACE[s], :]
            uys[k, s, 1] = field[2, Y_FACE[s], :]
            for t in SIDES:
                row = CORNER[s][t]
                cs[k, 2 * s + t, 0:1, :] = field[0, row : row + 1, :]
                cs[k, 2 * s + t, 1:2, :] = field[1, row : row + 1, :]

    def stage_v(k, field):
        for s in SIDES:
            vxs[k, s, 0] = field[1, X_FACE[s], :]
            vxs[k, s, 1] = field[2, X_FACE[s], :]
            vys[k, s, 0] = field[0, Y_FACE[s], :]
            vys[k, s, 1] = field[2, Y_FACE[s], :]

    def send_u(k, field):
        copies = []
        for s in SIDES:
            src = field.at[pl.ds(1, 2), pl.ds(s * (ROWS - NY), NY)]
            copies.append(
                remote(src, uxr.at[k, 1 - s], u_send.at[k, s], u_recv.at[k, s], (near_x[s], gy))
            )
        for s in SIDES:
            copies.append(
                remote(
                    uys.at[k, s], uyr.at[k, 1 - s], u_send.at[k, 2 + s], u_recv.at[k, 2 + s],
                    (gx, near_y[s]),
                )
            )
        return copies

    def send_corners(k):
        return [
            remote(
                cs.at[k, 2 * s + t], cr.at[k, 2 * (1 - s) + 1 - t],
                c_send.at[k, 2 * s + t], c_recv.at[k, 2 * s + t], (near_x[s], near_y[t]),
            )
            for s in SIDES
            for t in SIDES
        ]

    def send_v(k):
        copies = []
        for s in SIDES:
            copies.append(
                remote(
                    vxs.at[k, s], vxr.at[k, 1 - s], v_send.at[k, s], v_recv.at[k, s],
                    (near_x[s], gy),
                )
            )
        for s in SIDES:
            copies.append(
                remote(
                    vys.at[k, s], vyr.at[k, 1 - s], v_send.at[k, 2 + s], v_recv.at[k, 2 + s],
                    (gx, near_y[s]),
                )
            )
        return copies

    def arrived(copies):
        for copy in copies:
            copy.wait_recv()

    by_step = lambda rows: step[rows, :]
    by_dt = lambda rows: -DT
    by_one = lambda rows: 1.0
    by_step_dt = lambda rows: -DT * step[rows, :]

    in_e.wait()
    for c in range(3):
        e0[c] = eb[c].astype(F32)
    in_wz.wait()
    in_wy.wait()
    in_h.wait()
    for ex, rows in chunks():
        curl = curl_chunk(e0, ex, wz, wy, exact=True)
        for c in range(3):
            h1[c, rows, :] = hb[c, rows, :].astype(F32) - DT * curl[c]
    stage_u(F, e0)
    stage_v(F, h1)

    in_mat.wait()
    in_eps.wait()
    zpick = (
        lax.broadcasted_iota(jnp.int32, (EZ, NZ), 0) == lax.broadcasted_iota(jnp.int32, (EZ, NZ), 1) >> 2
    ).astype(F32).astype(BF16)
    ypick = (
        lax.broadcasted_iota(jnp.int32, (NY, EY), 0) >> 2 == lax.broadcasted_iota(jnp.int32, (NY, EY), 1)
    ).astype(F32).astype(BF16)
    for ex, rows in chunks():
        picked = jnp.dot(mat[ex].astype(F32).astype(BF16), zpick, preferred_element_type=F32)
        plane = jnp.dot(ypick, picked.astype(BF16), preferred_element_type=F32)
        for a in range(4):
            drude[CHUNK * ex + NY * a : CHUNK * ex + NY * (a + 1), :] = plane
    step[...] = DT / epsb[...].astype(F32)
    in_le.wait()
    in_lj.wait()
    for c in range(3):
        total = leb[c].astype(F32) + PDT * drude[...] * ljb[c].astype(F32)
        tot1[c] = total
        sc1[c] = step[...] * total
    in_lh.wait()
    for ex, rows in chunks():
        curl = curl_chunk(sc1, ex, wz, wy)
        for c in range(3):
            mid1[c, rows, :] = lhb[c, rows, :].astype(F32) + curl[c]
    stage_u(A, sc1)
    stage_v(A, mid1)

    in_blk.wait()
    ids[...] = jnp.zeros_like(ids)
    for s in SIDES:
        ids[s, 0:EY, 0:EZ] = blk[(EX - 1) * s]
        for ex in range(EX):
            ids[2 + s, ex : ex + 1, 0:EZ] = blk[ex, (EY - 1) * s : (EY - 1) * s + 1, :]
        for t in SIDES:
            ids[4 + 2 * s + t, 0:1, 0:EZ] = blk[(EX - 1) * s, (EY - 1) * t : (EY - 1) * t + 1, :]
    pl.semaphore_wait(barrier, len(peers))
    fu = send_u(F, e0)
    fv = send_v(F)
    fc = send_corners(F)
    au = send_u(A, sc1)
    av = send_v(A)
    ac = send_corners(A)
    marks = []
    for s in SIDES:
        marks.append(remote(ids.at[s], idr.at[1 - s], i_send.at[s], i_recv.at[s], (near_x[s], gy)))
        marks.append(
            remote(ids.at[2 + s], idr.at[3 - s], i_send.at[2 + s], i_recv.at[2 + s], (gx, near_y[s]))
        )
        for t in SIDES:
            here, there = 4 + 2 * s + t, 4 + 2 * (1 - s) + 1 - t
            marks.append(
                remote(
                    ids.at[here], idr.at[there], i_send.at[here], i_recv.at[here],
                    (near_x[s], near_y[t]),
                )
            )

    for c in range(3):
        q[c] = sc1[c] * step[...]
    m = 2.0 * gll_tables()
    w4 = (1.0, 5.0, 5.0, 1.0)
    for s in SIDES:
        end = 3 * s
        wxs[s, 0] = step[X_FACE[s], :]
        wxs[s, 1] = q[0, X_FACE[s], :]
        wys[s, 0] = step[Y_FACE[s], :]
        wys[s, 1] = q[1, Y_FACE[s], :]
        inner = [a for a in range(4) if a != end]
        for slot, c in ((2, 1), (3, 2)):
            acc = None
            for a in inner:
                r0 = NY * ((NX - 4) * s + a)
                term = (m[a, end] * w4[a]) * q[c, r0 : r0 + NY, :]
                acc = term if acc is None else acc + term
            wxs[s, slot] = acc
        for slot, c in ((2, 0), (3, 2)):
            acc = None
            for a in inner:
                term = (m[a, end] * w4[a]) * q[c, pl.ds((NY - 4) * s + a, NX, stride=NY), :]
                acc = term if acc is None else acc + term
            wys[s, slot] = acc
        for t in SIDES:
            row = CORNER[s][t]
            wcs[2 * s + t, 0:1, :] = q[0, row : row + 1, :]
            wcs[2 * s + t, 1:2, :] = q[1, row : row + 1, :]
    ws = []
    for s in SIDES:
        to_x, to_y = (near_x[s], gy), (gx, near_y[s])
        ws.append(remote(wxs.at[s], wxr.at[1 - s], w_send.at[s], w_recv.at[s], to_x))
        ws.append(remote(wys.at[s], wyr.at[1 - s], w_send.at[2 + s], w_recv.at[2 + s], to_y))
        for t in SIDES:
            here, there = 2 * s + t, 2 * (1 - s) + 1 - t
            to = (near_x[s], near_y[t])
            ws.append(remote(wcs.at[here], wcr.at[there], w_send.at[4 + here], w_recv.at[4 + here], to))

    n_rows = gsend.shape[0]
    eye = lax.broadcasted_iota(jnp.int32, (EZ, EZ), 0) == lax.broadcasted_iota(jnp.int32, (EZ, EZ), 1)
    ones = jnp.ones((EZ, 128), BF16)

    def mark(at, rows):
        coarse = jnp.concatenate(
            [jnp.where(eye, (r & -16).astype(F32), 0.0) for r in rows], axis=0
        ).astype(BF16)
        fine = jnp.concatenate(
            [jnp.where(eye, (r & 15).astype(F32), 0.0) for r in rows], axis=0
        ).astype(BF16)
        column = jnp.dot(coarse, ones, preferred_element_type=F32) + jnp.dot(
            fine, ones, preferred_element_type=F32
        )
        column = column.astype(jnp.int32)
        lane = lax.broadcasted_iota(jnp.int32, column.shape, 1)
        for n in range(n_rows):
            onehot[at : at + EZ * len(rows), 128 * n : 128 * (n + 1)] = (
                (column == lane + 128 * n).astype(F32).astype(BF16)
            )

    layer_len = EY * EZ
    for ex in range(EX):
        mark(layer_len * ex, [blk[ex, ey : ey + 1, :] for ey in range(EY)])
    x_at = layer_len * EX
    y_at = x_at + 2 * layer_len
    c_at = y_at + 2 * EX * EZ

    in_j.wait()
    arrived(fu)
    add_faces(uxr.at[F], uyr.at[F], h1, by_dt)
    for ex, rows in chunks():
        curl = curl_chunk(h1, ex, wz, wy)
        for c in range(3):
            e1[c, rows, :] = e0[c, rows, :] + step[rows, :] * (
                curl[c] - drude[rows, :] * jb[c, rows, :].astype(F32)
            )
    arrived(fv)
    arrived(fc)
    complete_faces(vxr.at[F], vyr.at[F], cr.at[F], e0, -DT)
    add_faces(vxr.at[F], vyr.at[F], e1, by_step)

    arrived(au)
    add_faces(uxr.at[A], uyr.at[A], mid1, by_one)
    for ex, rows in chunks():
        curl = curl_chunk(mid1, ex, wz, wy)
        for c in range(3):
            lj = drude[rows, :] * (DECAY * ljb[c, rows, :].astype(F32) - sc1[c, rows, :])
            lj1[c, rows, :] = lj
            total = tot1[c, rows, :] - DT * curl[c] + PDT * lj
            tot0[c, rows, :] = total
            sc0[c, rows, :] = step[rows, :] * total
    arrived(av)
    arrived(ac)
    complete_faces(vxr.at[A], vyr.at[A], cr.at[A], sc1, 1.0)
    add_faces(vxr.at[A], vyr.at[A], tot0, by_dt)
    add_faces(vxr.at[A], vyr.at[A], sc0, by_step_dt)
    stage_u(B, sc0)
    bu = send_u(B, sc0)
    bc = send_corners(B)
    for ex, rows in chunks():
        curl = curl_chunk(sc0, ex, wz, wy)
        for c in range(3):
            mid0[c, rows, :] = mid1[c, rows, :] + curl[c]
    stage_v(B, mid0)
    bv = send_v(B)

    for ex, rows in chunks():
        curl = curl_chunk(e1, ex, wz, wy)
        for c in range(3):
            h2[c, rows, :] = h1[c, rows, :] - DT * curl[c]
    for ex, rows in chunks():
        curl = curl_chunk(h2, ex, wz, wy)
        node, early = None, None
        for c in range(3):
            current = drude[rows, :] * (DECAY * jb[c, rows, :].astype(F32) + PDT * e1[c, rows, :])
            term = q[c, rows, :] * (curl[c] - current)
            node = term if node is None else node + term
            term = tot0[c, rows, :] * (e1[c, rows, :] - e0[c, rows, :])
            early = term if early is None else early + term
        part[rows, :] = node + step[rows, :] * early
    back = LIFT * LIFT * DT
    for s in SIDES:
        x, y = X_FACE[s], Y_FACE[s]
        part[x, :] -= back * (q[1, x, :] * e1[1, x, :] + q[2, x, :] * e1[2, x, :])
        part[y, :] -= back * (q[0, y, :] * e1[0, y, :] + q[2, y, :] * e1[2, y, :])

    arrived(marks)
    mark(x_at, [idr[s, ey : ey + 1, 0:EZ] for s in SIDES for ey in range(EY)])
    mark(y_at, [idr[2 + s, ex : ex + 1, 0:EZ] for s in SIDES for ex in range(EX)])
    mark(c_at, [idr[4 + k, 0:1, 0:EZ] for k in range(4)])
    xa = [-FACE[s] * DT * e1[2, X_FACE[s], :] for s in SIDES]
    xb = [FACE[s] * DT * e1[1, X_FACE[s], :] for s in SIDES]
    ya = [FACE[s] * DT * e1[2, Y_FACE[s], :] for s in SIDES]
    yb = [-FACE[s] * DT * e1[0, Y_FACE[s], :] for s in SIDES]

    def along_z(value):
        high, low = split(value)
        out = jnp.dot(jnp.concatenate([high, low], axis=1), wz[...], preferred_element_type=F32)
        return out[:, 0:NZ] + out[:, NZ : 2 * NZ]

    def along_rows(values):
        n = values[0].shape[0]
        high, low = split(jnp.concatenate(values, axis=1))
        top, rest = wy[0:n, 0:n], wy[CHUNK : CHUNK + n, 0:n]
        out = (
            jnp.dot(top, high, preferred_element_type=F32)
            + jnp.dot(top, low, preferred_element_type=F32)
            + jnp.dot(rest, high, preferred_element_type=F32)
        )
        return out[:, 0:NZ], out[:, NZ : 2 * NZ]

    xaz, yaz = [along_z(v) for v in xa], [along_z(v) for v in ya]
    xby, ybx = along_rows(xb), along_rows(yb)
    in_wt.wait()
    in_wm.wait()
    layers = []
    for ex in range(EX):
        n = [part[CHUNK * ex + NY * a : CHUNK * ex + NY * (a + 1), :] for a in range(4)]
        layers.append(n[0] + n[3] + 5.0 * (n[1] + n[2]))
    scale = -1.0 / (216.0 * 8.0 * DT)

    def by_element(layer, count, weights):
        high, low = split(layer)
        w = wt[:, 0 : count * EZ]
        wide = jnp.dot(high, w, preferred_element_type=F32) + jnp.dot(
            low, w, preferred_element_type=F32
        )
        return jnp.sum(wide * weights, axis=0, keepdims=True) * scale

    def by_block(flat, at):
        n = flat.shape[1]
        row = lax.broadcasted_iota(jnp.int32, (16, n), 0)
        flat = jnp.broadcast_to(flat, (16, n))
        top = flat.astype(BF16).astype(F32)
        mid = (flat - top).astype(BF16).astype(F32)
        pieces = jnp.where(
            row == 0, top, jnp.where(row == 1, mid, jnp.where(row == 2, flat - top - mid, 0.0))
        ).astype(BF16)
        return jnp.dot(pieces, onehot[at : at + n, :], preferred_element_type=F32)

    sums = jnp.zeros((16, 128 * n_rows), F32)
    for i, layer in enumerate(layers):
        sums = sums + by_block(by_element(layer, EY, wm[...]), layer_len * i)

    arrived(ws)
    planes = []
    for s in SIDES:
        w = wxr.at[s]
        hy, hz = h2[1, X_FACE[s], :], h2[2, X_FACE[s], :]
        planes.append(
            w[1] * (xby[s] - xaz[s]) - w[2] * xb[s] + w[3] * xa[s]
            + FACE[s] * w[0] * (uxr[A, s, 0] * hz - uxr[A, s, 1] * hy)
        )
    for s in SIDES:
        w = wyr.at[s]
        hx, hz = h2[0, Y_FACE[s], :], h2[2, Y_FACE[s], :]
        planes.append(
            w[1] * (yaz[s] - ybx[s]) + w[2] * yb[s] - w[3] * ya[s]
            + FACE[s] * w[0] * (uyr[A, s, 1] * hx - uyr[A, s, 0] * hz)
        )
    for s in SIDES:
        for t in SIDES:
            row = CORNER[s][t]
            planes.append(
                (-FACE[s] * FACE[t] * DT)
                * (
                    wcr[2 * s + t, 1:2, :] * e1[0, row : row + 1, :]
                    + wcr[2 * s + t, 0:1, :] * e1[1, row : row + 1, :]
                )
            )

    for s in SIDES:
        sums = sums + by_block(by_element(planes[s], EY, wm[...]), x_at + layer_len * s)
    for s in SIDES:
        flat = by_element(planes[2 + s], EX, wm[0:NX, 0 : EX * EZ])
        sums = sums + by_block(flat, y_at + EX * EZ * s)
    for k in range(4):
        flat = by_element(jnp.broadcast_to(planes[4 + k], (8, NZ)), 1, 0.125)
        sums = sums + by_block(flat, c_at + EZ * k)
    total = jnp.sum(sums, axis=0, keepdims=True)
    for n in range(n_rows):
        gsend[n] = total[:, 128 * n : 128 * (n + 1)]
    width = 2 * n_gy
    per_row = 128 // width
    phase1 = []
    for k in range(1, n_gx):
        p = lax.rem(gx + k, n_gx)
        phase1.append(
            remote(
                gsend.at[lax.div(p, per_row)], grecv.at[k], g_send_sem.at[k], g_recv_sem.at[k], (p, gy)
            )
        )

    for c in range(3):
        oj_out[c] = (drude[...] * (DECAY * lj1[c] - sc0[c])).astype(BF16)

    mine = gsend[lax.div(gx, per_row)]
    arrived(phase1)
    for k in range(1, n_gx):
        mine = mine + grecv[k]
    msend[...] = mine
    phase2 = []
    for k in range(1, n_gy):
        phase2.append(
            remote(
                msend, mrecv.at[k], m_send_sem.at[k], m_recv_sem.at[k], (gx, lax.rem(gy + k, n_gy))
            )
        )

    arrived(bu)
    add_faces(uxr.at[B], uyr.at[B], mid0, by_one)
    for c in range(3):
        oh_out[c] = mid0[c].astype(BF16)
    for ex, rows in chunks():
        curl = curl_chunk(mid0, ex, wz, wy)
        for c in range(3):
            le0[c, rows, :] = tot0[c, rows, :] - DT * curl[c]
    arrived(bv)
    arrived(bc)
    complete_faces(vxr.at[B], vyr.at[B], cr.at[B], sc0, 1.0)
    add_faces(vxr.at[B], vyr.at[B], le0, by_dt)
    for c in range(3):
        oe_out[c] = le0[c].astype(BF16)

    for copy in started:
        copy.wait_send()
    arrived(phase2)
    for k in range(1, n_gy):
        mine = mine + mrecv[k]
    at = lax.rem(gx, per_row) * width + 2 * gy
    lanes = lax.broadcasted_iota(jnp.int32, (1, 128), 1)
    first = jnp.sum(jnp.where(lanes == at, mine, 0.0), axis=1, keepdims=True)
    second = jnp.sum(jnp.where(lanes == at + 1, mine, 0.0), axis=1, keepdims=True)
    grad_ref[...] = jnp.where(lanes == 0, first, second)


def write_out(e_in, h_in, j_in, g_in, e_out, h_out, j_out, g_out, sem):
    pairs = ((e_in, e_out), (h_in, h_out), (j_in, j_out))
    copies = [pltpu.make_async_copy(a, b, sem.at[i]) for i, (a, b) in enumerate(pairs)]
    for copy in copies:
        copy.start()
    g_out[...] = g_in[0, 0:2]
    for copy in copies:
        copy.wait()


def per_device(n_gx, n_gy, *args):
    fields = [a.reshape(3, ROWS, NZ) for a in args[0:6]]
    eps = args[6].reshape(ROWS, NZ)
    blocks = EX * n_gx // CB * (EY * n_gy // CB)
    n_rows = -(-blocks // 128)
    consts = [jnp.asarray(a) for a in constant_arrays()]
    hbm = pl.BlockSpec(memory_space=pl.ANY)
    field32 = pltpu.VMEM((3, ROWS, NZ), F32)
    field16 = pltpu.VMEM((3, ROWS, NZ), BF16)
    plane32 = pltpu.VMEM((ROWS, NZ), F32)
    out16 = jax.ShapeDtypeStruct((3, ROWS, NZ), BF16)
    dma = pltpu.SemaphoreType.DMA
    x_faces = pltpu.VMEM((3, 2, 2, NY, NZ), F32)
    y_faces = pltpu.VMEM((3, 2, 2, NX, NZ), F32)
    corners = pltpu.VMEM((3, 4, 2, NZ), F32)
    weights = [
        pltpu.VMEM((2, 4, NY, NZ), F32),
        pltpu.VMEM((2, 4, NX, NZ), F32),
        pltpu.VMEM((4, 2, NZ), F32),
        pltpu.VMEM((8, 8, 128), jnp.int32),
    ]
    marked = EX * EY * EZ + 2 * EY * EZ + 2 * EX * EZ + 4 * EZ
    oe, oh, oj, grad = pl.pallas_call(
        functools.partial(kernel, n_gx, n_gy),
        out_shape=(pltpu.VMEM((3, ROWS, NZ), BF16),) * 3 + (pltpu.VMEM((1, 128), F32),),
        in_specs=[hbm] * 13,
        out_specs=(pl.BlockSpec(memory_space=pltpu.VMEM),) * 4,
        scratch_shapes=[
            *[field16] * 6,
            pltpu.VMEM((ROWS, NZ), BF16),
            pltpu.VMEM((EX, EY, EZ), jnp.int32),
            pltpu.VMEM((EX, EY, EZ), jnp.int32),
            *[pltpu.VMEM(a.shape, a.dtype) for a in consts],
            *[field32] * 13,
            plane32,
            plane32,
            plane32,
            pltpu.VMEM((marked, 128 * n_rows), BF16),
            y_faces, x_faces, y_faces, corners,
            x_faces, y_faces, x_faces, y_faces, corners,
            *weights,
            *weights,
            pltpu.VMEM((n_rows, 1, 128), F32),
            pltpu.VMEM((n_gx, 1, 128), F32),
            pltpu.VMEM((1, 128), F32),
            pltpu.VMEM((n_gy, 1, 128), F32),
            dma((13,)),
            dma((3, 4)), dma((3, 4)), dma((3, 4)), dma((3, 4)), dma((3, 4)), dma((3, 4)),
            dma((8,)), dma((8,)), dma((8,)), dma((8,)),
            dma((n_gx,)), dma((n_gx,)), dma((n_gy,)), dma((n_gy,)),
        ],
        compiler_params=pltpu.CompilerParams(
            collective_id=0, has_side_effects=True, vmem_limit_bytes=60 * 1024 * 1024
        ),
    )(*fields, eps, args[7], args[8], *consts)
    oe, oh, oj, grad = pl.pallas_call(
        write_out,
        out_shape=(out16, out16, out16, jax.ShapeDtypeStruct((2,), F32)),
        in_specs=[pl.BlockSpec(memory_space=pltpu.VMEM)] * 4,
        out_specs=(hbm, hbm, hbm, pl.BlockSpec(memory_space=pltpu.VMEM)),
        scratch_shapes=[dma((3,))],
        compiler_params=pltpu.CompilerParams(vmem_limit_bytes=4 * 1024 * 1024),
    )(oe, oh, oj, grad)
    shape = args[0].shape
    return oe.reshape(shape), oh.reshape(shape), oj.reshape(shape), grad


def solution(mesh):
    n_gx, n_gy = mesh.shape["gx"], mesh.shape["gy"]
    field = P(None, "gx", "gy", None)
    node = P("gx", "gy", None)
    return jax.shard_map(
        functools.partial(per_device, n_gx, n_gy),
        mesh=mesh,
        in_specs=(field,) * 6 + (node,) * 3,
        out_specs=(field, field, field, P(("gx", "gy"))),
        check_vma=False,
    )
```

```python
import functools
import math

import jax
import jax.numpy as jnp
import numpy as np
from jax import lax
from jax.experimental import pallas as pl
from jax.experimental.pallas import tpu as pltpu
from jax.sharding import PartitionSpec as P

CB = 3
DT = 0.06
DECAY = 0.96
PLASMA = 16.0
PDT = PLASMA * DT
LIFT = 6.0
MESH = pl.DeviceIdType.MESH
F32 = jnp.float32
BF16 = jnp.bfloat16

EX, EY, EZ = 3, 6, 32
NX, NY, NZ = 4 * EX, 4 * EY, 4 * EZ
ROWS = NX * NY
CHUNK = 4 * NY


def gll_tables():
    points = np.array([-1.0, -math.sqrt(0.2), math.sqrt(0.2), 1.0])
    products = np.array(
        [np.prod([points[i] - points[j] for j in range(4) if j != i]) for i in range(4)]
    )
    matrix = np.zeros((4, 4))
    for i in range(4):
        for j in range(4):
            if i != j:
                matrix[i, j] = products[i] / products[j] / (points[i] - points[j])
    for i in range(4):
        matrix[i, i] = -np.sum(matrix[i])
    return matrix


def line_matrix(elements):
    n = 4 * elements
    full = np.kron(np.eye(elements), 2.0 * gll_tables())
    for e in range(elements):
        lo, hi = 4 * e, 4 * e + 3
        full[hi, hi] -= LIFT
        if hi + 1 < n:
            full[hi, hi + 1] += LIFT
        full[lo, lo] += LIFT
        if lo > 0:
            full[lo, lo - 1] -= LIFT
    return full


def two_parts(matrix):
    high = matrix.astype(np.float32).astype(jnp.bfloat16)
    low = (matrix - high.astype(np.float64)).astype(np.float32).astype(jnp.bfloat16)
    return high, low


def constant_arrays():
    zh, zl = two_parts(line_matrix(EZ).T)
    wz = np.block([[zh, zl], [zh, zl]])
    yh, yl = two_parts(np.kron(np.eye(4), line_matrix(EY)))
    wy = np.block([[yh, yh], [yl, yl]])
    w4 = np.array([1.0, 5.0, 5.0, 1.0])
    wsum = np.kron(np.eye(EZ), w4.reshape(4, 1))
    wt = np.tile(wsum, (1, EY)).astype(jnp.bfloat16)
    wm = np.kron(np.kron(np.eye(EY), w4.reshape(4, 1)), np.ones((1, EZ))).astype(np.float32)
    return wz, wy, wt, wm


def split(value):
    high = value.astype(BF16)
    low = (value - high.astype(F32)).astype(BF16)
    return high, low


def curl_chunk(src, ex, wz_ref, wy_ref, exact=False):
    r0 = CHUNK * ex
    comps = [src[c, r0 : r0 + CHUNK, :] for c in range(3)]
    if exact:
        high = [v.astype(BF16) for v in comps]
        zin = jnp.concatenate([high[0], high[1]], axis=0)
        zout = jnp.dot(zin, wz_ref[0:NZ, :], preferred_element_type=F32)
        yin = jnp.concatenate([high[0], high[2]], axis=1)
        yout = jnp.dot(wy_ref[:, 0:CHUNK], yin, preferred_element_type=F32)
    else:
        high, low = zip(*[split(v) for v in comps])
        zin = jnp.concatenate(
            [
                jnp.concatenate([high[0], low[0]], axis=1),
                jnp.concatenate([high[1], low[1]], axis=1),
            ],
            axis=0,
        )
        zout = jnp.dot(zin, wz_ref[...], preferred_element_type=F32)
        yin = jnp.concatenate(
            [
                jnp.concatenate([high[0], high[2]], axis=1),
                jnp.concatenate([low[0], low[2]], axis=1),
            ],
            axis=0,
        )
        yout = jnp.dot(wy_ref[...], yin, preferred_element_type=F32)
    zsum = zout[:, 0:NZ] + zout[:, NZ : 2 * NZ]
    dz_x, dz_y = zsum[0:CHUNK], zsum[CHUNK : 2 * CHUNK]
    ysum = yout[0:CHUNK] + yout[CHUNK : 2 * CHUNK]
    dy_x, dy_z = ysum[:, 0:NZ], ysum[:, NZ : 2 * NZ]

    m = 2.0 * gll_tables()

    def along_x(c):
        p = [comps[c][NY * a : NY * (a + 1)] for a in range(4)]
        out0 = m[0, 1] * p[1] + m[0, 2] * p[2] + m[0, 3] * p[3]
        if ex > 0:
            out0 = out0 - LIFT * src[c, r0 - NY : r0, :]
        out1 = m[1, 0] * p[0] + m[1, 2] * p[2] + m[1, 3] * p[3]
        out2 = m[2, 0] * p[0] + m[2, 1] * p[1] + m[2, 3] * p[3]
        out3 = m[3, 0] * p[0] + m[3, 1] * p[1] + m[3, 2] * p[2]
        if ex < EX - 1:
            out3 = out3 + LIFT * src[c, r0 + CHUNK : r0 + CHUNK + NY, :]
        return jnp.concatenate([out0, out1, out2, out3], axis=0)

    dx_y, dx_z = along_x(1), along_x(2)
    return dy_z - dz_y, dz_x - dx_z, dx_y - dy_x


LOW, HIGH = 0, 1
SIDES = (LOW, HIGH)
FIRST_X = slice(0, NY)
LAST_X = slice(ROWS - NY, ROWS)
X_FACE = (FIRST_X, LAST_X)
Y_FACE = (pl.ds(0, NX, stride=NY), pl.ds(NY - 1, NX, stride=NY))
CORNER = ((0, NY - 1), (ROWS - NY, ROWS - 1))
FACE = (-LIFT, LIFT)
F, A, B = 0, 1, 2


def chunks():
    return [(ex, slice(CHUNK * ex, CHUNK * (ex + 1))) for ex in range(EX)]


def add_faces(xr, yr, field, factor):
    for s in SIDES:
        f = factor(X_FACE[s]) * FACE[s]
        field[1, X_FACE[s], :] -= f * xr[s, 1]
        field[2, X_FACE[s], :] += f * xr[s, 0]
    for s in SIDES:
        f = factor(Y_FACE[s]) * FACE[s]
        field[0, Y_FACE[s], :] += f * yr[s, 1]
        field[2, Y_FACE[s], :] -= f * yr[s, 0]


def complete_faces(xr, yr, corners, at, field, factor):
    for s in SIDES:
        f = -FACE[s] * factor
        xr[s, 0] -= f * field[2, X_FACE[s], :]
        xr[s, 1] += f * field[1, X_FACE[s], :]
        xr[s, 1, 0:1, :] -= FACE[LOW] * factor * corners[2 * s + LOW, at : at + 1, :]
        xr[s, 1, NY - 1 : NY, :] -= FACE[HIGH] * factor * corners[2 * s + HIGH, at : at + 1, :]
    for s in SIDES:
        f = -FACE[s] * factor
        yr[s, 0] += f * field[2, Y_FACE[s], :]
        yr[s, 1] -= f * field[0, Y_FACE[s], :]
        yr[s, 1, 0:1, :] += FACE[LOW] * factor * corners[2 * LOW + s, at + 1 : at + 2, :]
        yr[s, 1, NX - 1 : NX, :] += FACE[HIGH] * factor * corners[2 * HIGH + s, at + 1 : at + 2, :]


def kernel(
    n_gx,
    n_gy,
    e_in, h_in, j_in, le_in, lh_in, lj_in, eps_in, mat_in, blk_in, wz_in, wy_in, wt_in, wm_in,
    oe_out, oh_out, oj_out, grad_ref,
    eb, hb, jb, leb, lhb, ljb, epsb, mat, blk, wz, wy, wt, wm,
    e0, h1, e1, h2, tot1, sc1, mid1, tot0, sc0, mid0, le0, lj1, q,
    step, drude, part, xt, yt, sums, onehot,
    uys, vxs, vys, cs, uxr, uyr, vxr, vyr, cr,
    wxs, wys, ids, wxr, wyr, idr,
    gsend, grecv, msend, mrecv,
    in_sem, u_send, u_recv, v_send, v_recv, c_send, c_recv,
    w_send, w_recv, i_send, i_recv, g_send_sem, g_recv_sem, m_send_sem, m_recv_sem,
):
    gx, gy = lax.axis_index("gx"), lax.axis_index("gy")
    near_x = (lax.rem(gx + n_gx - 1, n_gx), lax.rem(gx + 1, n_gx))
    near_y = (lax.rem(gy + n_gy - 1, n_gy), lax.rem(gy + 1, n_gy))

    def load(index, src, dst):
        copy = pltpu.make_async_copy(src, dst, in_sem.at[index])
        copy.start()
        return copy

    in_e = load(0, e_in, eb)
    in_h = load(7, h_in, hb)
    in_wz = load(5, wz_in, wz)
    in_wy = load(6, wy_in, wy)

    barrier = pltpu.get_barrier_semaphore()
    peers = [(near_x[a], near_y[b]) for a in SIDES for b in SIDES]
    peers += [(lax.rem(gx + k, n_gx), gy) for k in range(1, n_gx)]
    peers += [(gx, lax.rem(gy + k, n_gy)) for k in range(1, n_gy)]
    for peer in peers:
        pl.semaphore_signal(barrier, inc=1, device_id=peer, device_id_type=MESH)

    in_le = load(1, le_in, leb)
    in_lj = load(2, lj_in, ljb)
    in_eps = load(3, eps_in, epsb)
    in_mat = load(4, mat_in, mat)
    in_lh = load(8, lh_in, lhb)
    in_j = load(9, j_in, jb)
    in_blk = load(10, blk_in, blk)
    in_wt = load(11, wt_in, wt)
    in_wm = load(12, wm_in, wm)

    started = []

    def remote(src, dst, send_sem, recv_sem, target):
        copy = pltpu.make_async_remote_copy(
            src_ref=src, dst_ref=dst, send_sem=send_sem, recv_sem=recv_sem,
            device_id=target, device_id_type=MESH,
        )
        copy.start()
        started.append(copy)
        return copy

    def stage_u(k, field):
        for s in SIDES:
            uys[k, s, 0] = field[0, Y_FACE[s], :]
            uys[k, s, 1] = field[2, Y_FACE[s], :]

    def stage_corners(k, at, field):
        for s in SIDES:
            for t in SIDES:
                row = CORNER[s][t]
                cs[k, 2 * s + t, at : at + 1, :] = field[0, row : row + 1, :]
                cs[k, 2 * s + t, at + 1 : at + 2, :] = field[1, row : row + 1, :]

    def stage_v(k, field):
        for s in SIDES:
            vxs[k, s, 0] = field[1, X_FACE[s], :]
            vxs[k, s, 1] = field[2, X_FACE[s], :]
            vys[k, s, 0] = field[0, Y_FACE[s], :]
            vys[k, s, 1] = field[2, Y_FACE[s], :]

    def send_u(k, field):
        copies = []
        for s in SIDES:
            src = field.at[pl.ds(1, 2), pl.ds(s * (ROWS - NY), NY)]
            copies.append(
                remote(src, uxr.at[k, 1 - s], u_send.at[k, s], u_recv.at[k, s], (near_x[s], gy))
            )
        for s in SIDES:
            copies.append(
                remote(
                    uys.at[k, s], uyr.at[k, 1 - s], u_send.at[k, 2 + s], u_recv.at[k, 2 + s],
                    (gx, near_y[s]),
                )
            )
        return copies

    def send_corners(k):
        return [
            remote(
                cs.at[k, 2 * s + t], cr.at[k, 2 * (1 - s) + 1 - t],
                c_send.at[k, 2 * s + t], c_recv.at[k, 2 * s + t], (near_x[s], near_y[t]),
            )
            for s in SIDES
            for t in SIDES
        ]

    def send_v(k):
        copies = []
        for s in SIDES:
            copies.append(
                remote(
                    vxs.at[k, s], vxr.at[k, 1 - s], v_send.at[k, s], v_recv.at[k, s],
                    (near_x[s], gy),
                )
            )
        for s in SIDES:
            copies.append(
                remote(
                    vys.at[k, s], vyr.at[k, 1 - s], v_send.at[k, 2 + s], v_recv.at[k, 2 + s],
                    (gx, near_y[s]),
                )
            )
        return copies

    def arrived(copies):
        for copy in copies:
            copy.wait_recv()

    by_step = lambda rows: step[rows, :]
    by_dt = lambda rows: -DT
    by_one = lambda rows: 1.0

    in_e.wait()
    for c in range(3):
        e0[c] = eb[c].astype(F32)
    in_wz.wait()
    in_wy.wait()
    in_h.wait()
    for ex, rows in chunks():
        curl = curl_chunk(e0, ex, wz, wy, exact=True)
        for c in range(3):
            h1[c, rows, :] = hb[c, rows, :].astype(F32) - DT * curl[c]
    stage_u(F, e0)
    stage_v(F, h1)
    cs[...] = jnp.zeros_like(cs)
    stage_corners(0, 0, e0)

    in_mat.wait()
    in_eps.wait()
    zpick = (
        lax.broadcasted_iota(jnp.int32, (EZ, NZ), 0) == lax.broadcasted_iota(jnp.int32, (EZ, NZ), 1) >> 2
    ).astype(F32).astype(BF16)
    ypick = (
        lax.broadcasted_iota(jnp.int32, (NY, EY), 0) >> 2 == lax.broadcasted_iota(jnp.int32, (NY, EY), 1)
    ).astype(F32).astype(BF16)
    for ex, rows in chunks():
        picked = jnp.dot(mat[ex].astype(F32).astype(BF16), zpick, preferred_element_type=F32)
        plane = jnp.dot(ypick, picked.astype(BF16), preferred_element_type=F32)
        for a in range(4):
            drude[CHUNK * ex + NY * a : CHUNK * ex + NY * (a + 1), :] = plane
    step[...] = DT / epsb[...].astype(F32)
    in_le.wait()
    in_lj.wait()
    for c in range(3):
        total = leb[c].astype(F32) + PDT * drude[...] * ljb[c].astype(F32)
        tot1[c] = total
        sc1[c] = step[...] * total
    in_lh.wait()
    for ex, rows in chunks():
        curl = curl_chunk(sc1, ex, wz, wy)
        for c in range(3):
            mid1[c, rows, :] = lhb[c, rows, :].astype(F32) + curl[c]
    stage_u(A, sc1)
    stage_v(A, mid1)
    stage_corners(0, 2, sc1)
    for c in range(3):
        q[c] = sc1[c] * step[...]
    stage_corners(0, 4, q)

    in_blk.wait()
    ids[...] = jnp.zeros_like(ids)
    for s in SIDES:
        ids[s, 0:EY, 0:EZ] = blk[(EX - 1) * s]
        for ex in range(EX):
            ids[2 + s, ex : ex + 1, 0:EZ] = blk[ex, (EY - 1) * s : (EY - 1) * s + 1, :]
        for t in SIDES:
            line = blk[(EX - 1) * s, (EY - 1) * t : (EY - 1) * t + 1, :]
            cs[0, 2 * s + t, 6:7, 0:EZ] = line.astype(F32)
    pl.semaphore_wait(barrier, len(peers))
    fu = send_u(F, e0)
    fv = send_v(F)
    rc = send_corners(0)
    au = send_u(A, sc1)
    av = send_v(A)
    marks = []
    for s in SIDES:
        marks.append(remote(ids.at[s], idr.at[1 - s], i_send.at[s], i_recv.at[s], (near_x[s], gy)))
        marks.append(
            remote(ids.at[2 + s], idr.at[3 - s], i_send.at[2 + s], i_recv.at[2 + s], (gx, near_y[s]))
        )

    m = 2.0 * gll_tables()
    w4 = (1.0, 5.0, 5.0, 1.0)
    for s in SIDES:
        end = 3 * s
        wxs[s, 0] = step[X_FACE[s], :]
        wxs[s, 1] = q[0, X_FACE[s], :]
        wys[s, 0] = step[Y_FACE[s], :]
        wys[s, 1] = q[1, Y_FACE[s], :]
        inner = [a for a in range(4) if a != end]
        for slot, c in ((2, 1), (3, 2)):
            acc = None
            for a in inner:
                r0 = NY * ((NX - 4) * s + a)
                term = (m[a, end] * w4[a]) * q[c, r0 : r0 + NY, :]
                acc = term if acc is None else acc + term
            wxs[s, slot] = acc
        for slot, c in ((2, 0), (3, 2)):
            acc = None
            for a in inner:
                term = (m[a, end] * w4[a]) * q[c, pl.ds((NY - 4) * s + a, NX, stride=NY), :]
                acc = term if acc is None else acc + term
            wys[s, slot] = acc
    ws = []
    for s in SIDES:
        to_x, to_y = (near_x[s], gy), (gx, near_y[s])
        ws.append(remote(wxs.at[s], wxr.at[1 - s], w_send.at[s], w_recv.at[s], to_x))
        ws.append(remote(wys.at[s], wyr.at[1 - s], w_send.at[2 + s], w_recv.at[2 + s], to_y))

    n_rows = gsend.shape[0]
    eye = lax.broadcasted_iota(jnp.int32, (EZ, EZ), 0) == lax.broadcasted_iota(jnp.int32, (EZ, EZ), 1)
    ones = jnp.ones((EZ, 128), BF16)

    def mark(at, rows):
        coarse = jnp.concatenate(
            [jnp.where(eye, (r & -16).astype(F32), 0.0) for r in rows], axis=0
        ).astype(BF16)
        fine = jnp.concatenate(
            [jnp.where(eye, (r & 15).astype(F32), 0.0) for r in rows], axis=0
        ).astype(BF16)
        column = jnp.dot(coarse, ones, preferred_element_type=F32) + jnp.dot(
            fine, ones, preferred_element_type=F32
        )
        column = column.astype(jnp.int32)
        lane = lax.broadcasted_iota(jnp.int32, column.shape, 1)
        for n in range(n_rows):
            onehot[at : at + EZ * len(rows), 128 * n : 128 * (n + 1)] = (
                (column == lane + 128 * n).astype(F32).astype(BF16)
            )

    layer_len = EY * EZ
    for ex in range(EX):
        mark(layer_len * ex, [blk[ex, ey : ey + 1, :] for ey in range(EY)])
    x_at = layer_len * EX
    y_at = x_at + 2 * layer_len
    c_at = y_at + 2 * EX * EZ

    in_j.wait()
    arrived(fu)
    add_faces(uxr.at[F], uyr.at[F], h1, by_dt)
    for ex, rows in chunks():
        curl = curl_chunk(h1, ex, wz, wy)
        for c in range(3):
            e1[c, rows, :] = e0[c, rows, :] + step[rows, :] * (
                curl[c] - drude[rows, :] * jb[c, rows, :].astype(F32)
            )
    arrived(fv)
    arrived(rc)
    complete_faces(vxr.at[F], vyr.at[F], cr.at[0], 0, e0, -DT)
    add_faces(vxr.at[F], vyr.at[F], e1, by_step)

    arrived(au)
    add_faces(uxr.at[A], uyr.at[A], mid1, by_one)
    for ex, rows in chunks():
        curl = curl_chunk(mid1, ex, wz, wy)
        for c in range(3):
            lj = drude[rows, :] * (DECAY * ljb[c, rows, :].astype(F32) - sc1[c, rows, :])
            lj1[c, rows, :] = lj
            tot0[c, rows, :] = tot1[c, rows, :] - DT * curl[c] + PDT * lj

    for ex, rows in chunks():
        curl = curl_chunk(e1, ex, wz, wy)
        for c in range(3):
            h2[c, rows, :] = h1[c, rows, :] - DT * curl[c]
    for ex, rows in chunks():
        curl = curl_chunk(h2, ex, wz, wy)
        node = None
        for c in range(3):
            current = drude[rows, :] * (DECAY * jb[c, rows, :].astype(F32) + PDT * e1[c, rows, :])
            term = q[c, rows, :] * (curl[c] - current)
            node = term if node is None else node + term
        part[rows, :] = node
    back = LIFT * LIFT * DT
    for s in SIDES:
        x, y = X_FACE[s], Y_FACE[s]
        part[x, :] -= back * (q[1, x, :] * e1[1, x, :] + q[2, x, :] * e1[2, x, :])
        part[y, :] -= back * (q[0, y, :] * e1[0, y, :] + q[2, y, :] * e1[2, y, :])

    arrived(marks)
    mark(x_at, [idr[s, ey : ey + 1, 0:EZ] for s in SIDES for ey in range(EY)])
    mark(y_at, [idr[2 + s, ex : ex + 1, 0:EZ] for s in SIDES for ex in range(EX)])
    mark(c_at, [cr[0, k, 6:7, 0:EZ].astype(jnp.int32) for k in range(4)])
    xa = [-FACE[s] * DT * e1[2, X_FACE[s], :] for s in SIDES]
    xb = [FACE[s] * DT * e1[1, X_FACE[s], :] for s in SIDES]
    ya = [FACE[s] * DT * e1[2, Y_FACE[s], :] for s in SIDES]
    yb = [-FACE[s] * DT * e1[0, Y_FACE[s], :] for s in SIDES]

    def along_z(value):
        high, low = split(value)
        out = jnp.dot(jnp.concatenate([high, low], axis=1), wz[...], preferred_element_type=F32)
        return out[:, 0:NZ] + out[:, NZ : 2 * NZ]

    def along_rows(values):
        n = values[0].shape[0]
        high, low = split(jnp.concatenate(values, axis=1))
        top, rest = wy[0:n, 0:n], wy[CHUNK : CHUNK + n, 0:n]
        out = (
            jnp.dot(top, high, preferred_element_type=F32)
            + jnp.dot(top, low, preferred_element_type=F32)
            + jnp.dot(rest, high, preferred_element_type=F32)
        )
        return out[:, 0:NZ], out[:, NZ : 2 * NZ]

    xaz, yaz = [along_z(v) for v in xa], [along_z(v) for v in ya]
    xby, ybx = along_rows(xb), along_rows(yb)
    for s in SIDES:
        xt[s] = xby[s] - xaz[s]
        yt[s] = yaz[s] - ybx[s]

    in_wt.wait()
    in_wm.wait()
    scale = -1.0 / (216.0 * 8.0 * DT)

    def by_element(layers, count, weights):
        n = layers[0].shape[0]
        high, low = split(jnp.concatenate(layers, axis=0))
        w = wt[:, 0 : count * EZ]
        wide = jnp.dot(high, w, preferred_element_type=F32) + jnp.dot(
            low, w, preferred_element_type=F32
        )
        return [
            jnp.sum(wide[n * i : n * (i + 1)] * weights, axis=0, keepdims=True)
            for i in range(len(layers))
        ]

    def by_block(flats, at):
        out = None
        for i, flat in enumerate(flats):
            n = flat.shape[1]
            row = lax.broadcasted_iota(jnp.int32, (16, n), 0)
            flat = jnp.broadcast_to(flat, (16, n))
            top = flat.astype(BF16).astype(F32)
            pieces = jnp.where(row == 0, top, jnp.where(row == 1, flat - top, 0.0)).astype(BF16)
            term = jnp.dot(
                pieces, onehot[at + n * i : at + n * (i + 1), :], preferred_element_type=F32
            )
            out = term if out is None else out + term
        return out

    def layers_of(values):
        out = []
        for ex in range(EX):
            n = [values[CHUNK * ex + NY * a : CHUNK * ex + NY * (a + 1), :] for a in range(4)]
            out.append(n[0] + n[3] + 5.0 * (n[1] + n[2]))
        return out

    sums[...] = by_block(by_element(layers_of(part), EY, wm[...]), 0)

    arrived(av)
    complete_faces(vxr.at[A], vyr.at[A], cr.at[0], 2, sc1, 1.0)
    add_faces(vxr.at[A], vyr.at[A], tot0, by_dt)
    for c in range(3):
        sc0[c] = step[...] * tot0[c]
    stage_u(B, sc0)
    stage_corners(1, 0, sc0)
    bu = send_u(B, sc0)
    bc = send_corners(1)
    early = None
    for c in range(3):
        term = sc0[c] * (e1[c] - e0[c])
        early = term if early is None else early + term
    part[...] = early
    sums[...] += by_block(by_element(layers_of(part), EY, wm[...]), 0)

    arrived(ws)
    planes = []
    for s in SIDES:
        w = wxr.at[s]
        hy, hz = h2[1, X_FACE[s], :], h2[2, X_FACE[s], :]
        planes.append(
            w[1] * xt[s] - w[2] * (FACE[s] * DT * e1[1, X_FACE[s], :])
            - w[3] * (FACE[s] * DT * e1[2, X_FACE[s], :])
            + FACE[s] * w[0] * (uxr[A, s, 0] * hz - uxr[A, s, 1] * hy)
        )
    for s in SIDES:
        w = wyr.at[s]
        hx, hz = h2[0, Y_FACE[s], :], h2[2, Y_FACE[s], :]
        planes.append(
            w[1] * yt[s] - w[2] * (FACE[s] * DT * e1[0, Y_FACE[s], :])
            - w[3] * (FACE[s] * DT * e1[2, Y_FACE[s], :])
            + FACE[s] * w[0] * (uyr[A, s, 1] * hx - uyr[A, s, 0] * hz)
        )
    for s in SIDES:
        for t in SIDES:
            row = CORNER[s][t]
            planes.append(
                (-FACE[s] * FACE[t] * DT)
                * (
                    cr[0, 2 * s + t, 5:6, :] * e1[0, row : row + 1, :]
                    + cr[0, 2 * s + t, 4:5, :] * e1[1, row : row + 1, :]
                )
            )
    eighths = [jnp.broadcast_to(p, (8, NZ)) for p in planes[4:8]]
    late = (
        sums[...]
        + by_block(by_element(planes[0:2], EY, wm[...]), x_at)
        + by_block(by_element(planes[2:4], EX, wm[0:NX, 0 : EX * EZ]), y_at)
        + by_block(by_element(eighths, 1, 0.125), c_at)
    )
    total = jnp.sum(late, axis=0, keepdims=True) * scale
    for n in range(n_rows):
        gsend[n] = total[:, 128 * n : 128 * (n + 1)]
    width = 2 * n_gy
    per_row = 128 // width
    phase1 = []
    for k in range(1, n_gx):
        p = lax.rem(gx + k, n_gx)
        phase1.append(
            remote(
                gsend.at[lax.div(p, per_row)], grecv.at[k], g_send_sem.at[k], g_recv_sem.at[k], (p, gy)
            )
        )

    for ex, rows in chunks():
        curl = curl_chunk(sc0, ex, wz, wy)
        for c in range(3):
            mid0[c, rows, :] = mid1[c, rows, :] + curl[c]
    stage_v(B, mid0)
    bv = send_v(B)
    for c in range(3):
        oj_out[c] = (drude[...] * (DECAY * lj1[c] - sc0[c])).astype(BF16)

    mine = gsend[lax.div(gx, per_row)]
    arrived(phase1)
    for k in range(1, n_gx):
        mine = mine + grecv[k]
    msend[...] = mine
    phase2 = []
    for k in range(1, n_gy):
        phase2.append(
            remote(
                msend, mrecv.at[k], m_send_sem.at[k], m_recv_sem.at[k], (gx, lax.rem(gy + k, n_gy))
            )
        )

    arrived(bu)
    add_faces(uxr.at[B], uyr.at[B], mid0, by_one)
    for c in range(3):
        oh_out[c] = mid0[c].astype(BF16)
    for ex, rows in chunks():
        curl = curl_chunk(mid0, ex, wz, wy)
        for c in range(3):
            le0[c, rows, :] = tot0[c, rows, :] - DT * curl[c]
    arrived(bv)
    arrived(bc)
    complete_faces(vxr.at[B], vyr.at[B], cr.at[1], 0, sc0, 1.0)
    add_faces(vxr.at[B], vyr.at[B], le0, by_dt)
    for c in range(3):
        oe_out[c] = le0[c].astype(BF16)

    for copy in started:
        copy.wait_send()
    arrived(phase2)
    for k in range(1, n_gy):
        mine = mine + mrecv[k]
    at = lax.rem(gx, per_row) * width + 2 * gy
    lanes = lax.broadcasted_iota(jnp.int32, (1, 128), 1)
    first = jnp.sum(jnp.where(lanes == at, mine, 0.0), axis=1, keepdims=True)
    second = jnp.sum(jnp.where(lanes == at + 1, mine, 0.0), axis=1, keepdims=True)
    grad_ref[...] = jnp.where(lanes == 0, first, second)


def write_out(e_in, h_in, j_in, g_in, e_out, h_out, j_out, g_out, sem):
    pairs = ((e_in, e_out), (h_in, h_out), (j_in, j_out))
    copies = [pltpu.make_async_copy(a, b, sem.at[i]) for i, (a, b) in enumerate(pairs)]
    for copy in copies:
        copy.start()
    g_out[...] = g_in[0, 0:2]
    for copy in copies:
        copy.wait()


def per_device(n_gx, n_gy, *args):
    fields = [a.reshape(3, ROWS, NZ) for a in args[0:6]]
    eps = args[6].reshape(ROWS, NZ)
    blocks = EX * n_gx // CB * (EY * n_gy // CB)
    n_rows = -(-blocks // 128)
    consts = [jnp.asarray(a) for a in constant_arrays()]
    hbm = pl.BlockSpec(memory_space=pl.ANY)
    field32 = pltpu.VMEM((3, ROWS, NZ), F32)
    field16 = pltpu.VMEM((3, ROWS, NZ), BF16)
    plane32 = pltpu.VMEM((ROWS, NZ), F32)
    out16 = jax.ShapeDtypeStruct((3, ROWS, NZ), BF16)
    dma = pltpu.SemaphoreType.DMA
    x_faces = pltpu.VMEM((3, 2, 2, NY, NZ), F32)
    y_faces = pltpu.VMEM((3, 2, 2, NX, NZ), F32)
    corners = pltpu.VMEM((2, 4, 8, NZ), F32)
    weights = [
        pltpu.VMEM((2, 4, NY, NZ), F32),
        pltpu.VMEM((2, 4, NX, NZ), F32),
        pltpu.VMEM((4, 8, 128), jnp.int32),
    ]
    marked = EX * EY * EZ + 2 * EY * EZ + 2 * EX * EZ + 4 * EZ
    oe, oh, oj, grad = pl.pallas_call(
        functools.partial(kernel, n_gx, n_gy),
        out_shape=(pltpu.VMEM((3, ROWS, NZ), BF16),) * 3 + (pltpu.VMEM((1, 128), F32),),
        in_specs=[hbm] * 13,
        out_specs=(pl.BlockSpec(memory_space=pltpu.VMEM),) * 4,
        scratch_shapes=[
            *[field16] * 6,
            pltpu.VMEM((ROWS, NZ), BF16),
            pltpu.VMEM((EX, EY, EZ), jnp.int32),
            pltpu.VMEM((EX, EY, EZ), jnp.int32),
            *[pltpu.VMEM(a.shape, a.dtype) for a in consts],
            *[field32] * 13,
            plane32,
            plane32,
            plane32,
            pltpu.VMEM((2, NY, NZ), F32),
            pltpu.VMEM((2, NX, NZ), F32),
            pltpu.VMEM((16, 128 * n_rows), F32),
            pltpu.VMEM((marked, 128 * n_rows), BF16),
            y_faces, x_faces, y_faces, corners,
            x_faces, y_faces, x_faces, y_faces, corners,
            *weights,
            *weights,
            pltpu.VMEM((n_rows, 1, 128), F32),
            pltpu.VMEM((n_gx, 1, 128), F32),
            pltpu.VMEM((1, 128), F32),
            pltpu.VMEM((n_gy, 1, 128), F32),
            dma((13,)),
            dma((3, 4)), dma((3, 4)), dma((3, 4)), dma((3, 4)), dma((2, 4)), dma((2, 4)),
            dma((4,)), dma((4,)), dma((4,)), dma((4,)),
            dma((n_gx,)), dma((n_gx,)), dma((n_gy,)), dma((n_gy,)),
        ],
        compiler_params=pltpu.CompilerParams(
            collective_id=0, has_side_effects=True, vmem_limit_bytes=60 * 1024 * 1024
        ),
    )(*fields, eps, args[7], args[8], *consts)
    oe, oh, oj, grad = pl.pallas_call(
        write_out,
        out_shape=(out16, out16, out16, jax.ShapeDtypeStruct((2,), F32)),
        in_specs=[pl.BlockSpec(memory_space=pltpu.VMEM)] * 4,
        out_specs=(hbm, hbm, hbm, pl.BlockSpec(memory_space=pltpu.VMEM)),
        scratch_shapes=[dma((3,))],
        compiler_params=pltpu.CompilerParams(vmem_limit_bytes=4 * 1024 * 1024),
    )(oe, oh, oj, grad)
    shape = args[0].shape
    return oe.reshape(shape), oh.reshape(shape), oj.reshape(shape), grad


def solution(mesh):
    n_gx, n_gy = mesh.shape["gx"], mesh.shape["gy"]
    field = P(None, "gx", "gy", None)
    node = P("gx", "gy", None)
    return jax.shard_map(
        functools.partial(per_device, n_gx, n_gy),
        mesh=mesh,
        in_specs=(field,) * 6 + (node,) * 3,
        out_specs=(field, field, field, P(("gx", "gy"))),
        check_vma=False,
    )
```

```python
import functools
import math

import jax
import jax.numpy as jnp
import numpy as np
from jax import lax
from jax.experimental import pallas as pl
from jax.experimental.pallas import tpu as pltpu
from jax.sharding import PartitionSpec as P

CB = 3
DT = 0.06
DECAY = 0.96
PLASMA = 16.0
PDT = PLASMA * DT
LIFT = 6.0
MESH = pl.DeviceIdType.MESH
F32 = jnp.float32
BF16 = jnp.bfloat16

EX, EY, EZ = 3, 6, 32
NX, NY, NZ = 4 * EX, 4 * EY, 4 * EZ
ROWS = NX * NY
CHUNK = 4 * NY


def gll_tables():
    points = np.array([-1.0, -math.sqrt(0.2), math.sqrt(0.2), 1.0])
    products = np.array(
        [np.prod([points[i] - points[j] for j in range(4) if j != i]) for i in range(4)]
    )
    matrix = np.zeros((4, 4))
    for i in range(4):
        for j in range(4):
            if i != j:
                matrix[i, j] = products[i] / products[j] / (points[i] - points[j])
    for i in range(4):
        matrix[i, i] = -np.sum(matrix[i])
    return matrix


def line_matrix(elements):
    n = 4 * elements
    full = np.kron(np.eye(elements), 2.0 * gll_tables())
    for e in range(elements):
        lo, hi = 4 * e, 4 * e + 3
        full[hi, hi] -= LIFT
        if hi + 1 < n:
            full[hi, hi + 1] += LIFT
        full[lo, lo] += LIFT
        if lo > 0:
            full[lo, lo - 1] -= LIFT
    return full


def two_parts(matrix):
    high = matrix.astype(np.float32).astype(jnp.bfloat16)
    low = (matrix - high.astype(np.float64)).astype(np.float32).astype(jnp.bfloat16)
    return high, low


def constant_arrays():
    zh, zl = two_parts(line_matrix(EZ).T)
    wz = np.block([[zh, zl], [zh, zl]])
    yh, yl = two_parts(np.kron(np.eye(4), line_matrix(EY)))
    wy = np.block([[yh, yh], [yl, yl]])
    w4 = np.array([1.0, 5.0, 5.0, 1.0])
    wsum = np.kron(np.eye(EZ), w4.reshape(4, 1))
    wt = np.tile(wsum, (1, EY)).astype(jnp.bfloat16)
    wm = np.kron(np.kron(np.eye(EY), w4.reshape(4, 1)), np.ones((1, EZ))).astype(np.float32)
    return wz, wy, wt, wm


def split(value):
    high = value.astype(BF16)
    low = (value - high.astype(F32)).astype(BF16)
    return high, low


def curl_chunk(src, ex, wz_ref, wy_ref, exact=False):
    r0 = CHUNK * ex
    comps = [src[c, r0 : r0 + CHUNK, :] for c in range(3)]
    if exact:
        high = [v.astype(BF16) for v in comps]
        zin = jnp.concatenate([high[0], high[1]], axis=0)
        zout = jnp.dot(zin, wz_ref[0:NZ, :], preferred_element_type=F32)
        yin = jnp.concatenate([high[0], high[2]], axis=1)
        yout = jnp.dot(wy_ref[:, 0:CHUNK], yin, preferred_element_type=F32)
    else:
        high, low = zip(*[split(v) for v in comps])
        zin = jnp.concatenate(
            [
                jnp.concatenate([high[0], low[0]], axis=1),
                jnp.concatenate([high[1], low[1]], axis=1),
            ],
            axis=0,
        )
        zout = jnp.dot(zin, wz_ref[...], preferred_element_type=F32)
        yin = jnp.concatenate(
            [
                jnp.concatenate([high[0], high[2]], axis=1),
                jnp.concatenate([low[0], low[2]], axis=1),
            ],
            axis=0,
        )
        yout = jnp.dot(wy_ref[...], yin, preferred_element_type=F32)
    zsum = zout[:, 0:NZ] + zout[:, NZ : 2 * NZ]
    dz_x, dz_y = zsum[0:CHUNK], zsum[CHUNK : 2 * CHUNK]
    ysum = yout[0:CHUNK] + yout[CHUNK : 2 * CHUNK]
    dy_x, dy_z = ysum[:, 0:NZ], ysum[:, NZ : 2 * NZ]

    m = 2.0 * gll_tables()

    def along_x(c):
        p = [comps[c][NY * a : NY * (a + 1)] for a in range(4)]
        out0 = m[0, 1] * p[1] + m[0, 2] * p[2] + m[0, 3] * p[3]
        if ex > 0:
            out0 = out0 - LIFT * src[c, r0 - NY : r0, :]
        out1 = m[1, 0] * p[0] + m[1, 2] * p[2] + m[1, 3] * p[3]
        out2 = m[2, 0] * p[0] + m[2, 1] * p[1] + m[2, 3] * p[3]
        out3 = m[3, 0] * p[0] + m[3, 1] * p[1] + m[3, 2] * p[2]
        if ex < EX - 1:
            out3 = out3 + LIFT * src[c, r0 + CHUNK : r0 + CHUNK + NY, :]
        return jnp.concatenate([out0, out1, out2, out3], axis=0)

    dx_y, dx_z = along_x(1), along_x(2)
    return dy_z - dz_y, dz_x - dx_z, dx_y - dy_x


LOW, HIGH = 0, 1
SIDES = (LOW, HIGH)
FIRST_X = slice(0, NY)
LAST_X = slice(ROWS - NY, ROWS)
X_FACE = (FIRST_X, LAST_X)
Y_FACE = (pl.ds(0, NX, stride=NY), pl.ds(NY - 1, NX, stride=NY))
CORNER = ((0, NY - 1), (ROWS - NY, ROWS - 1))
FACE = (-LIFT, LIFT)
F, A, B = 0, 1, 2


def gx_steps(n):
    return sorted({d % n for step in (1, 4) if step < n for d in (step, -step)} - {0})


def gx_waves(n):
    known, waves = {0, *gx_steps(n)}, 0
    while len(known) < n or not waves:
        known |= {(a + b) % n for a in known for b in gx_steps(n)}
        waves += 1
    return waves


def chunks():
    return [(ex, slice(CHUNK * ex, CHUNK * (ex + 1))) for ex in range(EX)]


def add_faces(xr, yr, field, factor):
    for s in SIDES:
        f = factor(X_FACE[s]) * FACE[s]
        field[1, X_FACE[s], :] -= f * xr[s, 1]
        field[2, X_FACE[s], :] += f * xr[s, 0]
    for s in SIDES:
        f = factor(Y_FACE[s]) * FACE[s]
        field[0, Y_FACE[s], :] += f * yr[s, 1]
        field[2, Y_FACE[s], :] -= f * yr[s, 0]


def complete_faces(xr, yr, corners, at, field, factor):
    for s in SIDES:
        f = -FACE[s] * factor
        xr[s, 0] -= f * field[2, X_FACE[s], :]
        xr[s, 1] += f * field[1, X_FACE[s], :]
        xr[s, 1, 0:1, :] -= FACE[LOW] * factor * corners[2 * s + LOW, at : at + 1, :]
        xr[s, 1, NY - 1 : NY, :] -= FACE[HIGH] * factor * corners[2 * s + HIGH, at : at + 1, :]
    for s in SIDES:
        f = -FACE[s] * factor
        yr[s, 0] += f * field[2, Y_FACE[s], :]
        yr[s, 1] -= f * field[0, Y_FACE[s], :]
        yr[s, 1, 0:1, :] += FACE[LOW] * factor * corners[2 * LOW + s, at + 1 : at + 2, :]
        yr[s, 1, NX - 1 : NX, :] += FACE[HIGH] * factor * corners[2 * HIGH + s, at + 1 : at + 2, :]


def kernel(
    n_gx,
    n_gy,
    e_in, h_in, j_in, le_in, lh_in, lj_in, eps_in, mat_in, blk_in, wz_in, wy_in, wt_in, wm_in,
    oe_out, oh_out, oj_out, grad_ref,
    eb, hb, jb, leb, lhb, ljb, epsb, mat, blk, wz, wy, wt, wm,
    e0, h1, e1, h2, tot1, sc1, mid1, tot0, sc0, mid0, le0, lj1, q,
    step, drude, part, xt, yt, sums, onehot,
    uys, vxs, vys, cs, uxr, uyr, vxr, vyr, cr,
    wxs, wys, ids, wxr, wyr, idr,
    gsend, grecv, msend, mrecv,
    in_sem, u_send, u_recv, v_send, v_recv, c_send, c_recv,
    w_send, w_recv, i_send, i_recv, g_send_sem, g_recv_sem, m_send_sem, m_recv_sem, heard,
):
    gx, gy = lax.axis_index("gx"), lax.axis_index("gy")
    near_x = (lax.rem(gx + n_gx - 1, n_gx), lax.rem(gx + 1, n_gx))
    near_y = (lax.rem(gy + n_gy - 1, n_gy), lax.rem(gy + 1, n_gy))

    def load(index, src, dst):
        copy = pltpu.make_async_copy(src, dst, in_sem.at[index])
        copy.start()
        return copy

    barrier = pltpu.get_barrier_semaphore()
    near = [(lax.rem(gx + d, n_gx), gy) for d in gx_steps(n_gx)]
    peers = near + [(gx, lax.rem(gy + k, n_gy)) for k in range(1, n_gy)]
    peers += [(near_x[a], near_y[b]) for a in SIDES for b in SIDES]
    for peer in peers:
        pl.semaphore_signal(barrier, inc=1, device_id=peer, device_id_type=MESH)

    in_e = load(0, e_in, eb)
    in_h = load(7, h_in, hb)
    in_wz = load(5, wz_in, wz)
    in_wy = load(6, wy_in, wy)

    in_le = load(1, le_in, leb)
    in_lj = load(2, lj_in, ljb)
    in_eps = load(3, eps_in, epsb)
    in_mat = load(4, mat_in, mat)
    in_lh = load(8, lh_in, lhb)
    in_j = load(9, j_in, jb)
    in_blk = load(10, blk_in, blk)
    in_wt = load(11, wt_in, wt)
    in_wm = load(12, wm_in, wm)

    started = []

    def remote(src, dst, send_sem, recv_sem, target):
        copy = pltpu.make_async_remote_copy(
            src_ref=src, dst_ref=dst, send_sem=send_sem, recv_sem=recv_sem,
            device_id=target, device_id_type=MESH,
        )
        copy.start()
        started.append(copy)
        return copy

    def stage_u(k, field):
        for s in SIDES:
            uys[k, s, 0] = field[0, Y_FACE[s], :]
            uys[k, s, 1] = field[2, Y_FACE[s], :]

    def stage_corners(k, at, field):
        for s in SIDES:
            for t in SIDES:
                row = CORNER[s][t]
                cs[k, 2 * s + t, at : at + 1, :] = field[0, row : row + 1, :]
                cs[k, 2 * s + t, at + 1 : at + 2, :] = field[1, row : row + 1, :]

    def stage_v(k, field):
        for s in SIDES:
            vxs[k, s, 0] = field[1, X_FACE[s], :]
            vxs[k, s, 1] = field[2, X_FACE[s], :]
            vys[k, s, 0] = field[0, Y_FACE[s], :]
            vys[k, s, 1] = field[2, Y_FACE[s], :]

    def send_u(k, field):
        copies = []
        for s in SIDES:
            src = field.at[pl.ds(1, 2), pl.ds(s * (ROWS - NY), NY)]
            copies.append(
                remote(src, uxr.at[k, 1 - s], u_send.at[k, s], u_recv.at[k, s], (near_x[s], gy))
            )
        for s in SIDES:
            copies.append(
                remote(
                    uys.at[k, s], uyr.at[k, 1 - s], u_send.at[k, 2 + s], u_recv.at[k, 2 + s],
                    (gx, near_y[s]),
                )
            )
        return copies

    def send_corners(k):
        return [
            remote(
                cs.at[k, 2 * s + t], cr.at[k, 2 * (1 - s) + 1 - t],
                c_send.at[k, 2 * s + t], c_recv.at[k, 2 * s + t], (near_x[s], near_y[t]),
            )
            for s in SIDES
            for t in SIDES
        ]

    def send_v(k):
        copies = []
        for s in SIDES:
            copies.append(
                remote(
                    vxs.at[k, s], vxr.at[k, 1 - s], v_send.at[k, s], v_recv.at[k, s],
                    (near_x[s], gy),
                )
            )
        for s in SIDES:
            copies.append(
                remote(
                    vys.at[k, s], vyr.at[k, 1 - s], v_send.at[k, 2 + s], v_recv.at[k, 2 + s],
                    (gx, near_y[s]),
                )
            )
        return copies

    def arrived(copies):
        for copy in copies:
            copy.wait_recv()

    by_step = lambda rows: step[rows, :]
    by_dt = lambda rows: -DT
    by_one = lambda rows: 1.0

    in_e.wait()
    for c in range(3):
        e0[c] = eb[c].astype(F32)
    in_wz.wait()
    in_wy.wait()
    in_h.wait()
    for ex, rows in chunks():
        curl = curl_chunk(e0, ex, wz, wy, exact=True)
        for c in range(3):
            h1[c, rows, :] = hb[c, rows, :].astype(F32) - DT * curl[c]
    stage_u(F, e0)
    stage_v(F, h1)
    cs[...] = jnp.zeros_like(cs)
    stage_corners(0, 0, e0)

    in_mat.wait()
    in_eps.wait()
    zpick = (
        lax.broadcasted_iota(jnp.int32, (EZ, NZ), 0) == lax.broadcasted_iota(jnp.int32, (EZ, NZ), 1) >> 2
    ).astype(F32).astype(BF16)
    ypick = (
        lax.broadcasted_iota(jnp.int32, (NY, EY), 0) >> 2 == lax.broadcasted_iota(jnp.int32, (NY, EY), 1)
    ).astype(F32).astype(BF16)
    for ex, rows in chunks():
        picked = jnp.dot(mat[ex].astype(F32).astype(BF16), zpick, preferred_element_type=F32)
        plane = jnp.dot(ypick, picked.astype(BF16), preferred_element_type=F32)
        for a in range(4):
            drude[CHUNK * ex + NY * a : CHUNK * ex + NY * (a + 1), :] = plane
    step[...] = DT / epsb[...].astype(F32)
    in_le.wait()
    in_lj.wait()
    for c in range(3):
        total = leb[c].astype(F32) + PDT * drude[...] * ljb[c].astype(F32)
        tot1[c] = total
        sc1[c] = step[...] * total
    in_lh.wait()
    for ex, rows in chunks():
        curl = curl_chunk(sc1, ex, wz, wy)
        for c in range(3):
            mid1[c, rows, :] = lhb[c, rows, :].astype(F32) + curl[c]
    stage_u(A, sc1)
    stage_v(A, mid1)
    stage_corners(0, 2, sc1)
    for c in range(3):
        q[c] = sc1[c] * step[...]
    stage_corners(0, 4, q)

    in_blk.wait()
    ids[...] = jnp.zeros_like(ids)
    for s in SIDES:
        ids[s, 0:EY, 0:EZ] = blk[(EX - 1) * s]
        for ex in range(EX):
            ids[2 + s, ex : ex + 1, 0:EZ] = blk[ex, (EY - 1) * s : (EY - 1) * s + 1, :]
        for t in SIDES:
            line = blk[(EX - 1) * s, (EY - 1) * t : (EY - 1) * t + 1, :]
            cs[0, 2 * s + t, 6:7, 0:EZ] = line.astype(F32)
    pl.semaphore_wait(barrier, len(peers))
    fu = send_u(F, e0)
    fv = send_v(F)

    def pass_on(wave):
        for peer in near:
            pl.semaphore_signal(heard.at[wave], inc=1, device_id=peer, device_id_type=MESH)

    rc = send_corners(0)
    waves = gx_waves(n_gx)
    pass_on(0)
    au = send_u(A, sc1)
    av = send_v(A)
    marks = []
    for s in SIDES:
        marks.append(remote(ids.at[s], idr.at[1 - s], i_send.at[s], i_recv.at[s], (near_x[s], gy)))
        marks.append(
            remote(ids.at[2 + s], idr.at[3 - s], i_send.at[2 + s], i_recv.at[2 + s], (gx, near_y[s]))
        )

    m = 2.0 * gll_tables()
    w4 = (1.0, 5.0, 5.0, 1.0)
    for s in SIDES:
        end = 3 * s
        wxs[s, 0] = step[X_FACE[s], :]
        wxs[s, 1] = q[0, X_FACE[s], :]
        wys[s, 0] = step[Y_FACE[s], :]
        wys[s, 1] = q[1, Y_FACE[s], :]
        inner = [a for a in range(4) if a != end]
        for slot, c in ((2, 1), (3, 2)):
            acc = None
            for a in inner:
                r0 = NY * ((NX - 4) * s + a)
                term = (m[a, end] * w4[a]) * q[c, r0 : r0 + NY, :]
                acc = term if acc is None else acc + term
            wxs[s, slot] = acc
        for slot, c in ((2, 0), (3, 2)):
            acc = None
            for a in inner:
                term = (m[a, end] * w4[a]) * q[c, pl.ds((NY - 4) * s + a, NX, stride=NY), :]
                acc = term if acc is None else acc + term
            wys[s, slot] = acc
    ws = []
    for s in SIDES:
        to_x, to_y = (near_x[s], gy), (gx, near_y[s])
        ws.append(remote(wxs.at[s], wxr.at[1 - s], w_send.at[s], w_recv.at[s], to_x))
        ws.append(remote(wys.at[s], wyr.at[1 - s], w_send.at[2 + s], w_recv.at[2 + s], to_y))

    n_rows = gsend.shape[0]
    eye = lax.broadcasted_iota(jnp.int32, (EZ, EZ), 0) == lax.broadcasted_iota(jnp.int32, (EZ, EZ), 1)
    ones = jnp.ones((EZ, 128), BF16)

    def mark(at, rows):
        coarse = jnp.concatenate(
            [jnp.where(eye, (r & -16).astype(F32), 0.0) for r in rows], axis=0
        ).astype(BF16)
        fine = jnp.concatenate(
            [jnp.where(eye, (r & 15).astype(F32), 0.0) for r in rows], axis=0
        ).astype(BF16)
        column = jnp.dot(coarse, ones, preferred_element_type=F32) + jnp.dot(
            fine, ones, preferred_element_type=F32
        )
        column = column.astype(jnp.int32)
        lane = lax.broadcasted_iota(jnp.int32, column.shape, 1)
        for n in range(n_rows):
            onehot[at : at + EZ * len(rows), 128 * n : 128 * (n + 1)] = (
                (column == lane + 128 * n).astype(F32).astype(BF16)
            )

    layer_len = EY * EZ
    for ex in range(EX):
        mark(layer_len * ex, [blk[ex, ey : ey + 1, :] for ey in range(EY)])
    x_at = layer_len * EX
    y_at = x_at + 2 * layer_len
    c_at = y_at + 2 * EX * EZ

    pl.semaphore_wait(heard.at[0], len(near))
    if waves > 1:
        pass_on(1)

    in_j.wait()
    arrived(fu)
    add_faces(uxr.at[F], uyr.at[F], h1, by_dt)
    for ex, rows in chunks():
        curl = curl_chunk(h1, ex, wz, wy)
        for c in range(3):
            e1[c, rows, :] = e0[c, rows, :] + step[rows, :] * (
                curl[c] - drude[rows, :] * jb[c, rows, :].astype(F32)
            )
    arrived(fv)
    arrived(rc)
    complete_faces(vxr.at[F], vyr.at[F], cr.at[0], 0, e0, -DT)
    add_faces(vxr.at[F], vyr.at[F], e1, by_step)

    arrived(au)
    add_faces(uxr.at[A], uyr.at[A], mid1, by_one)
    for ex, rows in chunks():
        curl = curl_chunk(mid1, ex, wz, wy)
        for c in range(3):
            lj = drude[rows, :] * (DECAY * ljb[c, rows, :].astype(F32) - sc1[c, rows, :])
            lj1[c, rows, :] = lj
            tot0[c, rows, :] = tot1[c, rows, :] - DT * curl[c] + PDT * lj

    for ex, rows in chunks():
        curl = curl_chunk(e1, ex, wz, wy)
        for c in range(3):
            h2[c, rows, :] = h1[c, rows, :] - DT * curl[c]
    for ex, rows in chunks():
        curl = curl_chunk(h2, ex, wz, wy)
        node = None
        for c in range(3):
            current = drude[rows, :] * (DECAY * jb[c, rows, :].astype(F32) + PDT * e1[c, rows, :])
            term = q[c, rows, :] * (curl[c] - current)
            node = term if node is None else node + term
        part[rows, :] = node
    back = LIFT * LIFT * DT
    for s in SIDES:
        x, y = X_FACE[s], Y_FACE[s]
        part[x, :] -= back * (q[1, x, :] * e1[1, x, :] + q[2, x, :] * e1[2, x, :])
        part[y, :] -= back * (q[0, y, :] * e1[0, y, :] + q[2, y, :] * e1[2, y, :])

    arrived(marks)
    mark(x_at, [idr[s, ey : ey + 1, 0:EZ] for s in SIDES for ey in range(EY)])
    mark(y_at, [idr[2 + s, ex : ex + 1, 0:EZ] for s in SIDES for ex in range(EX)])
    mark(c_at, [cr[0, k, 6:7, 0:EZ].astype(jnp.int32) for k in range(4)])
    xa = [-FACE[s] * DT * e1[2, X_FACE[s], :] for s in SIDES]
    xb = [FACE[s] * DT * e1[1, X_FACE[s], :] for s in SIDES]
    ya = [FACE[s] * DT * e1[2, Y_FACE[s], :] for s in SIDES]
    yb = [-FACE[s] * DT * e1[0, Y_FACE[s], :] for s in SIDES]

    def along_z(value):
        high, low = split(value)
        out = jnp.dot(jnp.concatenate([high, low], axis=1), wz[...], preferred_element_type=F32)
        return out[:, 0:NZ] + out[:, NZ : 2 * NZ]

    def along_rows(values):
        n = values[0].shape[0]
        high, low = split(jnp.concatenate(values, axis=1))
        top, rest = wy[0:n, 0:n], wy[CHUNK : CHUNK + n, 0:n]
        out = (
            jnp.dot(top, high, preferred_element_type=F32)
            + jnp.dot(top, low, preferred_element_type=F32)
            + jnp.dot(rest, high, preferred_element_type=F32)
        )
        return out[:, 0:NZ], out[:, NZ : 2 * NZ]

    xaz, yaz = [along_z(v) for v in xa], [along_z(v) for v in ya]
    xby, ybx = along_rows(xb), along_rows(yb)
    for s in SIDES:
        xt[s] = xby[s] - xaz[s]
        yt[s] = yaz[s] - ybx[s]

    in_wt.wait()
    in_wm.wait()
    scale = -1.0 / (216.0 * 8.0 * DT)

    def by_element(layers, count, weights):
        n = layers[0].shape[0]
        high, low = split(jnp.concatenate(layers, axis=0))
        w = wt[:, 0 : count * EZ]
        wide = jnp.dot(high, w, preferred_element_type=F32) + jnp.dot(
            low, w, preferred_element_type=F32
        )
        return [
            jnp.sum(wide[n * i : n * (i + 1)] * weights, axis=0, keepdims=True)
            for i in range(len(layers))
        ]

    def by_block(flats, at):
        out = None
        for i, flat in enumerate(flats):
            n = flat.shape[1]
            row = lax.broadcasted_iota(jnp.int32, (16, n), 0)
            flat = jnp.broadcast_to(flat, (16, n))
            top = flat.astype(BF16).astype(F32)
            pieces = jnp.where(row == 0, top, jnp.where(row == 1, flat - top, 0.0)).astype(BF16)
            term = jnp.dot(
                pieces, onehot[at + n * i : at + n * (i + 1), :], preferred_element_type=F32
            )
            out = term if out is None else out + term
        return out

    def layers_of(values):
        out = []
        for ex in range(EX):
            n = [values[CHUNK * ex + NY * a : CHUNK * ex + NY * (a + 1), :] for a in range(4)]
            out.append(n[0] + n[3] + 5.0 * (n[1] + n[2]))
        return out

    sums[...] = by_block(by_element(layers_of(part), EY, wm[...]), 0)

    arrived(av)
    complete_faces(vxr.at[A], vyr.at[A], cr.at[0], 2, sc1, 1.0)
    add_faces(vxr.at[A], vyr.at[A], tot0, by_dt)
    for c in range(3):
        sc0[c] = step[...] * tot0[c]
    stage_u(B, sc0)
    stage_corners(1, 0, sc0)
    bu = send_u(B, sc0)
    bc = send_corners(1)
    early = None
    for c in range(3):
        term = sc0[c] * (e1[c] - e0[c])
        early = term if early is None else early + term
    part[...] = early
    sums[...] += by_block(by_element(layers_of(part), EY, wm[...]), 0)

    arrived(ws)
    planes = []
    for s in SIDES:
        w = wxr.at[s]
        hy, hz = h2[1, X_FACE[s], :], h2[2, X_FACE[s], :]
        planes.append(
            w[1] * xt[s] - w[2] * (FACE[s] * DT * e1[1, X_FACE[s], :])
            - w[3] * (FACE[s] * DT * e1[2, X_FACE[s], :])
            + FACE[s] * w[0] * (uxr[A, s, 0] * hz - uxr[A, s, 1] * hy)
        )
    for s in SIDES:
        w = wyr.at[s]
        hx, hz = h2[0, Y_FACE[s], :], h2[2, Y_FACE[s], :]
        planes.append(
            w[1] * yt[s] - w[2] * (FACE[s] * DT * e1[0, Y_FACE[s], :])
            - w[3] * (FACE[s] * DT * e1[2, Y_FACE[s], :])
            + FACE[s] * w[0] * (uyr[A, s, 1] * hx - uyr[A, s, 0] * hz)
        )
    for s in SIDES:
        for t in SIDES:
            row = CORNER[s][t]
            planes.append(
                (-FACE[s] * FACE[t] * DT)
                * (
                    cr[0, 2 * s + t, 5:6, :] * e1[0, row : row + 1, :]
                    + cr[0, 2 * s + t, 4:5, :] * e1[1, row : row + 1, :]
                )
            )
    eighths = [jnp.broadcast_to(p, (8, NZ)) for p in planes[4:8]]
    late = (
        sums[...]
        + by_block(by_element(planes[0:2], EY, wm[...]), x_at)
        + by_block(by_element(planes[2:4], EX, wm[0:NX, 0 : EX * EZ]), y_at)
        + by_block(by_element(eighths, 1, 0.125), c_at)
    )
    total = jnp.sum(late, axis=0, keepdims=True) * scale
    for n in range(n_rows):
        gsend[n] = total[:, 128 * n : 128 * (n + 1)]
    for wave in range(1, waves):
        pl.semaphore_wait(heard.at[wave], len(near))
        if wave + 1 < waves:
            pass_on(wave + 1)
    width = 2 * n_gy
    per_row = 128 // width
    phase1 = []
    for k in range(1, n_gx):
        p = lax.rem(gx + k, n_gx)
        phase1.append(
            remote(
                gsend.at[lax.div(p, per_row)], grecv.at[k], g_send_sem.at[k], g_recv_sem.at[k], (p, gy)
            )
        )

    for ex, rows in chunks():
        curl = curl_chunk(sc0, ex, wz, wy)
        for c in range(3):
            mid0[c, rows, :] = mid1[c, rows, :] + curl[c]
    stage_v(B, mid0)
    bv = send_v(B)
    for c in range(3):
        oj_out[c] = (drude[...] * (DECAY * lj1[c] - sc0[c])).astype(BF16)

    mine = gsend[lax.div(gx, per_row)]
    arrived(phase1)
    for k in range(1, n_gx):
        mine = mine + grecv[k]
    msend[...] = mine
    phase2 = []
    for k in range(1, n_gy):
        phase2.append(
            remote(
                msend, mrecv.at[k], m_send_sem.at[k], m_recv_sem.at[k], (gx, lax.rem(gy + k, n_gy))
            )
        )

    arrived(bu)
    add_faces(uxr.at[B], uyr.at[B], mid0, by_one)
    for c in range(3):
        oh_out[c] = mid0[c].astype(BF16)
    for ex, rows in chunks():
        curl = curl_chunk(mid0, ex, wz, wy)
        for c in range(3):
            le0[c, rows, :] = tot0[c, rows, :] - DT * curl[c]
    arrived(bv)
    arrived(bc)
    complete_faces(vxr.at[B], vyr.at[B], cr.at[1], 0, sc0, 1.0)
    add_faces(vxr.at[B], vyr.at[B], le0, by_dt)
    for c in range(3):
        oe_out[c] = le0[c].astype(BF16)

    for copy in started:
        copy.wait_send()
    arrived(phase2)
    for k in range(1, n_gy):
        mine = mine + mrecv[k]
    at = lax.rem(gx, per_row) * width + 2 * gy
    lanes = lax.broadcasted_iota(jnp.int32, (1, 128), 1)
    first = jnp.sum(jnp.where(lanes == at, mine, 0.0), axis=1, keepdims=True)
    second = jnp.sum(jnp.where(lanes == at + 1, mine, 0.0), axis=1, keepdims=True)
    grad_ref[...] = jnp.where(lanes == 0, first, second)


def write_out(e_in, h_in, j_in, g_in, e_out, h_out, j_out, g_out, sem):
    pairs = ((e_in, e_out), (h_in, h_out), (j_in, j_out))
    copies = [pltpu.make_async_copy(a, b, sem.at[i]) for i, (a, b) in enumerate(pairs)]
    for copy in copies:
        copy.start()
    g_out[...] = g_in[0, 0:2]
    for copy in copies:
        copy.wait()


def per_device(n_gx, n_gy, *args):
    fields = [a.reshape(3, ROWS, NZ) for a in args[0:6]]
    eps = args[6].reshape(ROWS, NZ)
    blocks = EX * n_gx // CB * (EY * n_gy // CB)
    n_rows = -(-blocks // 128)
    consts = [jnp.asarray(a) for a in constant_arrays()]
    hbm = pl.BlockSpec(memory_space=pl.ANY)
    field32 = pltpu.VMEM((3, ROWS, NZ), F32)
    field16 = pltpu.VMEM((3, ROWS, NZ), BF16)
    plane32 = pltpu.VMEM((ROWS, NZ), F32)
    out16 = jax.ShapeDtypeStruct((3, ROWS, NZ), BF16)
    dma = pltpu.SemaphoreType.DMA
    x_faces = pltpu.VMEM((3, 2, 2, NY, NZ), F32)
    y_faces = pltpu.VMEM((3, 2, 2, NX, NZ), F32)
    corners = pltpu.VMEM((2, 4, 8, NZ), F32)
    weights = [
        pltpu.VMEM((2, 4, NY, NZ), F32),
        pltpu.VMEM((2, 4, NX, NZ), F32),
        pltpu.VMEM((4, 8, 128), jnp.int32),
    ]
    marked = EX * EY * EZ + 2 * EY * EZ + 2 * EX * EZ + 4 * EZ
    oe, oh, oj, grad = pl.pallas_call(
        functools.partial(kernel, n_gx, n_gy),
        out_shape=(pltpu.VMEM((3, ROWS, NZ), BF16),) * 3 + (pltpu.VMEM((1, 128), F32),),
        in_specs=[hbm] * 13,
        out_specs=(pl.BlockSpec(memory_space=pltpu.VMEM),) * 4,
        scratch_shapes=[
            *[field16] * 6,
            pltpu.VMEM((ROWS, NZ), BF16),
            pltpu.VMEM((EX, EY, EZ), jnp.int32),
            pltpu.VMEM((EX, EY, EZ), jnp.int32),
            *[pltpu.VMEM(a.shape, a.dtype) for a in consts],
            *[field32] * 13,
            plane32,
            plane32,
            plane32,
            pltpu.VMEM((2, NY, NZ), F32),
            pltpu.VMEM((2, NX, NZ), F32),
            pltpu.VMEM((16, 128 * n_rows), F32),
            pltpu.VMEM((marked, 128 * n_rows), BF16),
            y_faces, x_faces, y_faces, corners,
            x_faces, y_faces, x_faces, y_faces, corners,
            *weights,
            *weights,
            pltpu.VMEM((n_rows, 1, 128), F32),
            pltpu.VMEM((n_gx, 1, 128), F32),
            pltpu.VMEM((1, 128), F32),
            pltpu.VMEM((n_gy, 1, 128), F32),
            dma((13,)),
            dma((3, 4)), dma((3, 4)), dma((3, 4)), dma((3, 4)), dma((2, 4)), dma((2, 4)),
            dma((4,)), dma((4,)), dma((4,)), dma((4,)),
            dma((n_gx,)), dma((n_gx,)), dma((n_gy,)), dma((n_gy,)),
            pltpu.SemaphoreType.REGULAR((gx_waves(n_gx),)),
        ],
        compiler_params=pltpu.CompilerParams(
            collective_id=0, has_side_effects=True, vmem_limit_bytes=60 * 1024 * 1024
        ),
    )(*fields, eps, args[7], args[8], *consts)
    oe, oh, oj, grad = pl.pallas_call(
        write_out,
        out_shape=(out16, out16, out16, jax.ShapeDtypeStruct((2,), F32)),
        in_specs=[pl.BlockSpec(memory_space=pltpu.VMEM)] * 4,
        out_specs=(hbm, hbm, hbm, pl.BlockSpec(memory_space=pltpu.VMEM)),
        scratch_shapes=[dma((3,))],
        compiler_params=pltpu.CompilerParams(vmem_limit_bytes=4 * 1024 * 1024),
    )(oe, oh, oj, grad)
    shape = args[0].shape
    return oe.reshape(shape), oh.reshape(shape), oj.reshape(shape), grad


def solution(mesh):
    n_gx, n_gy = mesh.shape["gx"], mesh.shape["gy"]
    field = P(None, "gx", "gy", None)
    node = P("gx", "gy", None)
    return jax.shard_map(
        functools.partial(per_device, n_gx, n_gy),
        mesh=mesh,
        in_specs=(field,) * 6 + (node,) * 3,
        out_specs=(field, field, field, P(("gx", "gy"))),
        check_vma=False,
    )
```

```python
import functools
import math

import jax
import jax.numpy as jnp
import numpy as np
from jax import lax
from jax.experimental import pallas as pl
from jax.experimental.pallas import tpu as pltpu
from jax.sharding import PartitionSpec as P

CB = 3
DT = 0.06
DECAY = 0.96
PLASMA = 16.0
PDT = PLASMA * DT
LIFT = 6.0
MESH = pl.DeviceIdType.MESH
F32 = jnp.float32
BF16 = jnp.bfloat16

EX, EY, EZ = 3, 6, 32
NX, NY, NZ = 4 * EX, 4 * EY, 4 * EZ
ROWS = NX * NY
CHUNK = 4 * NY


def gll_tables():
    points = np.array([-1.0, -math.sqrt(0.2), math.sqrt(0.2), 1.0])
    products = np.array(
        [np.prod([points[i] - points[j] for j in range(4) if j != i]) for i in range(4)]
    )
    matrix = np.zeros((4, 4))
    for i in range(4):
        for j in range(4):
            if i != j:
                matrix[i, j] = products[i] / products[j] / (points[i] - points[j])
    for i in range(4):
        matrix[i, i] = -np.sum(matrix[i])
    return matrix


def line_matrix(elements):
    n = 4 * elements
    full = np.kron(np.eye(elements), 2.0 * gll_tables())
    for e in range(elements):
        lo, hi = 4 * e, 4 * e + 3
        full[hi, hi] -= LIFT
        if hi + 1 < n:
            full[hi, hi + 1] += LIFT
        full[lo, lo] += LIFT
        if lo > 0:
            full[lo, lo - 1] -= LIFT
    return full


def two_parts(matrix):
    high = matrix.astype(np.float32).astype(jnp.bfloat16)
    low = (matrix - high.astype(np.float64)).astype(np.float32).astype(jnp.bfloat16)
    return high, low


def constant_arrays():
    zh, zl = two_parts(line_matrix(EZ).T)
    wz = np.block([[zh, zl], [zh, zl]])
    yh, yl = two_parts(np.kron(np.eye(4), line_matrix(EY)))
    wy = np.block([[yh, yh], [yl, yl]])
    w4 = np.array([1.0, 5.0, 5.0, 1.0])
    wsum = np.kron(np.eye(EZ), w4.reshape(4, 1))
    wt = np.tile(wsum, (1, EY)).astype(jnp.bfloat16)
    wm = np.kron(np.kron(np.eye(EY), w4.reshape(4, 1)), np.ones((1, EZ))).astype(np.float32)
    return wz, wy, wt, wm


def split(value):
    high = value.astype(BF16)
    low = (value - high.astype(F32)).astype(BF16)
    return high, low


def curl_chunk(src, ex, wz_ref, wy_ref, exact=False):
    r0 = CHUNK * ex
    comps = [src[c, r0 : r0 + CHUNK, :] for c in range(3)]
    if exact:
        high = [v.astype(BF16) for v in comps]
        zin = jnp.concatenate([high[0], high[1]], axis=0)
        zout = jnp.dot(zin, wz_ref[0:NZ, :], preferred_element_type=F32)
        yin = jnp.concatenate([high[0], high[2]], axis=1)
        yout = jnp.dot(wy_ref[:, 0:CHUNK], yin, preferred_element_type=F32)
    else:
        high, low = zip(*[split(v) for v in comps])
        zin = jnp.concatenate(
            [
                jnp.concatenate([high[0], low[0]], axis=1),
                jnp.concatenate([high[1], low[1]], axis=1),
            ],
            axis=0,
        )
        zout = jnp.dot(zin, wz_ref[...], preferred_element_type=F32)
        yin = jnp.concatenate(
            [
                jnp.concatenate([high[0], high[2]], axis=1),
                jnp.concatenate([low[0], low[2]], axis=1),
            ],
            axis=0,
        )
        yout = jnp.dot(wy_ref[...], yin, preferred_element_type=F32)
    zsum = zout[:, 0:NZ] + zout[:, NZ : 2 * NZ]
    dz_x, dz_y = zsum[0:CHUNK], zsum[CHUNK : 2 * CHUNK]
    ysum = yout[0:CHUNK] + yout[CHUNK : 2 * CHUNK]
    dy_x, dy_z = ysum[:, 0:NZ], ysum[:, NZ : 2 * NZ]

    m = 2.0 * gll_tables()

    def along_x(c):
        p = [comps[c][NY * a : NY * (a + 1)] for a in range(4)]
        out0 = m[0, 1] * p[1] + m[0, 2] * p[2] + m[0, 3] * p[3]
        if ex > 0:
            out0 = out0 - LIFT * src[c, r0 - NY : r0, :]
        out1 = m[1, 0] * p[0] + m[1, 2] * p[2] + m[1, 3] * p[3]
        out2 = m[2, 0] * p[0] + m[2, 1] * p[1] + m[2, 3] * p[3]
        out3 = m[3, 0] * p[0] + m[3, 1] * p[1] + m[3, 2] * p[2]
        if ex < EX - 1:
            out3 = out3 + LIFT * src[c, r0 + CHUNK : r0 + CHUNK + NY, :]
        return jnp.concatenate([out0, out1, out2, out3], axis=0)

    dx_y, dx_z = along_x(1), along_x(2)
    return dy_z - dz_y, dz_x - dx_z, dx_y - dy_x


LOW, HIGH = 0, 1
SIDES = (LOW, HIGH)
FIRST_X = slice(0, NY)
LAST_X = slice(ROWS - NY, ROWS)
X_FACE = (FIRST_X, LAST_X)
Y_FACE = (pl.ds(0, NX, stride=NY), pl.ds(NY - 1, NX, stride=NY))
CORNER = ((0, NY - 1), (ROWS - NY, ROWS - 1))
FACE = (-LIFT, LIFT)
F, A, B = 0, 1, 2


def gx_steps(n):
    return sorted({d % n for step in (1, 4) if step < n for d in (step, -step)} - {0})


def gx_waves(n):
    known, waves = {0, *gx_steps(n)}, 0
    while len(known) < n or not waves:
        known |= {(a + b) % n for a in known for b in gx_steps(n)}
        waves += 1
    return waves


def chunks():
    return [(ex, slice(CHUNK * ex, CHUNK * (ex + 1))) for ex in range(EX)]


def add_faces(xr, yr, field, factor):
    for s in SIDES:
        f = factor(X_FACE[s]) * FACE[s]
        field[1, X_FACE[s], :] -= f * xr[s, 1]
        field[2, X_FACE[s], :] += f * xr[s, 0]
    for s in SIDES:
        f = factor(Y_FACE[s]) * FACE[s]
        field[0, Y_FACE[s], :] += f * yr[s, 1]
        field[2, Y_FACE[s], :] -= f * yr[s, 0]


def complete_faces(xr, yr, corners, at, field, factor):
    for s in SIDES:
        f = -FACE[s] * factor
        xr[s, 0] -= f * field[2, X_FACE[s], :]
        xr[s, 1] += f * field[1, X_FACE[s], :]
        xr[s, 1, 0:1, :] -= FACE[LOW] * factor * corners[2 * s + LOW, at : at + 1, :]
        xr[s, 1, NY - 1 : NY, :] -= FACE[HIGH] * factor * corners[2 * s + HIGH, at : at + 1, :]
    for s in SIDES:
        f = -FACE[s] * factor
        yr[s, 0] += f * field[2, Y_FACE[s], :]
        yr[s, 1] -= f * field[0, Y_FACE[s], :]
        yr[s, 1, 0:1, :] += FACE[LOW] * factor * corners[2 * LOW + s, at + 1 : at + 2, :]
        yr[s, 1, NX - 1 : NX, :] += FACE[HIGH] * factor * corners[2 * HIGH + s, at + 1 : at + 2, :]


def kernel(
    n_gx,
    n_gy,
    e_in, h_in, j_in, le_in, lh_in, lj_in, eps_in, mat_in, blk_in, wz_in, wy_in, wt_in, wm_in,
    oe_out, oh_out, oj_out, grad_ref,
    eb, hb, jb, leb, lhb, ljb, epsb, mat, blk, wz, wy, wt, wm,
    e0, h1, e1, h2, tot1, sc1, mid1, tot0, sc0, mid0, le0, lj1, q,
    step, drude, part, xt, yt, sums, onehot,
    uys, vxs, vys, cs, uxr, uyr, vxr, vyr, cr,
    wxs, wys, ids, wxr, wyr, idr,
    gsend, grecv, msend, mrecv,
    in_sem, u_send, u_recv, v_send, v_recv, c_send, c_recv,
    w_send, w_recv, i_send, i_recv, g_send_sem, g_recv_sem, m_send_sem, m_recv_sem, heard,
):
    gx, gy = lax.axis_index("gx"), lax.axis_index("gy")
    near_x = (lax.rem(gx + n_gx - 1, n_gx), lax.rem(gx + 1, n_gx))
    near_y = (lax.rem(gy + n_gy - 1, n_gy), lax.rem(gy + 1, n_gy))

    def load(index, src, dst):
        copy = pltpu.make_async_copy(src, dst, in_sem.at[index])
        copy.start()
        return copy

    barrier = pltpu.get_barrier_semaphore()
    near = [(lax.rem(gx + d, n_gx), gy) for d in gx_steps(n_gx)]
    peers = near + [(gx, lax.rem(gy + k, n_gy)) for k in range(1, n_gy)]
    peers += [(near_x[a], near_y[b]) for a in SIDES for b in SIDES]
    for peer in peers:
        pl.semaphore_signal(barrier, inc=1, device_id=peer, device_id_type=MESH)

    in_e = load(0, e_in, eb)
    in_h = load(7, h_in, hb)
    in_wz = load(5, wz_in, wz)
    in_wy = load(6, wy_in, wy)

    in_le = load(1, le_in, leb)
    in_lj = load(2, lj_in, ljb)
    in_eps = load(3, eps_in, epsb)
    in_mat = load(4, mat_in, mat)
    in_lh = load(8, lh_in, lhb)
    in_j = load(9, j_in, jb)
    in_blk = load(10, blk_in, blk)
    in_wt = load(11, wt_in, wt)
    in_wm = load(12, wm_in, wm)

    started = []

    def remote(src, dst, send_sem, recv_sem, target):
        copy = pltpu.make_async_remote_copy(
            src_ref=src, dst_ref=dst, send_sem=send_sem, recv_sem=recv_sem,
            device_id=target, device_id_type=MESH,
        )
        copy.start()
        started.append(copy)
        return copy

    def stage_u(k, field):
        for s in SIDES:
            uys[k, s, 0] = field[0, Y_FACE[s], :]
            uys[k, s, 1] = field[2, Y_FACE[s], :]

    def stage_corners(k, at, field):
        for s in SIDES:
            for t in SIDES:
                row = CORNER[s][t]
                cs[k, 2 * s + t, at : at + 1, :] = field[0, row : row + 1, :]
                cs[k, 2 * s + t, at + 1 : at + 2, :] = field[1, row : row + 1, :]

    def stage_v(k, field):
        for s in SIDES:
            vxs[k, s, 0] = field[1, X_FACE[s], :]
            vxs[k, s, 1] = field[2, X_FACE[s], :]
            vys[k, s, 0] = field[0, Y_FACE[s], :]
            vys[k, s, 1] = field[2, Y_FACE[s], :]

    def send_u(k, field):
        copies = []
        for s in SIDES:
            src = field.at[pl.ds(1, 2), pl.ds(s * (ROWS - NY), NY)]
            copies.append(
                remote(src, uxr.at[k, 1 - s], u_send.at[k, s], u_recv.at[k, s], (near_x[s], gy))
            )
        for s in SIDES:
            copies.append(
                remote(
                    uys.at[k, s], uyr.at[k, 1 - s], u_send.at[k, 2 + s], u_recv.at[k, 2 + s],
                    (gx, near_y[s]),
                )
            )
        return copies

    def send_corners(k):
        return [
            remote(
                cs.at[k, 2 * s + t], cr.at[k, 2 * (1 - s) + 1 - t],
                c_send.at[k, 2 * s + t], c_recv.at[k, 2 * s + t], (near_x[s], near_y[t]),
            )
            for s in SIDES
            for t in SIDES
        ]

    def send_v(k):
        copies = []
        for s in SIDES:
            copies.append(
                remote(
                    vxs.at[k, s], vxr.at[k, 1 - s], v_send.at[k, s], v_recv.at[k, s],
                    (near_x[s], gy),
                )
            )
        for s in SIDES:
            copies.append(
                remote(
                    vys.at[k, s], vyr.at[k, 1 - s], v_send.at[k, 2 + s], v_recv.at[k, 2 + s],
                    (gx, near_y[s]),
                )
            )
        return copies

    def arrived(copies):
        for copy in copies:
            copy.wait_recv()

    by_step = lambda rows: step[rows, :]
    by_dt = lambda rows: -DT
    by_one = lambda rows: 1.0

    in_e.wait()
    for c in range(3):
        e0[c] = eb[c].astype(F32)
    in_wz.wait()
    in_wy.wait()
    in_h.wait()
    for ex, rows in chunks():
        curl = curl_chunk(e0, ex, wz, wy, exact=True)
        for c in range(3):
            h1[c, rows, :] = hb[c, rows, :].astype(F32) - DT * curl[c]
    stage_u(F, e0)
    stage_v(F, h1)
    cs[...] = jnp.zeros_like(cs)
    stage_corners(0, 0, e0)

    pl.semaphore_wait(barrier, len(peers))
    fu = send_u(F, e0)
    fv = send_v(F)

    def pass_on(wave):
        for peer in near:
            pl.semaphore_signal(heard.at[wave], inc=1, device_id=peer, device_id_type=MESH)


    in_mat.wait()
    in_eps.wait()
    zpick = (
        lax.broadcasted_iota(jnp.int32, (EZ, NZ), 0) == lax.broadcasted_iota(jnp.int32, (EZ, NZ), 1) >> 2
    ).astype(F32).astype(BF16)
    ypick = (
        lax.broadcasted_iota(jnp.int32, (NY, EY), 0) >> 2 == lax.broadcasted_iota(jnp.int32, (NY, EY), 1)
    ).astype(F32).astype(BF16)
    for ex, rows in chunks():
        picked = jnp.dot(mat[ex].astype(F32).astype(BF16), zpick, preferred_element_type=F32)
        plane = jnp.dot(ypick, picked.astype(BF16), preferred_element_type=F32)
        for a in range(4):
            drude[CHUNK * ex + NY * a : CHUNK * ex + NY * (a + 1), :] = plane
    step[...] = DT / epsb[...].astype(F32)
    in_le.wait()
    in_lj.wait()
    for c in range(3):
        total = leb[c].astype(F32) + PDT * drude[...] * ljb[c].astype(F32)
        tot1[c] = total
        sc1[c] = step[...] * total
    in_lh.wait()
    for ex, rows in chunks():
        curl = curl_chunk(sc1, ex, wz, wy)
        for c in range(3):
            mid1[c, rows, :] = lhb[c, rows, :].astype(F32) + curl[c]
    stage_u(A, sc1)
    stage_v(A, mid1)
    stage_corners(0, 2, sc1)
    for c in range(3):
        q[c] = sc1[c] * step[...]
    stage_corners(0, 4, q)

    in_blk.wait()
    ids[...] = jnp.zeros_like(ids)
    for s in SIDES:
        ids[s, 0:EY, 0:EZ] = blk[(EX - 1) * s]
        for ex in range(EX):
            ids[2 + s, ex : ex + 1, 0:EZ] = blk[ex, (EY - 1) * s : (EY - 1) * s + 1, :]
        for t in SIDES:
            line = blk[(EX - 1) * s, (EY - 1) * t : (EY - 1) * t + 1, :]
            cs[0, 2 * s + t, 6:7, 0:EZ] = line.astype(F32)
    rc = send_corners(0)
    waves = gx_waves(n_gx)
    pass_on(0)
    au = send_u(A, sc1)
    av = send_v(A)
    marks = []
    for s in SIDES:
        marks.append(remote(ids.at[s], idr.at[1 - s], i_send.at[s], i_recv.at[s], (near_x[s], gy)))
        marks.append(
            remote(ids.at[2 + s], idr.at[3 - s], i_send.at[2 + s], i_recv.at[2 + s], (gx, near_y[s]))
        )

    m = 2.0 * gll_tables()
    w4 = (1.0, 5.0, 5.0, 1.0)
    for s in SIDES:
        end = 3 * s
        wxs[s, 0] = step[X_FACE[s], :]
        wxs[s, 1] = q[0, X_FACE[s], :]
        wys[s, 0] = step[Y_FACE[s], :]
        wys[s, 1] = q[1, Y_FACE[s], :]
        inner = [a for a in range(4) if a != end]
        for slot, c in ((2, 1), (3, 2)):
            acc = None
            for a in inner:
                r0 = NY * ((NX - 4) * s + a)
                term = (m[a, end] * w4[a]) * q[c, r0 : r0 + NY, :]
                acc = term if acc is None else acc + term
            wxs[s, slot] = acc
        for slot, c in ((2, 0), (3, 2)):
            acc = None
            for a in inner:
                term = (m[a, end] * w4[a]) * q[c, pl.ds((NY - 4) * s + a, NX, stride=NY), :]
                acc = term if acc is None else acc + term
            wys[s, slot] = acc
    ws = []
    for s in SIDES:
        to_x, to_y = (near_x[s], gy), (gx, near_y[s])
        ws.append(remote(wxs.at[s], wxr.at[1 - s], w_send.at[s], w_recv.at[s], to_x))
        ws.append(remote(wys.at[s], wyr.at[1 - s], w_send.at[2 + s], w_recv.at[2 + s], to_y))

    n_rows = gsend.shape[0]
    eye = lax.broadcasted_iota(jnp.int32, (EZ, EZ), 0) == lax.broadcasted_iota(jnp.int32, (EZ, EZ), 1)
    ones = jnp.ones((EZ, 128), BF16)

    def mark(at, rows):
        coarse = jnp.concatenate(
            [jnp.where(eye, (r & -16).astype(F32), 0.0) for r in rows], axis=0
        ).astype(BF16)
        fine = jnp.concatenate(
            [jnp.where(eye, (r & 15).astype(F32), 0.0) for r in rows], axis=0
        ).astype(BF16)
        column = jnp.dot(coarse, ones, preferred_element_type=F32) + jnp.dot(
            fine, ones, preferred_element_type=F32
        )
        column = column.astype(jnp.int32)
        lane = lax.broadcasted_iota(jnp.int32, column.shape, 1)
        for n in range(n_rows):
            onehot[at : at + EZ * len(rows), 128 * n : 128 * (n + 1)] = (
                (column == lane + 128 * n).astype(F32).astype(BF16)
            )

    layer_len = EY * EZ
    for ex in range(EX):
        mark(layer_len * ex, [blk[ex, ey : ey + 1, :] for ey in range(EY)])
    x_at = layer_len * EX
    y_at = x_at + 2 * layer_len
    c_at = y_at + 2 * EX * EZ

    pl.semaphore_wait(heard.at[0], len(near))
    if waves > 1:
        pass_on(1)

    in_j.wait()
    arrived(fu)
    add_faces(uxr.at[F], uyr.at[F], h1, by_dt)
    for ex, rows in chunks():
        curl = curl_chunk(h1, ex, wz, wy)
        for c in range(3):
            e1[c, rows, :] = e0[c, rows, :] + step[rows, :] * (
                curl[c] - drude[rows, :] * jb[c, rows, :].astype(F32)
            )
    arrived(fv)
    arrived(rc)
    complete_faces(vxr.at[F], vyr.at[F], cr.at[0], 0, e0, -DT)
    add_faces(vxr.at[F], vyr.at[F], e1, by_step)

    arrived(au)
    add_faces(uxr.at[A], uyr.at[A], mid1, by_one)
    for ex, rows in chunks():
        curl = curl_chunk(mid1, ex, wz, wy)
        for c in range(3):
            lj = drude[rows, :] * (DECAY * ljb[c, rows, :].astype(F32) - sc1[c, rows, :])
            lj1[c, rows, :] = lj
            tot0[c, rows, :] = tot1[c, rows, :] - DT * curl[c] + PDT * lj

    for ex, rows in chunks():
        curl = curl_chunk(e1, ex, wz, wy)
        for c in range(3):
            h2[c, rows, :] = h1[c, rows, :] - DT * curl[c]
    for ex, rows in chunks():
        curl = curl_chunk(h2, ex, wz, wy)
        node = None
        for c in range(3):
            current = drude[rows, :] * (DECAY * jb[c, rows, :].astype(F32) + PDT * e1[c, rows, :])
            term = q[c, rows, :] * (curl[c] - current)
            node = term if node is None else node + term
        part[rows, :] = node
    back = LIFT * LIFT * DT
    for s in SIDES:
        x, y = X_FACE[s], Y_FACE[s]
        part[x, :] -= back * (q[1, x, :] * e1[1, x, :] + q[2, x, :] * e1[2, x, :])
        part[y, :] -= back * (q[0, y, :] * e1[0, y, :] + q[2, y, :] * e1[2, y, :])

    arrived(marks)
    mark(x_at, [idr[s, ey : ey + 1, 0:EZ] for s in SIDES for ey in range(EY)])
    mark(y_at, [idr[2 + s, ex : ex + 1, 0:EZ] for s in SIDES for ex in range(EX)])
    mark(c_at, [cr[0, k, 6:7, 0:EZ].astype(jnp.int32) for k in range(4)])
    xa = [-FACE[s] * DT * e1[2, X_FACE[s], :] for s in SIDES]
    xb = [FACE[s] * DT * e1[1, X_FACE[s], :] for s in SIDES]
    ya = [FACE[s] * DT * e1[2, Y_FACE[s], :] for s in SIDES]
    yb = [-FACE[s] * DT * e1[0, Y_FACE[s], :] for s in SIDES]

    def along_z(value):
        high, low = split(value)
        out = jnp.dot(jnp.concatenate([high, low], axis=1), wz[...], preferred_element_type=F32)
        return out[:, 0:NZ] + out[:, NZ : 2 * NZ]

    def along_rows(values):
        n = values[0].shape[0]
        high, low = split(jnp.concatenate(values, axis=1))
        top, rest = wy[0:n, 0:n], wy[CHUNK : CHUNK + n, 0:n]
        out = (
            jnp.dot(top, high, preferred_element_type=F32)
            + jnp.dot(top, low, preferred_element_type=F32)
            + jnp.dot(rest, high, preferred_element_type=F32)
        )
        return out[:, 0:NZ], out[:, NZ : 2 * NZ]

    xaz, yaz = [along_z(v) for v in xa], [along_z(v) for v in ya]
    xby, ybx = along_rows(xb), along_rows(yb)
    for s in SIDES:
        xt[s] = xby[s] - xaz[s]
        yt[s] = yaz[s] - ybx[s]

    in_wt.wait()
    in_wm.wait()
    scale = -1.0 / (216.0 * 8.0 * DT)

    def by_element(layers, count, weights):
        n = layers[0].shape[0]
        high, low = split(jnp.concatenate(layers, axis=0))
        w = wt[:, 0 : count * EZ]
        wide = jnp.dot(high, w, preferred_element_type=F32) + jnp.dot(
            low, w, preferred_element_type=F32
        )
        return [
            jnp.sum(wide[n * i : n * (i + 1)] * weights, axis=0, keepdims=True)
            for i in range(len(layers))
        ]

    def by_block(flats, at):
        out = None
        for i, flat in enumerate(flats):
            n = flat.shape[1]
            row = lax.broadcasted_iota(jnp.int32, (16, n), 0)
            flat = jnp.broadcast_to(flat, (16, n))
            top = flat.astype(BF16).astype(F32)
            pieces = jnp.where(row == 0, top, jnp.where(row == 1, flat - top, 0.0)).astype(BF16)
            term = jnp.dot(
                pieces, onehot[at + n * i : at + n * (i + 1), :], preferred_element_type=F32
            )
            out = term if out is None else out + term
        return out

    def layers_of(values):
        out = []
        for ex in range(EX):
            n = [values[CHUNK * ex + NY * a : CHUNK * ex + NY * (a + 1), :] for a in range(4)]
            out.append(n[0] + n[3] + 5.0 * (n[1] + n[2]))
        return out

    sums[...] = by_block(by_element(layers_of(part), EY, wm[...]), 0)

    arrived(av)
    complete_faces(vxr.at[A], vyr.at[A], cr.at[0], 2, sc1, 1.0)
    add_faces(vxr.at[A], vyr.at[A], tot0, by_dt)
    for c in range(3):
        sc0[c] = step[...] * tot0[c]
    stage_u(B, sc0)
    stage_corners(1, 0, sc0)
    bu = send_u(B, sc0)
    bc = send_corners(1)
    early = None
    for c in range(3):
        term = sc0[c] * (e1[c] - e0[c])
        early = term if early is None else early + term
    part[...] = early
    sums[...] += by_block(by_element(layers_of(part), EY, wm[...]), 0)

    arrived(ws)
    planes = []
    for s in SIDES:
        w = wxr.at[s]
        hy, hz = h2[1, X_FACE[s], :], h2[2, X_FACE[s], :]
        planes.append(
            w[1] * xt[s] - w[2] * (FACE[s] * DT * e1[1, X_FACE[s], :])
            - w[3] * (FACE[s] * DT * e1[2, X_FACE[s], :])
            + FACE[s] * w[0] * (uxr[A, s, 0] * hz - uxr[A, s, 1] * hy)
        )
    for s in SIDES:
        w = wyr.at[s]
        hx, hz = h2[0, Y_FACE[s], :], h2[2, Y_FACE[s], :]
        planes.append(
            w[1] * yt[s] - w[2] * (FACE[s] * DT * e1[0, Y_FACE[s], :])
            - w[3] * (FACE[s] * DT * e1[2, Y_FACE[s], :])
            + FACE[s] * w[0] * (uyr[A, s, 1] * hx - uyr[A, s, 0] * hz)
        )
    for s in SIDES:
        for t in SIDES:
            row = CORNER[s][t]
            planes.append(
                (-FACE[s] * FACE[t] * DT)
                * (
                    cr[0, 2 * s + t, 5:6, :] * e1[0, row : row + 1, :]
                    + cr[0, 2 * s + t, 4:5, :] * e1[1, row : row + 1, :]
                )
            )
    eighths = [jnp.broadcast_to(p, (8, NZ)) for p in planes[4:8]]
    late = (
        sums[...]
        + by_block(by_element(planes[0:2], EY, wm[...]), x_at)
        + by_block(by_element(planes[2:4], EX, wm[0:NX, 0 : EX * EZ]), y_at)
        + by_block(by_element(eighths, 1, 0.125), c_at)
    )
    total = jnp.sum(late, axis=0, keepdims=True) * scale
    for n in range(n_rows):
        gsend[n] = total[:, 128 * n : 128 * (n + 1)]
    for wave in range(1, waves):
        pl.semaphore_wait(heard.at[wave], len(near))
        if wave + 1 < waves:
            pass_on(wave + 1)
    width = 2 * n_gy
    per_row = 128 // width
    phase1 = []
    for k in range(1, n_gx):
        p = lax.rem(gx + k, n_gx)
        phase1.append(
            remote(
                gsend.at[lax.div(p, per_row)], grecv.at[k], g_send_sem.at[k], g_recv_sem.at[k], (p, gy)
            )
        )

    for ex, rows in chunks():
        curl = curl_chunk(sc0, ex, wz, wy)
        for c in range(3):
            mid0[c, rows, :] = mid1[c, rows, :] + curl[c]
    stage_v(B, mid0)
    bv = send_v(B)
    for c in range(3):
        oj_out[c] = (drude[...] * (DECAY * lj1[c] - sc0[c])).astype(BF16)

    mine = gsend[lax.div(gx, per_row)]
    arrived(phase1)
    for k in range(1, n_gx):
        mine = mine + grecv[k]
    msend[...] = mine
    phase2 = []
    for k in range(1, n_gy):
        phase2.append(
            remote(
                msend, mrecv.at[k], m_send_sem.at[k], m_recv_sem.at[k], (gx, lax.rem(gy + k, n_gy))
            )
        )

    arrived(bu)
    add_faces(uxr.at[B], uyr.at[B], mid0, by_one)
    for c in range(3):
        oh_out[c] = mid0[c].astype(BF16)
    for ex, rows in chunks():
        curl = curl_chunk(mid0, ex, wz, wy)
        for c in range(3):
            le0[c, rows, :] = tot0[c, rows, :] - DT * curl[c]
    arrived(bv)
    arrived(bc)
    complete_faces(vxr.at[B], vyr.at[B], cr.at[1], 0, sc0, 1.0)
    add_faces(vxr.at[B], vyr.at[B], le0, by_dt)
    for c in range(3):
        oe_out[c] = le0[c].astype(BF16)

    for copy in started:
        copy.wait_send()
    arrived(phase2)
    for k in range(1, n_gy):
        mine = mine + mrecv[k]
    at = lax.rem(gx, per_row) * width + 2 * gy
    lanes = lax.broadcasted_iota(jnp.int32, (1, 128), 1)
    first = jnp.sum(jnp.where(lanes == at, mine, 0.0), axis=1, keepdims=True)
    second = jnp.sum(jnp.where(lanes == at + 1, mine, 0.0), axis=1, keepdims=True)
    grad_ref[...] = jnp.where(lanes == 0, first, second)


def write_out(e_in, h_in, j_in, g_in, e_out, h_out, j_out, g_out, sem):
    pairs = ((e_in, e_out), (h_in, h_out), (j_in, j_out))
    copies = [pltpu.make_async_copy(a, b, sem.at[i]) for i, (a, b) in enumerate(pairs)]
    for copy in copies:
        copy.start()
    g_out[...] = g_in[0, 0:2]
    for copy in copies:
        copy.wait()


def per_device(n_gx, n_gy, *args):
    fields = [a.reshape(3, ROWS, NZ) for a in args[0:6]]
    eps = args[6].reshape(ROWS, NZ)
    blocks = EX * n_gx // CB * (EY * n_gy // CB)
    n_rows = -(-blocks // 128)
    consts = [jnp.asarray(a) for a in constant_arrays()]
    hbm = pl.BlockSpec(memory_space=pl.ANY)
    field32 = pltpu.VMEM((3, ROWS, NZ), F32)
    field16 = pltpu.VMEM((3, ROWS, NZ), BF16)
    plane32 = pltpu.VMEM((ROWS, NZ), F32)
    out16 = jax.ShapeDtypeStruct((3, ROWS, NZ), BF16)
    dma = pltpu.SemaphoreType.DMA
    x_faces = pltpu.VMEM((3, 2, 2, NY, NZ), F32)
    y_faces = pltpu.VMEM((3, 2, 2, NX, NZ), F32)
    corners = pltpu.VMEM((2, 4, 8, NZ), F32)
    weights = [
        pltpu.VMEM((2, 4, NY, NZ), F32),
        pltpu.VMEM((2, 4, NX, NZ), F32),
        pltpu.VMEM((4, 8, 128), jnp.int32),
    ]
    marked = EX * EY * EZ + 2 * EY * EZ + 2 * EX * EZ + 4 * EZ
    oe, oh, oj, grad = pl.pallas_call(
        functools.partial(kernel, n_gx, n_gy),
        out_shape=(pltpu.VMEM((3, ROWS, NZ), BF16),) * 3 + (pltpu.VMEM((1, 128), F32),),
        in_specs=[hbm] * 13,
        out_specs=(pl.BlockSpec(memory_space=pltpu.VMEM),) * 4,
        scratch_shapes=[
            *[field16] * 6,
            pltpu.VMEM((ROWS, NZ), BF16),
            pltpu.VMEM((EX, EY, EZ), jnp.int32),
            pltpu.VMEM((EX, EY, EZ), jnp.int32),
            *[pltpu.VMEM(a.shape, a.dtype) for a in consts],
            *[field32] * 13,
            plane32,
            plane32,
            plane32,
            pltpu.VMEM((2, NY, NZ), F32),
            pltpu.VMEM((2, NX, NZ), F32),
            pltpu.VMEM((16, 128 * n_rows), F32),
            pltpu.VMEM((marked, 128 * n_rows), BF16),
            y_faces, x_faces, y_faces, corners,
            x_faces, y_faces, x_faces, y_faces, corners,
            *weights,
            *weights,
            pltpu.VMEM((n_rows, 1, 128), F32),
            pltpu.VMEM((n_gx, 1, 128), F32),
            pltpu.VMEM((1, 128), F32),
            pltpu.VMEM((n_gy, 1, 128), F32),
            dma((13,)),
            dma((3, 4)), dma((3, 4)), dma((3, 4)), dma((3, 4)), dma((2, 4)), dma((2, 4)),
            dma((4,)), dma((4,)), dma((4,)), dma((4,)),
            dma((n_gx,)), dma((n_gx,)), dma((n_gy,)), dma((n_gy,)),
            pltpu.SemaphoreType.REGULAR((gx_waves(n_gx),)),
        ],
        compiler_params=pltpu.CompilerParams(
            collective_id=0, has_side_effects=True, vmem_limit_bytes=60 * 1024 * 1024
        ),
    )(*fields, eps, args[7], args[8], *consts)
    oe, oh, oj, grad = pl.pallas_call(
        write_out,
        out_shape=(out16, out16, out16, jax.ShapeDtypeStruct((2,), F32)),
        in_specs=[pl.BlockSpec(memory_space=pltpu.VMEM)] * 4,
        out_specs=(hbm, hbm, hbm, pl.BlockSpec(memory_space=pltpu.VMEM)),
        scratch_shapes=[dma((3,))],
        compiler_params=pltpu.CompilerParams(vmem_limit_bytes=4 * 1024 * 1024),
    )(oe, oh, oj, grad)
    shape = args[0].shape
    return oe.reshape(shape), oh.reshape(shape), oj.reshape(shape), grad


def solution(mesh):
    n_gx, n_gy = mesh.shape["gx"], mesh.shape["gy"]
    field = P(None, "gx", "gy", None)
    node = P("gx", "gy", None)
    return jax.shard_map(
        functools.partial(per_device, n_gx, n_gy),
        mesh=mesh,
        in_specs=(field,) * 6 + (node,) * 3,
        out_specs=(field, field, field, P(("gx", "gy"))),
        check_vma=False,
    )
```

```python
import functools
import math

import jax
import jax.numpy as jnp
import numpy as np
from jax import lax
from jax.experimental import pallas as pl
from jax.experimental.pallas import tpu as pltpu
from jax.sharding import PartitionSpec as P

CB = 3
DT = 0.06
DECAY = 0.96
PLASMA = 16.0
PDT = PLASMA * DT
LIFT = 6.0
MESH = pl.DeviceIdType.MESH
F32 = jnp.float32
BF16 = jnp.bfloat16

EX, EY, EZ = 3, 6, 32
NX, NY, NZ = 4 * EX, 4 * EY, 4 * EZ
ROWS = NX * NY
CHUNK = 4 * NY


def gll_tables():
    points = np.array([-1.0, -math.sqrt(0.2), math.sqrt(0.2), 1.0])
    products = np.array(
        [np.prod([points[i] - points[j] for j in range(4) if j != i]) for i in range(4)]
    )
    matrix = np.zeros((4, 4))
    for i in range(4):
        for j in range(4):
            if i != j:
                matrix[i, j] = products[i] / products[j] / (points[i] - points[j])
    for i in range(4):
        matrix[i, i] = -np.sum(matrix[i])
    return matrix


def line_matrix(elements):
    n = 4 * elements
    full = np.kron(np.eye(elements), 2.0 * gll_tables())
    for e in range(elements):
        lo, hi = 4 * e, 4 * e + 3
        full[hi, hi] -= LIFT
        if hi + 1 < n:
            full[hi, hi + 1] += LIFT
        full[lo, lo] += LIFT
        if lo > 0:
            full[lo, lo - 1] -= LIFT
    return full


def two_parts(matrix):
    high = matrix.astype(np.float32).astype(jnp.bfloat16)
    low = (matrix - high.astype(np.float64)).astype(np.float32).astype(jnp.bfloat16)
    return high, low


def constant_arrays():
    zh, zl = two_parts(line_matrix(EZ).T)
    wz = np.block([[zh, zl], [zh, zl]])
    yh, yl = two_parts(np.kron(np.eye(4), line_matrix(EY)))
    wy = np.block([[yh, yh], [yl, yl]])
    w4 = np.array([1.0, 5.0, 5.0, 1.0])
    wsum = np.kron(np.eye(EZ), w4.reshape(4, 1))
    wt = np.tile(wsum, (1, EY)).astype(jnp.bfloat16)
    wm = np.kron(np.kron(np.eye(EY), w4.reshape(4, 1)), np.ones((1, EZ))).astype(np.float32)
    return wz, wy, wt, wm


def split(value):
    high = value.astype(BF16)
    low = (value - high.astype(F32)).astype(BF16)
    return high, low


def curl_chunk(src, ex, wz_ref, wy_ref, exact=False):
    r0 = CHUNK * ex
    comps = [src[c, r0 : r0 + CHUNK, :] for c in range(3)]
    if exact:
        high = [v.astype(BF16) for v in comps]
        zin = jnp.concatenate([high[0], high[1]], axis=0)
        zout = jnp.dot(zin, wz_ref[0:NZ, :], preferred_element_type=F32)
        yin = jnp.concatenate([high[0], high[2]], axis=1)
        yout = jnp.dot(wy_ref[:, 0:CHUNK], yin, preferred_element_type=F32)
    else:
        high, low = zip(*[split(v) for v in comps])
        zin = jnp.concatenate(
            [
                jnp.concatenate([high[0], low[0]], axis=1),
                jnp.concatenate([high[1], low[1]], axis=1),
            ],
            axis=0,
        )
        zout = jnp.dot(zin, wz_ref[...], preferred_element_type=F32)
        yin = jnp.concatenate(
            [
                jnp.concatenate([high[0], high[2]], axis=1),
                jnp.concatenate([low[0], low[2]], axis=1),
            ],
            axis=0,
        )
        yout = jnp.dot(wy_ref[...], yin, preferred_element_type=F32)
    zsum = zout[:, 0:NZ] + zout[:, NZ : 2 * NZ]
    dz_x, dz_y = zsum[0:CHUNK], zsum[CHUNK : 2 * CHUNK]
    ysum = yout[0:CHUNK] + yout[CHUNK : 2 * CHUNK]
    dy_x, dy_z = ysum[:, 0:NZ], ysum[:, NZ : 2 * NZ]

    m = 2.0 * gll_tables()

    def along_x(c):
        p = [comps[c][NY * a : NY * (a + 1)] for a in range(4)]
        out0 = m[0, 1] * p[1] + m[0, 2] * p[2] + m[0, 3] * p[3]
        if ex > 0:
            out0 = out0 - LIFT * src[c, r0 - NY : r0, :]
        out1 = m[1, 0] * p[0] + m[1, 2] * p[2] + m[1, 3] * p[3]
        out2 = m[2, 0] * p[0] + m[2, 1] * p[1] + m[2, 3] * p[3]
        out3 = m[3, 0] * p[0] + m[3, 1] * p[1] + m[3, 2] * p[2]
        if ex < EX - 1:
            out3 = out3 + LIFT * src[c, r0 + CHUNK : r0 + CHUNK + NY, :]
        return jnp.concatenate([out0, out1, out2, out3], axis=0)

    dx_y, dx_z = along_x(1), along_x(2)
    return dy_z - dz_y, dz_x - dx_z, dx_y - dy_x


LOW, HIGH = 0, 1
SIDES = (LOW, HIGH)
FIRST_X = slice(0, NY)
LAST_X = slice(ROWS - NY, ROWS)
X_FACE = (FIRST_X, LAST_X)
Y_FACE = (pl.ds(0, NX, stride=NY), pl.ds(NY - 1, NX, stride=NY))
CORNER = ((0, NY - 1), (ROWS - NY, ROWS - 1))
FACE = (-LIFT, LIFT)
F, A, B = 0, 1, 2


def gx_steps(n):
    return sorted({d % n for step in (1, 4) if step < n for d in (step, -step)} - {0})


def gx_waves(n):
    known, waves = {0, *gx_steps(n)}, 0
    while len(known) < n or not waves:
        known |= {(a + b) % n for a in known for b in gx_steps(n)}
        waves += 1
    return waves


def chunks():
    return [(ex, slice(CHUNK * ex, CHUNK * (ex + 1))) for ex in range(EX)]


def add_faces(xr, yr, field, factor):
    for s in SIDES:
        f = factor(X_FACE[s]) * FACE[s]
        field[1, X_FACE[s], :] -= f * xr[s, 1]
        field[2, X_FACE[s], :] += f * xr[s, 0]
    for s in SIDES:
        f = factor(Y_FACE[s]) * FACE[s]
        field[0, Y_FACE[s], :] += f * yr[s, 1]
        field[2, Y_FACE[s], :] -= f * yr[s, 0]


def complete_faces(xr, yr, corners, at, field, factor):
    for s in SIDES:
        f = -FACE[s] * factor
        xr[s, 0] -= f * field[2, X_FACE[s], :]
        xr[s, 1] += f * field[1, X_FACE[s], :]
        xr[s, 1, 0:1, :] -= FACE[LOW] * factor * corners[2 * s + LOW, at : at + 1, :]
        xr[s, 1, NY - 1 : NY, :] -= FACE[HIGH] * factor * corners[2 * s + HIGH, at : at + 1, :]
    for s in SIDES:
        f = -FACE[s] * factor
        yr[s, 0] += f * field[2, Y_FACE[s], :]
        yr[s, 1] -= f * field[0, Y_FACE[s], :]
        yr[s, 1, 0:1, :] += FACE[LOW] * factor * corners[2 * LOW + s, at + 1 : at + 2, :]
        yr[s, 1, NX - 1 : NX, :] += FACE[HIGH] * factor * corners[2 * HIGH + s, at + 1 : at + 2, :]


def kernel(
    n_gx,
    n_gy,
    e_in, h_in, j_in, le_in, lh_in, lj_in, eps_in, mat_in, blk_in, wz_in, wy_in, wt_in, wm_in,
    oe_out, oh_out, oj_out, grad_ref,
    eb, hb, jb, leb, lhb, ljb, epsb, mat, blk, wz, wy, wt, wm,
    e0, h1, e1, h2, tot1, sc1, mid1, tot0, sc0, mid0, le0, lj1, q,
    step, drude, part, xt, yt, sums, onehot,
    uys, vxs, vys, cs, uxr, uyr, vxr, vyr, cr,
    wxs, wys, ids, wxr, wyr, idr,
    gsend, grecv, msend, mrecv,
    in_sem, u_send, u_recv, v_send, v_recv, c_send, c_recv,
    w_send, w_recv, i_send, i_recv, g_send_sem, g_recv_sem, m_send_sem, m_recv_sem, heard,
):
    gx, gy = lax.axis_index("gx"), lax.axis_index("gy")
    near_x = (lax.rem(gx + n_gx - 1, n_gx), lax.rem(gx + 1, n_gx))
    near_y = (lax.rem(gy + n_gy - 1, n_gy), lax.rem(gy + 1, n_gy))

    def load(index, src, dst):
        copy = pltpu.make_async_copy(src, dst, in_sem.at[index])
        copy.start()
        return copy

    barrier = pltpu.get_barrier_semaphore()
    near = [(lax.rem(gx + d, n_gx), gy) for d in gx_steps(n_gx)]
    peers = near + [(gx, lax.rem(gy + k, n_gy)) for k in range(1, n_gy)]
    peers += [(near_x[a], near_y[b]) for a in SIDES for b in SIDES]
    for peer in peers:
        pl.semaphore_signal(barrier, inc=1, device_id=peer, device_id_type=MESH)

    in_e = load(0, e_in, eb)
    in_h = load(7, h_in, hb)
    in_wz = load(5, wz_in, wz)
    in_wy = load(6, wy_in, wy)

    in_le = load(1, le_in, leb)
    in_lj = load(2, lj_in, ljb)
    in_eps = load(3, eps_in, epsb)
    in_mat = load(4, mat_in, mat)
    in_lh = load(8, lh_in, lhb)
    in_j = load(9, j_in, jb)
    in_blk = load(10, blk_in, blk)
    in_wt = load(11, wt_in, wt)
    in_wm = load(12, wm_in, wm)

    started = []

    def remote(src, dst, send_sem, recv_sem, target):
        copy = pltpu.make_async_remote_copy(
            src_ref=src, dst_ref=dst, send_sem=send_sem, recv_sem=recv_sem,
            device_id=target, device_id_type=MESH,
        )
        copy.start()
        started.append(copy)
        return copy

    def stage_u(k, field):
        for s in SIDES:
            uys[k, s, 0] = field[0, Y_FACE[s], :]
            uys[k, s, 1] = field[2, Y_FACE[s], :]

    def stage_corners(k, at, field):
        for s in SIDES:
            for t in SIDES:
                row = CORNER[s][t]
                cs[k, 2 * s + t, at : at + 1, :] = field[0, row : row + 1, :]
                cs[k, 2 * s + t, at + 1 : at + 2, :] = field[1, row : row + 1, :]

    def stage_v(k, field):
        for s in SIDES:
            vxs[k, s, 0] = field[1, X_FACE[s], :]
            vxs[k, s, 1] = field[2, X_FACE[s], :]
            vys[k, s, 0] = field[0, Y_FACE[s], :]
            vys[k, s, 1] = field[2, Y_FACE[s], :]

    def send_u(k, field):
        copies = []
        for s in SIDES:
            src = field.at[pl.ds(1, 2), pl.ds(s * (ROWS - NY), NY)]
            copies.append(
                remote(src, uxr.at[k, 1 - s], u_send.at[k, s], u_recv.at[k, s], (near_x[s], gy))
            )
        for s in SIDES:
            copies.append(
                remote(
                    uys.at[k, s], uyr.at[k, 1 - s], u_send.at[k, 2 + s], u_recv.at[k, 2 + s],
                    (gx, near_y[s]),
                )
            )
        return copies

    def send_corners(k):
        return [
            remote(
                cs.at[k, 2 * s + t], cr.at[k, 2 * (1 - s) + 1 - t],
                c_send.at[k, 2 * s + t], c_recv.at[k, 2 * s + t], (near_x[s], near_y[t]),
            )
            for s in SIDES
            for t in SIDES
        ]

    def send_v(k):
        copies = []
        for s in SIDES:
            copies.append(
                remote(
                    vxs.at[k, s], vxr.at[k, 1 - s], v_send.at[k, s], v_recv.at[k, s],
                    (near_x[s], gy),
                )
            )
        for s in SIDES:
            copies.append(
                remote(
                    vys.at[k, s], vyr.at[k, 1 - s], v_send.at[k, 2 + s], v_recv.at[k, 2 + s],
                    (gx, near_y[s]),
                )
            )
        return copies

    def arrived(copies):
        for copy in copies:
            copy.wait_recv()

    by_step = lambda rows: step[rows, :]
    by_dt = lambda rows: -DT
    by_one = lambda rows: 1.0

    in_e.wait()
    for c in range(3):
        e0[c] = eb[c].astype(F32)
    in_wz.wait()
    in_wy.wait()
    in_h.wait()
    for ex, rows in chunks():
        curl = curl_chunk(e0, ex, wz, wy, exact=True)
        for c in range(3):
            h1[c, rows, :] = hb[c, rows, :].astype(F32) - DT * curl[c]
    stage_u(F, e0)
    stage_v(F, h1)
    cs[...] = jnp.zeros_like(cs)
    stage_corners(0, 0, e0)

    pl.semaphore_wait(barrier, len(peers))
    fu = send_u(F, e0)
    fv = send_v(F)

    def pass_on(wave):
        for peer in near:
            pl.semaphore_signal(heard.at[wave], inc=1, device_id=peer, device_id_type=MESH)


    in_mat.wait()
    in_eps.wait()
    zpick = (
        lax.broadcasted_iota(jnp.int32, (EZ, NZ), 0) == lax.broadcasted_iota(jnp.int32, (EZ, NZ), 1) >> 2
    ).astype(F32).astype(BF16)
    ypick = (
        lax.broadcasted_iota(jnp.int32, (NY, EY), 0) >> 2 == lax.broadcasted_iota(jnp.int32, (NY, EY), 1)
    ).astype(F32).astype(BF16)
    for ex, rows in chunks():
        picked = jnp.dot(mat[ex].astype(F32).astype(BF16), zpick, preferred_element_type=F32)
        plane = jnp.dot(ypick, picked.astype(BF16), preferred_element_type=F32)
        for a in range(4):
            drude[CHUNK * ex + NY * a : CHUNK * ex + NY * (a + 1), :] = plane
    step[...] = DT / epsb[...].astype(F32)
    in_le.wait()
    in_lj.wait()
    for c in range(3):
        total = leb[c].astype(F32) + PDT * drude[...] * ljb[c].astype(F32)
        tot1[c] = total
        sc1[c] = step[...] * total
    in_lh.wait()
    for ex, rows in chunks():
        curl = curl_chunk(sc1, ex, wz, wy)
        for c in range(3):
            mid1[c, rows, :] = lhb[c, rows, :].astype(F32) + curl[c]
    stage_u(A, sc1)
    stage_v(A, mid1)
    stage_corners(0, 2, sc1)
    for c in range(3):
        q[c] = sc1[c] * step[...]
    stage_corners(0, 4, q)

    in_blk.wait()
    ids[...] = jnp.zeros_like(ids)
    for s in SIDES:
        ids[s, 0:EY, 0:EZ] = blk[(EX - 1) * s]
        for ex in range(EX):
            ids[2 + s, ex : ex + 1, 0:EZ] = blk[ex, (EY - 1) * s : (EY - 1) * s + 1, :]
        for t in SIDES:
            line = blk[(EX - 1) * s, (EY - 1) * t : (EY - 1) * t + 1, :]
            cs[0, 2 * s + t, 6:7, 0:EZ] = line.astype(F32)
    rc = send_corners(0)
    waves = gx_waves(n_gx)
    pass_on(0)
    au = send_u(A, sc1)
    av = send_v(A)
    marks = []
    for s in SIDES:
        marks.append(remote(ids.at[s], idr.at[1 - s], i_send.at[s], i_recv.at[s], (near_x[s], gy)))
        marks.append(
            remote(ids.at[2 + s], idr.at[3 - s], i_send.at[2 + s], i_recv.at[2 + s], (gx, near_y[s]))
        )

    m = 2.0 * gll_tables()
    w4 = (1.0, 5.0, 5.0, 1.0)
    for s in SIDES:
        end = 3 * s
        wxs[s, 0] = step[X_FACE[s], :]
        wxs[s, 1] = q[0, X_FACE[s], :]
        wys[s, 0] = step[Y_FACE[s], :]
        wys[s, 1] = q[1, Y_FACE[s], :]
        inner = [a for a in range(4) if a != end]
        for slot, c in ((2, 1), (3, 2)):
            acc = None
            for a in inner:
                r0 = NY * ((NX - 4) * s + a)
                term = (m[a, end] * w4[a]) * q[c, r0 : r0 + NY, :]
                acc = term if acc is None else acc + term
            wxs[s, slot] = acc
        for slot, c in ((2, 0), (3, 2)):
            acc = None
            for a in inner:
                term = (m[a, end] * w4[a]) * q[c, pl.ds((NY - 4) * s + a, NX, stride=NY), :]
                acc = term if acc is None else acc + term
            wys[s, slot] = acc
    ws = []
    for s in SIDES:
        to_x, to_y = (near_x[s], gy), (gx, near_y[s])
        ws.append(remote(wxs.at[s], wxr.at[1 - s], w_send.at[s], w_recv.at[s], to_x))
        ws.append(remote(wys.at[s], wyr.at[1 - s], w_send.at[2 + s], w_recv.at[2 + s], to_y))

    n_rows = gsend.shape[0]
    eye = lax.broadcasted_iota(jnp.int32, (EZ, EZ), 0) == lax.broadcasted_iota(jnp.int32, (EZ, EZ), 1)
    ones = jnp.ones((EZ, 128), BF16)

    def mark(at, rows):
        coarse = jnp.concatenate(
            [jnp.where(eye, (r & -16).astype(F32), 0.0) for r in rows], axis=0
        ).astype(BF16)
        fine = jnp.concatenate(
            [jnp.where(eye, (r & 15).astype(F32), 0.0) for r in rows], axis=0
        ).astype(BF16)
        column = jnp.dot(coarse, ones, preferred_element_type=F32) + jnp.dot(
            fine, ones, preferred_element_type=F32
        )
        column = column.astype(jnp.int32)
        lane = lax.broadcasted_iota(jnp.int32, column.shape, 1)
        for n in range(n_rows):
            onehot[at : at + EZ * len(rows), 128 * n : 128 * (n + 1)] = (
                (column == lane + 128 * n).astype(F32).astype(BF16)
            )

    layer_len = EY * EZ
    for ex in range(EX):
        mark(layer_len * ex, [blk[ex, ey : ey + 1, :] for ey in range(EY)])
    x_at = layer_len * EX
    y_at = x_at + 2 * layer_len
    c_at = y_at + 2 * EX * EZ

    pl.semaphore_wait(heard.at[0], len(near))
    if waves > 1:
        pass_on(1)

    in_j.wait()
    arrived(fu)
    add_faces(uxr.at[F], uyr.at[F], h1, by_dt)
    for ex, rows in chunks():
        curl = curl_chunk(h1, ex, wz, wy)
        for c in range(3):
            e1[c, rows, :] = e0[c, rows, :] + step[rows, :] * (
                curl[c] - drude[rows, :] * jb[c, rows, :].astype(F32)
            )
    arrived(fv)
    arrived(rc)
    complete_faces(vxr.at[F], vyr.at[F], cr.at[0], 0, e0, -DT)
    add_faces(vxr.at[F], vyr.at[F], e1, by_step)

    arrived(au)
    add_faces(uxr.at[A], uyr.at[A], mid1, by_one)
    for ex, rows in chunks():
        curl = curl_chunk(mid1, ex, wz, wy)
        for c in range(3):
            lj = drude[rows, :] * (DECAY * ljb[c, rows, :].astype(F32) - sc1[c, rows, :])
            lj1[c, rows, :] = lj
            tot0[c, rows, :] = tot1[c, rows, :] - DT * curl[c] + PDT * lj

    for ex, rows in chunks():
        curl = curl_chunk(e1, ex, wz, wy)
        for c in range(3):
            h2[c, rows, :] = h1[c, rows, :] - DT * curl[c]
    for ex, rows in chunks():
        curl = curl_chunk(h2, ex, wz, wy)
        node = None
        for c in range(3):
            current = drude[rows, :] * (DECAY * jb[c, rows, :].astype(F32) + PDT * e1[c, rows, :])
            term = q[c, rows, :] * (curl[c] - current)
            node = term if node is None else node + term
        part[rows, :] = node
    back = LIFT * LIFT * DT
    for s in SIDES:
        x, y = X_FACE[s], Y_FACE[s]
        part[x, :] -= back * (q[1, x, :] * e1[1, x, :] + q[2, x, :] * e1[2, x, :])
        part[y, :] -= back * (q[0, y, :] * e1[0, y, :] + q[2, y, :] * e1[2, y, :])

    arrived(marks)
    mark(x_at, [idr[s, ey : ey + 1, 0:EZ] for s in SIDES for ey in range(EY)])
    mark(y_at, [idr[2 + s, ex : ex + 1, 0:EZ] for s in SIDES for ex in range(EX)])
    mark(c_at, [cr[0, k, 6:7, 0:EZ].astype(jnp.int32) for k in range(4)])
    xa = [-FACE[s] * DT * e1[2, X_FACE[s], :] for s in SIDES]
    xb = [FACE[s] * DT * e1[1, X_FACE[s], :] for s in SIDES]
    ya = [FACE[s] * DT * e1[2, Y_FACE[s], :] for s in SIDES]
    yb = [-FACE[s] * DT * e1[0, Y_FACE[s], :] for s in SIDES]

    def along_z(value):
        high, low = split(value)
        out = jnp.dot(jnp.concatenate([high, low], axis=1), wz[...], preferred_element_type=F32)
        return out[:, 0:NZ] + out[:, NZ : 2 * NZ]

    def along_rows(values):
        n = values[0].shape[0]
        high, low = split(jnp.concatenate(values, axis=1))
        top, rest = wy[0:n, 0:n], wy[CHUNK : CHUNK + n, 0:n]
        out = (
            jnp.dot(top, high, preferred_element_type=F32)
            + jnp.dot(top, low, preferred_element_type=F32)
            + jnp.dot(rest, high, preferred_element_type=F32)
        )
        return out[:, 0:NZ], out[:, NZ : 2 * NZ]

    xaz, yaz = [along_z(v) for v in xa], [along_z(v) for v in ya]
    xby, ybx = along_rows(xb), along_rows(yb)
    for s in SIDES:
        xt[s] = xby[s] - xaz[s]
        yt[s] = yaz[s] - ybx[s]

    in_wt.wait()
    in_wm.wait()
    scale = -1.0 / (216.0 * 8.0 * DT)

    def by_element(layers, count, weights):
        n = layers[0].shape[0]
        high, low = split(jnp.concatenate(layers, axis=0))
        w = wt[:, 0 : count * EZ]
        wide = jnp.dot(high, w, preferred_element_type=F32) + jnp.dot(
            low, w, preferred_element_type=F32
        )
        return [
            jnp.sum(wide[n * i : n * (i + 1)] * weights, axis=0, keepdims=True)
            for i in range(len(layers))
        ]

    def by_block(flats, at):
        out = None
        for i, flat in enumerate(flats):
            n = flat.shape[1]
            row = lax.broadcasted_iota(jnp.int32, (16, n), 0)
            flat = jnp.broadcast_to(flat, (16, n))
            top = flat.astype(BF16).astype(F32)
            pieces = jnp.where(row == 0, top, jnp.where(row == 1, flat - top, 0.0)).astype(BF16)
            term = jnp.dot(
                pieces, onehot[at + n * i : at + n * (i + 1), :], preferred_element_type=F32
            )
            out = term if out is None else out + term
        return out

    def layers_of(values):
        out = []
        for ex in range(EX):
            n = [values[CHUNK * ex + NY * a : CHUNK * ex + NY * (a + 1), :] for a in range(4)]
            out.append(n[0] + n[3] + 5.0 * (n[1] + n[2]))
        return out

    eighths = []
    for s in SIDES:
        for t in SIDES:
            row = CORNER[s][t]
            line = (
                (-FACE[s] * FACE[t] * DT)
                * (
                    cr[0, 2 * s + t, 5:6, :] * e1[0, row : row + 1, :]
                    + cr[0, 2 * s + t, 4:5, :] * e1[1, row : row + 1, :]
                )
            )
            eighths.append(jnp.broadcast_to(line, (8, NZ)))
    sums[...] = by_block(by_element(layers_of(part), EY, wm[...]), 0) + by_block(
        by_element(eighths, 1, 0.125), c_at
    )

    arrived(av)
    complete_faces(vxr.at[A], vyr.at[A], cr.at[0], 2, sc1, 1.0)
    add_faces(vxr.at[A], vyr.at[A], tot0, by_dt)
    for c in range(3):
        sc0[c] = step[...] * tot0[c]
    stage_u(B, sc0)
    stage_corners(1, 0, sc0)
    bu = send_u(B, sc0)
    bc = send_corners(1)
    early = None
    for c in range(3):
        term = sc0[c] * (e1[c] - e0[c])
        early = term if early is None else early + term
    part[...] = early
    sums[...] += by_block(by_element(layers_of(part), EY, wm[...]), 0)

    arrived(ws)
    planes = []
    for s in SIDES:
        w = wxr.at[s]
        hy, hz = h2[1, X_FACE[s], :], h2[2, X_FACE[s], :]
        planes.append(
            w[1] * xt[s] - w[2] * (FACE[s] * DT * e1[1, X_FACE[s], :])
            - w[3] * (FACE[s] * DT * e1[2, X_FACE[s], :])
            + FACE[s] * w[0] * (uxr[A, s, 0] * hz - uxr[A, s, 1] * hy)
        )
    for s in SIDES:
        w = wyr.at[s]
        hx, hz = h2[0, Y_FACE[s], :], h2[2, Y_FACE[s], :]
        planes.append(
            w[1] * yt[s] - w[2] * (FACE[s] * DT * e1[0, Y_FACE[s], :])
            - w[3] * (FACE[s] * DT * e1[2, Y_FACE[s], :])
            + FACE[s] * w[0] * (uyr[A, s, 1] * hx - uyr[A, s, 0] * hz)
        )
    late = (
        sums[...]
        + by_block(by_element(planes[0:2], EY, wm[...]), x_at)
        + by_block(by_element(planes[2:4], EX, wm[0:NX, 0 : EX * EZ]), y_at)
    )
    total = jnp.sum(late, axis=0, keepdims=True) * scale
    for n in range(n_rows):
        gsend[n] = total[:, 128 * n : 128 * (n + 1)]
    for wave in range(1, waves):
        pl.semaphore_wait(heard.at[wave], len(near))
        if wave + 1 < waves:
            pass_on(wave + 1)
    width = 2 * n_gy
    per_row = 128 // width
    phase1 = []
    for k in range(1, n_gx):
        p = lax.rem(gx + k, n_gx)
        phase1.append(
            remote(
                gsend.at[lax.div(p, per_row)], grecv.at[k], g_send_sem.at[k], g_recv_sem.at[k], (p, gy)
            )
        )

    for ex, rows in chunks():
        curl = curl_chunk(sc0, ex, wz, wy)
        for c in range(3):
            mid0[c, rows, :] = mid1[c, rows, :] + curl[c]
    stage_v(B, mid0)
    bv = send_v(B)
    for c in range(3):
        oj_out[c] = (drude[...] * (DECAY * lj1[c] - sc0[c])).astype(BF16)

    mine = gsend[lax.div(gx, per_row)]
    arrived(phase1)
    for k in range(1, n_gx):
        mine = mine + grecv[k]
    msend[...] = mine
    phase2 = []
    for k in range(1, n_gy):
        phase2.append(
            remote(
                msend, mrecv.at[k], m_send_sem.at[k], m_recv_sem.at[k], (gx, lax.rem(gy + k, n_gy))
            )
        )

    arrived(bu)
    add_faces(uxr.at[B], uyr.at[B], mid0, by_one)
    for c in range(3):
        oh_out[c] = mid0[c].astype(BF16)
    for ex, rows in chunks():
        curl = curl_chunk(mid0, ex, wz, wy)
        for c in range(3):
            le0[c, rows, :] = tot0[c, rows, :] - DT * curl[c]
    arrived(bv)
    arrived(bc)
    complete_faces(vxr.at[B], vyr.at[B], cr.at[1], 0, sc0, 1.0)
    add_faces(vxr.at[B], vyr.at[B], le0, by_dt)
    for c in range(3):
        oe_out[c] = le0[c].astype(BF16)

    for copy in started:
        copy.wait_send()
    arrived(phase2)
    for k in range(1, n_gy):
        mine = mine + mrecv[k]
    at = lax.rem(gx, per_row) * width + 2 * gy
    lanes = lax.broadcasted_iota(jnp.int32, (1, 128), 1)
    first = jnp.sum(jnp.where(lanes == at, mine, 0.0), axis=1, keepdims=True)
    second = jnp.sum(jnp.where(lanes == at + 1, mine, 0.0), axis=1, keepdims=True)
    grad_ref[...] = jnp.where(lanes == 0, first, second)


def write_out(e_in, h_in, j_in, g_in, e_out, h_out, j_out, g_out, sem):
    pairs = ((e_in, e_out), (h_in, h_out), (j_in, j_out))
    copies = [pltpu.make_async_copy(a, b, sem.at[i]) for i, (a, b) in enumerate(pairs)]
    for copy in copies:
        copy.start()
    g_out[...] = g_in[0, 0:2]
    for copy in copies:
        copy.wait()


def per_device(n_gx, n_gy, *args):
    fields = [a.reshape(3, ROWS, NZ) for a in args[0:6]]
    eps = args[6].reshape(ROWS, NZ)
    blocks = EX * n_gx // CB * (EY * n_gy // CB)
    n_rows = -(-blocks // 128)
    consts = [jnp.asarray(a) for a in constant_arrays()]
    hbm = pl.BlockSpec(memory_space=pl.ANY)
    field32 = pltpu.VMEM((3, ROWS, NZ), F32)
    field16 = pltpu.VMEM((3, ROWS, NZ), BF16)
    plane32 = pltpu.VMEM((ROWS, NZ), F32)
    out16 = jax.ShapeDtypeStruct((3, ROWS, NZ), BF16)
    dma = pltpu.SemaphoreType.DMA
    x_faces = pltpu.VMEM((3, 2, 2, NY, NZ), F32)
    y_faces = pltpu.VMEM((3, 2, 2, NX, NZ), F32)
    corners = pltpu.VMEM((2, 4, 8, NZ), F32)
    weights = [
        pltpu.VMEM((2, 4, NY, NZ), F32),
        pltpu.VMEM((2, 4, NX, NZ), F32),
        pltpu.VMEM((4, 8, 128), jnp.int32),
    ]
    marked = EX * EY * EZ + 2 * EY * EZ + 2 * EX * EZ + 4 * EZ
    oe, oh, oj, grad = pl.pallas_call(
        functools.partial(kernel, n_gx, n_gy),
        out_shape=(pltpu.VMEM((3, ROWS, NZ), BF16),) * 3 + (pltpu.VMEM((1, 128), F32),),
        in_specs=[hbm] * 13,
        out_specs=(pl.BlockSpec(memory_space=pltpu.VMEM),) * 4,
        scratch_shapes=[
            *[field16] * 6,
            pltpu.VMEM((ROWS, NZ), BF16),
            pltpu.VMEM((EX, EY, EZ), jnp.int32),
            pltpu.VMEM((EX, EY, EZ), jnp.int32),
            *[pltpu.VMEM(a.shape, a.dtype) for a in consts],
            *[field32] * 13,
            plane32,
            plane32,
            plane32,
            pltpu.VMEM((2, NY, NZ), F32),
            pltpu.VMEM((2, NX, NZ), F32),
            pltpu.VMEM((16, 128 * n_rows), F32),
            pltpu.VMEM((marked, 128 * n_rows), BF16),
            y_faces, x_faces, y_faces, corners,
            x_faces, y_faces, x_faces, y_faces, corners,
            *weights,
            *weights,
            pltpu.VMEM((n_rows, 1, 128), F32),
            pltpu.VMEM((n_gx, 1, 128), F32),
            pltpu.VMEM((1, 128), F32),
            pltpu.VMEM((n_gy, 1, 128), F32),
            dma((13,)),
            dma((3, 4)), dma((3, 4)), dma((3, 4)), dma((3, 4)), dma((2, 4)), dma((2, 4)),
            dma((4,)), dma((4,)), dma((4,)), dma((4,)),
            dma((n_gx,)), dma((n_gx,)), dma((n_gy,)), dma((n_gy,)),
            pltpu.SemaphoreType.REGULAR((gx_waves(n_gx),)),
        ],
        compiler_params=pltpu.CompilerParams(
            collective_id=0, has_side_effects=True, vmem_limit_bytes=60 * 1024 * 1024
        ),
    )(*fields, eps, args[7], args[8], *consts)
    oe, oh, oj, grad = pl.pallas_call(
        write_out,
        out_shape=(out16, out16, out16, jax.ShapeDtypeStruct((2,), F32)),
        in_specs=[pl.BlockSpec(memory_space=pltpu.VMEM)] * 4,
        out_specs=(hbm, hbm, hbm, pl.BlockSpec(memory_space=pltpu.VMEM)),
        scratch_shapes=[dma((3,))],
        compiler_params=pltpu.CompilerParams(vmem_limit_bytes=4 * 1024 * 1024),
    )(oe, oh, oj, grad)
    shape = args[0].shape
    return oe.reshape(shape), oh.reshape(shape), oj.reshape(shape), grad


def solution(mesh):
    n_gx, n_gy = mesh.shape["gx"], mesh.shape["gy"]
    field = P(None, "gx", "gy", None)
    node = P("gx", "gy", None)
    return jax.shard_map(
        functools.partial(per_device, n_gx, n_gy),
        mesh=mesh,
        in_specs=(field,) * 6 + (node,) * 3,
        out_specs=(field, field, field, P(("gx", "gy"))),
        check_vma=False,
    )
```

```python
import functools
import math

import jax
import jax.numpy as jnp
import numpy as np
from jax import lax
from jax.experimental import pallas as pl
from jax.experimental.pallas import tpu as pltpu
from jax.sharding import PartitionSpec as P

CB = 3
DT = 0.06
DECAY = 0.96
PLASMA = 16.0
PDT = PLASMA * DT
LIFT = 6.0
MESH = pl.DeviceIdType.MESH
F32 = jnp.float32
BF16 = jnp.bfloat16

EX, EY, EZ = 3, 6, 32
NX, NY, NZ = 4 * EX, 4 * EY, 4 * EZ
ROWS = NX * NY
CHUNK = 4 * NY


def gll_tables():
    points = np.array([-1.0, -math.sqrt(0.2), math.sqrt(0.2), 1.0])
    products = np.array(
        [np.prod([points[i] - points[j] for j in range(4) if j != i]) for i in range(4)]
    )
    matrix = np.zeros((4, 4))
    for i in range(4):
        for j in range(4):
            if i != j:
                matrix[i, j] = products[i] / products[j] / (points[i] - points[j])
    for i in range(4):
        matrix[i, i] = -np.sum(matrix[i])
    return matrix


def line_matrix(elements):
    n = 4 * elements
    full = np.kron(np.eye(elements), 2.0 * gll_tables())
    for e in range(elements):
        lo, hi = 4 * e, 4 * e + 3
        full[hi, hi] -= LIFT
        if hi + 1 < n:
            full[hi, hi + 1] += LIFT
        full[lo, lo] += LIFT
        if lo > 0:
            full[lo, lo - 1] -= LIFT
    return full


def two_parts(matrix):
    high = matrix.astype(np.float32).astype(jnp.bfloat16)
    low = (matrix - high.astype(np.float64)).astype(np.float32).astype(jnp.bfloat16)
    return high, low


def constant_arrays():
    zh, zl = two_parts(line_matrix(EZ).T)
    wz = np.block([[zh, zl], [zh, zl]])
    yh, yl = two_parts(np.kron(np.eye(4), line_matrix(EY)))
    wy = np.block([[yh, yh], [yl, yl]])
    w4 = np.array([1.0, 5.0, 5.0, 1.0])
    wsum = np.kron(np.eye(EZ), w4.reshape(4, 1))
    wt = np.tile(wsum, (1, EY)).astype(jnp.bfloat16)
    wm = np.kron(np.kron(np.eye(EY), w4.reshape(4, 1)), np.ones((1, EZ))).astype(np.float32)
    return wz, wy, wt, wm


def split(value):
    high = value.astype(BF16)
    low = (value - high.astype(F32)).astype(BF16)
    return high, low


def curl_chunk(src, ex, wz_ref, wy_ref, exact=False):
    r0 = CHUNK * ex
    comps = [src[c, r0 : r0 + CHUNK, :] for c in range(3)]
    if exact:
        high = [v.astype(BF16) for v in comps]
        zin = jnp.concatenate([high[0], high[1]], axis=0)
        zout = jnp.dot(zin, wz_ref[0:NZ, :], preferred_element_type=F32)
        yin = jnp.concatenate([high[0], high[2]], axis=1)
        yout = jnp.dot(wy_ref[:, 0:CHUNK], yin, preferred_element_type=F32)
    else:
        high, low = zip(*[split(v) for v in comps])
        zin = jnp.concatenate(
            [
                jnp.concatenate([high[0], low[0]], axis=1),
                jnp.concatenate([high[1], low[1]], axis=1),
            ],
            axis=0,
        )
        zout = jnp.dot(zin, wz_ref[...], preferred_element_type=F32)
        yin = jnp.concatenate(
            [
                jnp.concatenate([high[0], high[2]], axis=1),
                jnp.concatenate([low[0], low[2]], axis=1),
            ],
            axis=0,
        )
        yout = jnp.dot(wy_ref[...], yin, preferred_element_type=F32)
    zsum = zout[:, 0:NZ] + zout[:, NZ : 2 * NZ]
    dz_x, dz_y = zsum[0:CHUNK], zsum[CHUNK : 2 * CHUNK]
    ysum = yout[0:CHUNK] + yout[CHUNK : 2 * CHUNK]
    dy_x, dy_z = ysum[:, 0:NZ], ysum[:, NZ : 2 * NZ]

    m = 2.0 * gll_tables()

    def along_x(c):
        p = [comps[c][NY * a : NY * (a + 1)] for a in range(4)]
        out0 = m[0, 1] * p[1] + m[0, 2] * p[2] + m[0, 3] * p[3]
        if ex > 0:
            out0 = out0 - LIFT * src[c, r0 - NY : r0, :]
        out1 = m[1, 0] * p[0] + m[1, 2] * p[2] + m[1, 3] * p[3]
        out2 = m[2, 0] * p[0] + m[2, 1] * p[1] + m[2, 3] * p[3]
        out3 = m[3, 0] * p[0] + m[3, 1] * p[1] + m[3, 2] * p[2]
        if ex < EX - 1:
            out3 = out3 + LIFT * src[c, r0 + CHUNK : r0 + CHUNK + NY, :]
        return jnp.concatenate([out0, out1, out2, out3], axis=0)

    dx_y, dx_z = along_x(1), along_x(2)
    return dy_z - dz_y, dz_x - dx_z, dx_y - dy_x


LOW, HIGH = 0, 1
SIDES = (LOW, HIGH)
FIRST_X = slice(0, NY)
LAST_X = slice(ROWS - NY, ROWS)
X_FACE = (FIRST_X, LAST_X)
Y_FACE = (pl.ds(0, NX, stride=NY), pl.ds(NY - 1, NX, stride=NY))
CORNER = ((0, NY - 1), (ROWS - NY, ROWS - 1))
FACE = (-LIFT, LIFT)
F, A, B = 0, 1, 2


def gx_steps(n):
    return sorted({d % n for step in (1, 4) if step < n for d in (step, -step)} - {0})


def gx_waves(n):
    known, waves = {0, *gx_steps(n)}, 0
    while len(known) < n or not waves:
        known |= {(a + b) % n for a in known for b in gx_steps(n)}
        waves += 1
    return waves


def chunks():
    return [(ex, slice(CHUNK * ex, CHUNK * (ex + 1))) for ex in range(EX)]


def add_faces(xr, yr, field, factor):
    for s in SIDES:
        f = factor(X_FACE[s]) * FACE[s]
        field[1, X_FACE[s], :] -= f * xr[s, 1]
        field[2, X_FACE[s], :] += f * xr[s, 0]
    for s in SIDES:
        f = factor(Y_FACE[s]) * FACE[s]
        field[0, Y_FACE[s], :] += f * yr[s, 1]
        field[2, Y_FACE[s], :] -= f * yr[s, 0]


def complete_faces(xr, yr, corners, at, field, factor):
    for s in SIDES:
        f = -FACE[s] * factor
        xr[s, 0] -= f * field[2, X_FACE[s], :]
        xr[s, 1] += f * field[1, X_FACE[s], :]
        xr[s, 1, 0:1, :] -= FACE[LOW] * factor * corners[2 * s + LOW, at : at + 1, :]
        xr[s, 1, NY - 1 : NY, :] -= FACE[HIGH] * factor * corners[2 * s + HIGH, at : at + 1, :]
    for s in SIDES:
        f = -FACE[s] * factor
        yr[s, 0] += f * field[2, Y_FACE[s], :]
        yr[s, 1] -= f * field[0, Y_FACE[s], :]
        yr[s, 1, 0:1, :] += FACE[LOW] * factor * corners[2 * LOW + s, at + 1 : at + 2, :]
        yr[s, 1, NX - 1 : NX, :] += FACE[HIGH] * factor * corners[2 * HIGH + s, at + 1 : at + 2, :]


def kernel(
    n_gx,
    n_gy,
    e_in, h_in, j_in, le_in, lh_in, lj_in, eps_in, mat_in, blk_in, wz_in, wy_in, wt_in, wm_in,
    oe_out, oh_out, oj_out, grad_ref,
    eb, hb, jb, leb, lhb, ljb, epsb, mat, blk, wz, wy, wt, wm,
    e0, h1, e1, h2, tot1, sc1, mid1, tot0, sc0, mid0, le0, lj1, q,
    step, drude, part, xt, yt, sums, onehot,
    uys, vxs, vys, cs, uxr, uyr, vxr, vyr, cr,
    wxs, wys, ids, wxr, wyr, idr,
    gsend, grecv, msend, mrecv,
    in_sem, u_send, u_recv, v_send, v_recv, c_send, c_recv,
    w_send, w_recv, i_send, i_recv, g_send_sem, g_recv_sem, m_send_sem, m_recv_sem, heard,
):
    gx, gy = lax.axis_index("gx"), lax.axis_index("gy")
    near_x = (lax.rem(gx + n_gx - 1, n_gx), lax.rem(gx + 1, n_gx))
    near_y = (lax.rem(gy + n_gy - 1, n_gy), lax.rem(gy + 1, n_gy))

    def load(index, src, dst):
        copy = pltpu.make_async_copy(src, dst, in_sem.at[index])
        copy.start()
        return copy

    barrier = pltpu.get_barrier_semaphore()
    near = [(lax.rem(gx + d, n_gx), gy) for d in gx_steps(n_gx)]
    peers = near + [(gx, lax.rem(gy + k, n_gy)) for k in range(1, n_gy)]
    peers += [(near_x[a], near_y[b]) for a in SIDES for b in SIDES]
    for peer in peers:
        pl.semaphore_signal(barrier, inc=1, device_id=peer, device_id_type=MESH)

    in_e = load(0, e_in, eb)
    in_h = load(7, h_in, hb)
    in_wz = load(5, wz_in, wz)
    in_wy = load(6, wy_in, wy)

    in_le = load(1, le_in, leb)
    in_lj = load(2, lj_in, ljb)
    in_eps = load(3, eps_in, epsb)
    in_mat = load(4, mat_in, mat)
    in_lh = load(8, lh_in, lhb)
    in_j = load(9, j_in, jb)
    in_blk = load(10, blk_in, blk)
    in_wt = load(11, wt_in, wt)
    in_wm = load(12, wm_in, wm)

    started = []

    def remote(src, dst, send_sem, recv_sem, target):
        copy = pltpu.make_async_remote_copy(
            src_ref=src, dst_ref=dst, send_sem=send_sem, recv_sem=recv_sem,
            device_id=target, device_id_type=MESH,
        )
        copy.start()
        started.append(copy)
        return copy

    def stage_u(k, field):
        for s in SIDES:
            uys[k, s, 0] = field[0, Y_FACE[s], :]
            uys[k, s, 1] = field[2, Y_FACE[s], :]

    def stage_corners(k, at, field):
        for s in SIDES:
            for t in SIDES:
                row = CORNER[s][t]
                cs[k, 2 * s + t, at : at + 1, :] = field[0, row : row + 1, :]
                cs[k, 2 * s + t, at + 1 : at + 2, :] = field[1, row : row + 1, :]

    def stage_v(k, field):
        for s in SIDES:
            vxs[k, s, 0] = field[1, X_FACE[s], :]
            vxs[k, s, 1] = field[2, X_FACE[s], :]
            vys[k, s, 0] = field[0, Y_FACE[s], :]
            vys[k, s, 1] = field[2, Y_FACE[s], :]

    def send_u(k, field):
        copies = []
        for s in SIDES:
            src = field.at[pl.ds(1, 2), pl.ds(s * (ROWS - NY), NY)]
            copies.append(
                remote(src, uxr.at[k, 1 - s], u_send.at[k, s], u_recv.at[k, s], (near_x[s], gy))
            )
        for s in SIDES:
            copies.append(
                remote(
                    uys.at[k, s], uyr.at[k, 1 - s], u_send.at[k, 2 + s], u_recv.at[k, 2 + s],
                    (gx, near_y[s]),
                )
            )
        return copies

    def send_corners(k):
        return [
            remote(
                cs.at[k, 2 * s + t], cr.at[k, 2 * (1 - s) + 1 - t],
                c_send.at[k, 2 * s + t], c_recv.at[k, 2 * s + t], (near_x[s], near_y[t]),
            )
            for s in SIDES
            for t in SIDES
        ]

    def send_v(k):
        copies = []
        for s in SIDES:
            copies.append(
                remote(
                    vxs.at[k, s], vxr.at[k, 1 - s], v_send.at[k, s], v_recv.at[k, s],
                    (near_x[s], gy),
                )
            )
        for s in SIDES:
            copies.append(
                remote(
                    vys.at[k, s], vyr.at[k, 1 - s], v_send.at[k, 2 + s], v_recv.at[k, 2 + s],
                    (gx, near_y[s]),
                )
            )
        return copies

    def arrived(copies):
        for copy in copies:
            copy.wait_recv()

    by_step = lambda rows: step[rows, :]
    by_dt = lambda rows: -DT
    by_one = lambda rows: 1.0

    in_e.wait()
    for c in range(3):
        e0[c] = eb[c].astype(F32)
    in_wz.wait()
    in_wy.wait()
    in_h.wait()
    for ex, rows in chunks():
        curl = curl_chunk(e0, ex, wz, wy, exact=True)
        for c in range(3):
            h1[c, rows, :] = hb[c, rows, :].astype(F32) - DT * curl[c]
    stage_u(F, e0)
    stage_v(F, h1)
    cs[...] = jnp.zeros_like(cs)
    stage_corners(0, 0, e0)

    pl.semaphore_wait(barrier, len(peers))
    fu = send_u(F, e0)
    fv = send_v(F)

    def pass_on(wave):
        for peer in near:
            pl.semaphore_signal(heard.at[wave], inc=1, device_id=peer, device_id_type=MESH)


    in_mat.wait()
    in_eps.wait()
    zpick = (
        lax.broadcasted_iota(jnp.int32, (EZ, NZ), 0) == lax.broadcasted_iota(jnp.int32, (EZ, NZ), 1) >> 2
    ).astype(F32).astype(BF16)
    ypick = (
        lax.broadcasted_iota(jnp.int32, (NY, EY), 0) >> 2 == lax.broadcasted_iota(jnp.int32, (NY, EY), 1)
    ).astype(F32).astype(BF16)
    for ex, rows in chunks():
        picked = jnp.dot(mat[ex].astype(F32).astype(BF16), zpick, preferred_element_type=F32)
        plane = jnp.dot(ypick, picked.astype(BF16), preferred_element_type=F32)
        for a in range(4):
            drude[CHUNK * ex + NY * a : CHUNK * ex + NY * (a + 1), :] = plane
    step[...] = DT / epsb[...].astype(F32)
    in_le.wait()
    in_lj.wait()
    for c in range(3):
        total = leb[c].astype(F32) + PDT * drude[...] * ljb[c].astype(F32)
        tot1[c] = total
        sc1[c] = step[...] * total
    in_lh.wait()
    for ex, rows in chunks():
        curl = curl_chunk(sc1, ex, wz, wy)
        for c in range(3):
            mid1[c, rows, :] = lhb[c, rows, :].astype(F32) + curl[c]
    stage_u(A, sc1)
    stage_v(A, mid1)
    stage_corners(0, 2, sc1)
    for c in range(3):
        q[c] = sc1[c] * step[...]
    stage_corners(0, 4, q)

    in_blk.wait()
    ids[...] = jnp.zeros_like(ids)
    for s in SIDES:
        ids[s, 0:EY, 0:EZ] = blk[(EX - 1) * s]
        for ex in range(EX):
            ids[2 + s, ex : ex + 1, 0:EZ] = blk[ex, (EY - 1) * s : (EY - 1) * s + 1, :]
        for t in SIDES:
            line = blk[(EX - 1) * s, (EY - 1) * t : (EY - 1) * t + 1, :]
            cs[0, 2 * s + t, 6:7, 0:EZ] = line.astype(F32)
    rc = send_corners(0)
    waves = gx_waves(n_gx)
    pass_on(0)
    au = send_u(A, sc1)
    av = send_v(A)
    marks = []
    for s in SIDES:
        marks.append(remote(ids.at[s], idr.at[1 - s], i_send.at[s], i_recv.at[s], (near_x[s], gy)))
        marks.append(
            remote(ids.at[2 + s], idr.at[3 - s], i_send.at[2 + s], i_recv.at[2 + s], (gx, near_y[s]))
        )

    m = 2.0 * gll_tables()
    w4 = (1.0, 5.0, 5.0, 1.0)
    for s in SIDES:
        end = 3 * s
        wxs[s, 0] = step[X_FACE[s], :]
        wxs[s, 1] = q[0, X_FACE[s], :]
        wys[s, 0] = step[Y_FACE[s], :]
        wys[s, 1] = q[1, Y_FACE[s], :]
        inner = [a for a in range(4) if a != end]
        for slot, c in ((2, 1), (3, 2)):
            acc = None
            for a in inner:
                r0 = NY * ((NX - 4) * s + a)
                term = (m[a, end] * w4[a]) * q[c, r0 : r0 + NY, :]
                acc = term if acc is None else acc + term
            wxs[s, slot] = acc
        for slot, c in ((2, 0), (3, 2)):
            acc = None
            for a in inner:
                term = (m[a, end] * w4[a]) * q[c, pl.ds((NY - 4) * s + a, NX, stride=NY), :]
                acc = term if acc is None else acc + term
            wys[s, slot] = acc
    ws = []
    for s in SIDES:
        to_x, to_y = (near_x[s], gy), (gx, near_y[s])
        ws.append(remote(wxs.at[s], wxr.at[1 - s], w_send.at[s], w_recv.at[s], to_x))
        ws.append(remote(wys.at[s], wyr.at[1 - s], w_send.at[2 + s], w_recv.at[2 + s], to_y))

    n_rows = gsend.shape[0]
    eye = lax.broadcasted_iota(jnp.int32, (EZ, EZ), 0) == lax.broadcasted_iota(jnp.int32, (EZ, EZ), 1)
    ones = jnp.ones((EZ, 128), BF16)

    def mark(at, rows):
        coarse = jnp.concatenate(
            [jnp.where(eye, (r & -16).astype(F32), 0.0) for r in rows], axis=0
        ).astype(BF16)
        fine = jnp.concatenate(
            [jnp.where(eye, (r & 15).astype(F32), 0.0) for r in rows], axis=0
        ).astype(BF16)
        column = jnp.dot(coarse, ones, preferred_element_type=F32) + jnp.dot(
            fine, ones, preferred_element_type=F32
        )
        column = column.astype(jnp.int32)
        lane = lax.broadcasted_iota(jnp.int32, column.shape, 1)
        for n in range(n_rows):
            onehot[at : at + EZ * len(rows), 128 * n : 128 * (n + 1)] = (
                (column == lane + 128 * n).astype(F32).astype(BF16)
            )

    layer_len = EY * EZ
    for ex in range(EX):
        mark(layer_len * ex, [blk[ex, ey : ey + 1, :] for ey in range(EY)])
    x_at = layer_len * EX
    y_at = x_at + 2 * layer_len
    c_at = y_at + 2 * EX * EZ

    pl.semaphore_wait(heard.at[0], len(near))
    if waves > 1:
        pass_on(1)

    in_j.wait()
    arrived(fu)
    add_faces(uxr.at[F], uyr.at[F], h1, by_dt)
    for ex, rows in chunks():
        curl = curl_chunk(h1, ex, wz, wy)
        for c in range(3):
            e1[c, rows, :] = e0[c, rows, :] + step[rows, :] * (
                curl[c] - drude[rows, :] * jb[c, rows, :].astype(F32)
            )
    arrived(fv)
    arrived(rc)
    complete_faces(vxr.at[F], vyr.at[F], cr.at[0], 0, e0, -DT)
    add_faces(vxr.at[F], vyr.at[F], e1, by_step)

    arrived(au)
    add_faces(uxr.at[A], uyr.at[A], mid1, by_one)
    for ex, rows in chunks():
        curl = curl_chunk(mid1, ex, wz, wy)
        for c in range(3):
            lj = drude[rows, :] * (DECAY * ljb[c, rows, :].astype(F32) - sc1[c, rows, :])
            lj1[c, rows, :] = lj
            tot0[c, rows, :] = tot1[c, rows, :] - DT * curl[c] + PDT * lj

    for ex, rows in chunks():
        curl = curl_chunk(e1, ex, wz, wy)
        for c in range(3):
            h2[c, rows, :] = h1[c, rows, :] - DT * curl[c]
    for ex, rows in chunks():
        curl = curl_chunk(h2, ex, wz, wy)
        node = None
        for c in range(3):
            current = drude[rows, :] * (DECAY * jb[c, rows, :].astype(F32) + PDT * e1[c, rows, :])
            term = q[c, rows, :] * (curl[c] - current)
            node = term if node is None else node + term
        part[rows, :] = node
    back = LIFT * LIFT * DT
    for s in SIDES:
        x, y = X_FACE[s], Y_FACE[s]
        part[x, :] -= back * (q[1, x, :] * e1[1, x, :] + q[2, x, :] * e1[2, x, :])
        part[y, :] -= back * (q[0, y, :] * e1[0, y, :] + q[2, y, :] * e1[2, y, :])

    arrived(marks)
    mark(x_at, [idr[s, ey : ey + 1, 0:EZ] for s in SIDES for ey in range(EY)])
    mark(y_at, [idr[2 + s, ex : ex + 1, 0:EZ] for s in SIDES for ex in range(EX)])
    mark(c_at, [cr[0, k, 6:7, 0:EZ].astype(jnp.int32) for k in range(4)])
    xa = [-FACE[s] * DT * e1[2, X_FACE[s], :] for s in SIDES]
    xb = [FACE[s] * DT * e1[1, X_FACE[s], :] for s in SIDES]
    ya = [FACE[s] * DT * e1[2, Y_FACE[s], :] for s in SIDES]
    yb = [-FACE[s] * DT * e1[0, Y_FACE[s], :] for s in SIDES]

    def along_z(value):
        high, low = split(value)
        out = jnp.dot(jnp.concatenate([high, low], axis=1), wz[...], preferred_element_type=F32)
        return out[:, 0:NZ] + out[:, NZ : 2 * NZ]

    def along_rows(values):
        n = values[0].shape[0]
        high, low = split(jnp.concatenate(values, axis=1))
        top, rest = wy[0:n, 0:n], wy[CHUNK : CHUNK + n, 0:n]
        out = (
            jnp.dot(top, high, preferred_element_type=F32)
            + jnp.dot(top, low, preferred_element_type=F32)
            + jnp.dot(rest, high, preferred_element_type=F32)
        )
        return out[:, 0:NZ], out[:, NZ : 2 * NZ]

    xaz, yaz = [along_z(v) for v in xa], [along_z(v) for v in ya]
    xby, ybx = along_rows(xb), along_rows(yb)
    for s in SIDES:
        xt[s] = xby[s] - xaz[s]
        yt[s] = yaz[s] - ybx[s]

    in_wt.wait()
    in_wm.wait()
    scale = -1.0 / (216.0 * 8.0 * DT)

    def by_element(layers, count, weights):
        n = layers[0].shape[0]
        high, low = split(jnp.concatenate(layers, axis=0))
        w = wt[:, 0 : count * EZ]
        wide = jnp.dot(high, w, preferred_element_type=F32) + jnp.dot(
            low, w, preferred_element_type=F32
        )
        return [
            jnp.sum(wide[n * i : n * (i + 1)] * weights, axis=0, keepdims=True)
            for i in range(len(layers))
        ]

    def by_block(flats, at):
        out = None
        for i, flat in enumerate(flats):
            n = flat.shape[1]
            row = lax.broadcasted_iota(jnp.int32, (16, n), 0)
            flat = jnp.broadcast_to(flat, (16, n))
            top = flat.astype(BF16).astype(F32)
            pieces = jnp.where(row == 0, top, jnp.where(row == 1, flat - top, 0.0)).astype(BF16)
            term = jnp.dot(
                pieces, onehot[at + n * i : at + n * (i + 1), :], preferred_element_type=F32
            )
            out = term if out is None else out + term
        return out

    def layers_of(values):
        out = []
        for ex in range(EX):
            n = [values[CHUNK * ex + NY * a : CHUNK * ex + NY * (a + 1), :] for a in range(4)]
            out.append(n[0] + n[3] + 5.0 * (n[1] + n[2]))
        return out

    eighths = []
    for s in SIDES:
        for t in SIDES:
            row = CORNER[s][t]
            line = (
                (-FACE[s] * FACE[t] * DT)
                * (
                    cr[0, 2 * s + t, 5:6, :] * e1[0, row : row + 1, :]
                    + cr[0, 2 * s + t, 4:5, :] * e1[1, row : row + 1, :]
                )
            )
            eighths.append(jnp.broadcast_to(line, (8, NZ)))
    sums[...] = by_block(by_element(layers_of(part), EY, wm[...]), 0) + by_block(
        by_element(eighths, 1, 0.125), c_at
    )

    arrived([c for i, c in enumerate(ws) if i % 2])
    planes = []
    for s in SIDES:
        w = wyr.at[s]
        hx, hz = h2[0, Y_FACE[s], :], h2[2, Y_FACE[s], :]
        planes.append(
            w[1] * yt[s] - w[2] * (FACE[s] * DT * e1[0, Y_FACE[s], :])
            - w[3] * (FACE[s] * DT * e1[2, Y_FACE[s], :])
            + FACE[s] * w[0] * (uyr[A, s, 1] * hx - uyr[A, s, 0] * hz)
        )
    sums[...] += by_block(by_element(planes, EX, wm[0:NX, 0 : EX * EZ]), y_at)

    arrived(av)
    complete_faces(vxr.at[A], vyr.at[A], cr.at[0], 2, sc1, 1.0)
    add_faces(vxr.at[A], vyr.at[A], tot0, by_dt)
    for c in range(3):
        sc0[c] = step[...] * tot0[c]
    stage_u(B, sc0)
    stage_corners(1, 0, sc0)
    bu = send_u(B, sc0)
    bc = send_corners(1)
    early = None
    for c in range(3):
        term = sc0[c] * (e1[c] - e0[c])
        early = term if early is None else early + term
    part[...] = early
    sums[...] += by_block(by_element(layers_of(part), EY, wm[...]), 0)

    arrived([c for i, c in enumerate(ws) if i % 2 == 0])
    planes = []
    for s in SIDES:
        w = wxr.at[s]
        hy, hz = h2[1, X_FACE[s], :], h2[2, X_FACE[s], :]
        planes.append(
            w[1] * xt[s] - w[2] * (FACE[s] * DT * e1[1, X_FACE[s], :])
            - w[3] * (FACE[s] * DT * e1[2, X_FACE[s], :])
            + FACE[s] * w[0] * (uxr[A, s, 0] * hz - uxr[A, s, 1] * hy)
        )
    late = (
        sums[...]
        + by_block(by_element(planes, EY, wm[...]), x_at)
    )
    total = jnp.sum(late, axis=0, keepdims=True) * scale
    for n in range(n_rows):
        gsend[n] = total[:, 128 * n : 128 * (n + 1)]
    for wave in range(1, waves):
        pl.semaphore_wait(heard.at[wave], len(near))
        if wave + 1 < waves:
            pass_on(wave + 1)
    width = 2 * n_gy
    per_row = 128 // width
    phase1 = []
    for k in range(1, n_gx):
        p = lax.rem(gx + k, n_gx)
        phase1.append(
            remote(
                gsend.at[lax.div(p, per_row)], grecv.at[k], g_send_sem.at[k], g_recv_sem.at[k], (p, gy)
            )
        )

    for ex, rows in chunks():
        curl = curl_chunk(sc0, ex, wz, wy)
        for c in range(3):
            mid0[c, rows, :] = mid1[c, rows, :] + curl[c]
    stage_v(B, mid0)
    bv = send_v(B)
    for c in range(3):
        oj_out[c] = (drude[...] * (DECAY * lj1[c] - sc0[c])).astype(BF16)

    mine = gsend[lax.div(gx, per_row)]
    arrived(phase1)
    for k in range(1, n_gx):
        mine = mine + grecv[k]
    msend[...] = mine
    phase2 = []
    for k in range(1, n_gy):
        phase2.append(
            remote(
                msend, mrecv.at[k], m_send_sem.at[k], m_recv_sem.at[k], (gx, lax.rem(gy + k, n_gy))
            )
        )

    arrived(bu)
    add_faces(uxr.at[B], uyr.at[B], mid0, by_one)
    for c in range(3):
        oh_out[c] = mid0[c].astype(BF16)
    for ex, rows in chunks():
        curl = curl_chunk(mid0, ex, wz, wy)
        for c in range(3):
            le0[c, rows, :] = tot0[c, rows, :] - DT * curl[c]
    arrived(bv)
    arrived(bc)
    complete_faces(vxr.at[B], vyr.at[B], cr.at[1], 0, sc0, 1.0)
    add_faces(vxr.at[B], vyr.at[B], le0, by_dt)
    for c in range(3):
        oe_out[c] = le0[c].astype(BF16)

    for copy in started:
        copy.wait_send()
    arrived(phase2)
    for k in range(1, n_gy):
        mine = mine + mrecv[k]
    at = lax.rem(gx, per_row) * width + 2 * gy
    lanes = lax.broadcasted_iota(jnp.int32, (1, 128), 1)
    first = jnp.sum(jnp.where(lanes == at, mine, 0.0), axis=1, keepdims=True)
    second = jnp.sum(jnp.where(lanes == at + 1, mine, 0.0), axis=1, keepdims=True)
    grad_ref[...] = jnp.where(lanes == 0, first, second)


def write_out(e_in, h_in, j_in, g_in, e_out, h_out, j_out, g_out, sem):
    pairs = ((e_in, e_out), (h_in, h_out), (j_in, j_out))
    copies = [pltpu.make_async_copy(a, b, sem.at[i]) for i, (a, b) in enumerate(pairs)]
    for copy in copies:
        copy.start()
    g_out[...] = g_in[0, 0:2]
    for copy in copies:
        copy.wait()


def per_device(n_gx, n_gy, *args):
    fields = [a.reshape(3, ROWS, NZ) for a in args[0:6]]
    eps = args[6].reshape(ROWS, NZ)
    blocks = EX * n_gx // CB * (EY * n_gy // CB)
    n_rows = -(-blocks // 128)
    consts = [jnp.asarray(a) for a in constant_arrays()]
    hbm = pl.BlockSpec(memory_space=pl.ANY)
    field32 = pltpu.VMEM((3, ROWS, NZ), F32)
    field16 = pltpu.VMEM((3, ROWS, NZ), BF16)
    plane32 = pltpu.VMEM((ROWS, NZ), F32)
    out16 = jax.ShapeDtypeStruct((3, ROWS, NZ), BF16)
    dma = pltpu.SemaphoreType.DMA
    x_faces = pltpu.VMEM((3, 2, 2, NY, NZ), F32)
    y_faces = pltpu.VMEM((3, 2, 2, NX, NZ), F32)
    corners = pltpu.VMEM((2, 4, 8, NZ), F32)
    weights = [
        pltpu.VMEM((2, 4, NY, NZ), F32),
        pltpu.VMEM((2, 4, NX, NZ), F32),
        pltpu.VMEM((4, 8, 128), jnp.int32),
    ]
    marked = EX * EY * EZ + 2 * EY * EZ + 2 * EX * EZ + 4 * EZ
    oe, oh, oj, grad = pl.pallas_call(
        functools.partial(kernel, n_gx, n_gy),
        out_shape=(pltpu.VMEM((3, ROWS, NZ), BF16),) * 3 + (pltpu.VMEM((1, 128), F32),),
        in_specs=[hbm] * 13,
        out_specs=(pl.BlockSpec(memory_space=pltpu.VMEM),) * 4,
        scratch_shapes=[
            *[field16] * 6,
            pltpu.VMEM((ROWS, NZ), BF16),
            pltpu.VMEM((EX, EY, EZ), jnp.int32),
            pltpu.VMEM((EX, EY, EZ), jnp.int32),
            *[pltpu.VMEM(a.shape, a.dtype) for a in consts],
            *[field32] * 13,
            plane32,
            plane32,
            plane32,
            pltpu.VMEM((2, NY, NZ), F32),
            pltpu.VMEM((2, NX, NZ), F32),
            pltpu.VMEM((16, 128 * n_rows), F32),
            pltpu.VMEM((marked, 128 * n_rows), BF16),
            y_faces, x_faces, y_faces, corners,
            x_faces, y_faces, x_faces, y_faces, corners,
            *weights,
            *weights,
            pltpu.VMEM((n_rows, 1, 128), F32),
            pltpu.VMEM((n_gx, 1, 128), F32),
            pltpu.VMEM((1, 128), F32),
            pltpu.VMEM((n_gy, 1, 128), F32),
            dma((13,)),
            dma((3, 4)), dma((3, 4)), dma((3, 4)), dma((3, 4)), dma((2, 4)), dma((2, 4)),
            dma((4,)), dma((4,)), dma((4,)), dma((4,)),
            dma((n_gx,)), dma((n_gx,)), dma((n_gy,)), dma((n_gy,)),
            pltpu.SemaphoreType.REGULAR((gx_waves(n_gx),)),
        ],
        compiler_params=pltpu.CompilerParams(
            collective_id=0, has_side_effects=True, vmem_limit_bytes=60 * 1024 * 1024
        ),
    )(*fields, eps, args[7], args[8], *consts)
    oe, oh, oj, grad = pl.pallas_call(
        write_out,
        out_shape=(out16, out16, out16, jax.ShapeDtypeStruct((2,), F32)),
        in_specs=[pl.BlockSpec(memory_space=pltpu.VMEM)] * 4,
        out_specs=(hbm, hbm, hbm, pl.BlockSpec(memory_space=pltpu.VMEM)),
        scratch_shapes=[dma((3,))],
        compiler_params=pltpu.CompilerParams(vmem_limit_bytes=4 * 1024 * 1024),
    )(oe, oh, oj, grad)
    shape = args[0].shape
    return oe.reshape(shape), oh.reshape(shape), oj.reshape(shape), grad


def solution(mesh):
    n_gx, n_gy = mesh.shape["gx"], mesh.shape["gy"]
    field = P(None, "gx", "gy", None)
    node = P("gx", "gy", None)
    return jax.shard_map(
        functools.partial(per_device, n_gx, n_gy),
        mesh=mesh,
        in_specs=(field,) * 6 + (node,) * 3,
        out_specs=(field, field, field, P(("gx", "gy"))),
        check_vma=False,
    )
```
